256 devices in a mesh: dp: 64 (over x, y_hi, z), mp: 4 (over y_lo, core).
Axes of the slice: x: 4, y: 4 (y_hi: 2, y_lo: 2; y = y_hi * 2 + y_lo), z: 8, core: 2. Of those that a mesh axis runs over, the one named last changes fastest.
Arguments:
- images: bfloat16 [128, 729, 1152], P('dp', None, 'mp'), may hold values from -8 to 8
- ln_gain: float32 [1152], replicated, may hold values from 0.1 to 1.9
- w_in: bfloat16 [1152, 4304], P(None, 'mp'), may hold values from -0.1875 to 0.1875
- b_in: float32 [4304], P('mp'), may hold values from -3 to 3
- w_out: bfloat16 [4304, 1152], P('mp'), may hold values from -0.09375 to 0.09375
- texts: bfloat16 [128, 1152], P('dp'), may hold values from -6 to 6
- w_text: bfloat16 [1152, 1152], replicated, may hold values from -0.1875 to 0.1875
- b_text: float32 [1152], replicated, may hold values from -3 to 3
- logit_scale: float32 [1], replicated, may hold values from 8 to 32
- logit_bias: float32 [1], replicated, may hold values from -4 to 0
Outputs:
- grad_w_in: float32 [1152, 4304], P('dp', 'mp')
- grad_w_out: float32 [4304, 1152], P('mp', 'dp')
- grad_w_text: float32 [1152, 1152], P('dp')
- grad_texts: bfloat16 [128, 1152], P('dp')
The draws below stay inside these ranges and needn't reach their ends.
All inputs are finite; a program needn't handle non-finite values.
Results may differ from the reference program's by a relative error of at most 0.011.
Values may be sent and summed in bfloat16 or wider, within the bound.
A program may use at most 128 MiB of HBM per device.

```python
import math
import jax
import jax.numpy as jnp
from jax import lax

D = 1152
FF = 4304
PATCH = 729
BATCH = 128


def draw_images(key, part):
    key = jax.random.fold_in(key, 7)
    key_mean, key_noise = jax.random.split(key, 2)
    common = jax.random.normal(key_mean, (BATCH, 1, D), jnp.float32)
    patch_noise = jax.random.normal(key_noise, (BATCH, PATCH, D), jnp.float32)
    values = 0.2 * common + patch_noise
    return jnp.clip(values, -8.0, 8.0).astype(jnp.bfloat16)


def level_of(own_key, shape, cuts, low, high):
    factor_of, own = 1.0, jax.random.fold_in(own_key, 6)
    for dim, shards_of in cuts:
        heights = jnp.exp(jax.random.uniform(jax.random.fold_in(own, dim), (shards_of,), jnp.float32, low / len(cuts), high / len(cuts)))
        factor_of = factor_of * jnp.repeat(heights, shape[dim] // shards_of).reshape([-1 if axis == dim else 1 for axis in range(len(shape))])
    return factor_of


def centred(rng, dims, width, limit, pieces=(), kind=jnp.bfloat16):
    drawn = jax.random.normal(rng, dims, jnp.float32) * width
    if len(pieces) > 0:
        drawn = level_of(rng, dims, pieces, -0.22, 0.18) * drawn
    return jnp.clip(drawn, min=-limit, max=limit).astype(kind)


def setup_inputs(seed: int = 0) -> dict:
    keys = jax.random.split(jax.random.key(seed), 11)
    images = draw_images(jax.random.fold_in(keys[10], 71), 0)
    ln_gain = jnp.clip(1.0 + 0.18 * jax.random.normal(keys[1], (D,), jnp.float32), 0.1, 1.9)
    w_in = centred(keys[2], (D, FF), D ** -0.5, 0.1875, ((1, 4),))
    b_in = centred(keys[3], (FF,), 0.5, 3.0, ((0, 4),), jnp.float32)
    w_out = centred(keys[4], (FF, D), FF ** -0.5, 0.09375, ((0, 4),))
    texts = centred(keys[5], (BATCH, D), 1.0, 6.0, ((0, 64),))
    w_text = centred(keys[6], (D, D), D ** -0.5, 0.1875)
    b_text = centred(keys[7], (D,), 0.5, 3.0, (), jnp.float32)
    logit_scale = jnp.clip(jnp.exp(jax.random.uniform(keys[8], (1,), jnp.float32, math.log(8.0), math.log(32.0))), 8.0, 32.0)
    logit_bias = jnp.clip(jax.random.uniform(keys[9], (1,), jnp.float32, -4.0, 0.0), -4.0, 0.0)
    return {"images": images, "ln_gain": ln_gain, "w_in": w_in, "b_in": b_in, "w_out": w_out, "texts": texts, "w_text": w_text, "b_text": b_text, "logit_scale": logit_scale, "logit_bias": logit_bias}


sqrt_two_pi = 0.7978845608028654
cubic_term = 0.044715
epsilon = 1e-06

def gelu_tanh(values):
    return 0.5 * values * (1.0 + jnp.tanh(sqrt_two_pi * (values + cubic_term * values * values * values)))

def gelu_slope(values):
    tanh_part = jnp.tanh(sqrt_two_pi * (values + cubic_term * values * values * values))
    return 0.5 * (1.0 + tanh_part) + 0.5 * values * (1.0 - tanh_part * tanh_part) * sqrt_two_pi * (1.0 + 3.0 * cubic_term * values * values)

def layer_norm(image_rows, ln_gain):
    values = image_rows.astype(jnp.float32)
    centered = values - lax.optimization_barrier(jnp.mean(values, axis=-1, keepdims=True))
    spread = lax.optimization_barrier(jnp.mean(centered * centered, axis=-1, keepdims=True))
    return (centered * lax.rsqrt(spread + epsilon) * ln_gain).astype(jnp.bfloat16)

def reference(images, ln_gain, w_in, b_in, w_out, texts, w_text, b_text, logit_scale, logit_bias):

    def forward_one(picture):
        normed = layer_norm(picture, ln_gain)
        before = jnp.dot(normed, w_in, preferred_element_type=jnp.float32) + b_in
        activated = gelu_tanh(before).astype(jnp.bfloat16)
        block_out = picture.astype(jnp.float32) + jnp.dot(activated, w_out, preferred_element_type=jnp.float32)
        return (lax.optimization_barrier(jnp.mean(block_out, axis=0)), lax.optimization_barrier(jnp.sum(activated, axis=0, dtype=jnp.float32)))
    pooled, act_sum = lax.map(forward_one, images)
    image_norm = jnp.sqrt(lax.optimization_barrier(jnp.sum(pooled * pooled, axis=1, keepdims=True)) + epsilon)
    image_unit = pooled / image_norm
    image_emb = image_unit.astype(jnp.bfloat16)
    text_proj = jnp.dot(texts, w_text, preferred_element_type=jnp.float32) + b_text
    text_norm = jnp.sqrt(lax.optimization_barrier(jnp.sum(text_proj * text_proj, axis=1, keepdims=True)) + epsilon)
    text_unit = text_proj / text_norm
    text_emb = text_unit.astype(jnp.bfloat16)
    logits = logit_scale[0] * jnp.dot(image_emb, text_emb.T, preferred_element_type=jnp.float32) + logit_bias[0]
    pair_signs = 2.0 * jnp.eye(BATCH, dtype=jnp.float32) - 1.0
    pair_coef = -pair_signs * jax.nn.sigmoid(-pair_signs * logits)
    scaled = (logit_scale[0] * pair_coef).astype(jnp.bfloat16)
    grad_image_emb = jnp.dot(scaled, text_emb, preferred_element_type=jnp.float32)
    grad_text_emb = jnp.dot(scaled.T, image_emb, preferred_element_type=jnp.float32)
    grad_pooled = (grad_image_emb - image_unit * lax.optimization_barrier(jnp.sum(image_unit * grad_image_emb, axis=1, keepdims=True))) / image_norm
    grad_block = (grad_pooled / PATCH).astype(jnp.bfloat16)
    grad_act = jnp.dot(grad_block, w_out.T, preferred_element_type=jnp.float32)
    grad_w_out = jnp.dot(act_sum.T, grad_block.astype(jnp.float32), precision=lax.Precision.HIGHEST)

    def accumulate(running, inputs_pair):
        picture, grad_row = inputs_pair
        normed = layer_norm(picture, ln_gain)
        before = jnp.dot(normed, w_in, preferred_element_type=jnp.float32) + b_in
        grad_pre = (grad_row * gelu_slope(before)).astype(jnp.bfloat16)
        return (running + jnp.dot(normed.T, grad_pre, preferred_element_type=jnp.float32), None)
    grad_w_in, leftover = lax.scan(accumulate, jnp.zeros((D, FF), jnp.float32), (images, grad_act))
    grad_text_proj = ((grad_text_emb - text_unit * lax.optimization_barrier(jnp.sum(text_unit * grad_text_emb, axis=1, keepdims=True))) / text_norm).astype(jnp.bfloat16)
    grad_w_text = jnp.dot(texts.T, grad_text_proj, preferred_element_type=jnp.float32)
    grad_texts = jnp.dot(grad_text_proj, w_text.T, preferred_element_type=jnp.float32).astype(jnp.bfloat16)
    return (grad_w_in, grad_w_out, grad_w_text, grad_texts)
```

```python
import jax
import jax.numpy as jnp
from jax import lax
from jax.sharding import PartitionSpec as P

sqrt_two_pi = 0.7978845608028654
cubic_term = 0.044715
epsilon = 1e-06
HIGHEST = lax.Precision.HIGHEST


def gelu_and_slope(values):
    squared = values * values
    tanh_part = jnp.tanh(sqrt_two_pi * (values + cubic_term * values * squared))
    half = 0.5 * (1.0 + tanh_part)
    slope = half + 0.5 * values * (1.0 - tanh_part * tanh_part) * sqrt_two_pi * (
        1.0 + 3.0 * cubic_term * squared
    )
    return values * half, slope


def layer_norm(image_rows, ln_gain):
    values = image_rows.astype(jnp.float32)
    centered = values - jnp.mean(values, axis=-1, keepdims=True)
    spread = jnp.mean(centered * centered, axis=-1, keepdims=True)
    return (centered * lax.rsqrt(spread + epsilon) * ln_gain).astype(jnp.bfloat16)


def dot(a, b, dims, precision=None):
    return lax.dot_general(
        a, b, (dims, ((), ())), preferred_element_type=jnp.float32, precision=precision
    )


def shards(images, ln_gain, w_in, b_in, w_out, texts, w_text, b_text, logit_scale, logit_bias):
    count, patches, _ = images.shape
    full = lax.all_gather(images, "mp", axis=2, tiled=True)
    texts_all = lax.all_gather(texts, "dp", axis=0, tiled=True)
    width = full.shape[2]
    batch = texts_all.shape[0]
    act_sums, products = [], []
    for i in range(count):
        normed = layer_norm(full[i], ln_gain)
        before = dot(normed, w_in, ((1,), (0,))) + b_in
        act, slope = gelu_and_slope(before)
        act_sums.append(
            jnp.sum(act.astype(jnp.bfloat16), axis=0, keepdims=True, dtype=jnp.float32)
        )
        products.append(dot(normed, slope.astype(jnp.bfloat16), ((0,), (0,))))
    act_sum = jnp.concatenate(act_sums, axis=0)
    block_sum = dot(act_sum, w_out.astype(jnp.float32), ((1,), (0,)), HIGHEST)
    block_sum = lax.psum(block_sum, "mp")
    pooled_own = (jnp.sum(full.astype(jnp.float32), axis=1) + block_sum) / patches
    pooled = lax.all_gather(pooled_own, "dp", axis=0, tiled=True)
    act_sum_all = lax.all_gather(act_sum, "dp", axis=0, tiled=True)

    image_norm = jnp.sqrt(jnp.sum(pooled * pooled, axis=1, keepdims=True) + epsilon)
    image_unit = pooled / image_norm
    image_emb = image_unit.astype(jnp.bfloat16)
    text_proj = dot(texts_all, w_text, ((1,), (0,))) + b_text
    text_norm = jnp.sqrt(jnp.sum(text_proj * text_proj, axis=1, keepdims=True) + epsilon)
    text_unit = text_proj / text_norm
    text_emb = text_unit.astype(jnp.bfloat16)
    logits = logit_scale[0] * dot(image_emb, text_emb, ((1,), (1,))) + logit_bias[0]
    signs = jnp.where(jnp.eye(batch, dtype=bool), 1.0, -1.0)
    scaled = (logit_scale[0] * (-signs * jax.nn.sigmoid(-signs * logits))).astype(jnp.bfloat16)
    grad_image_emb = dot(scaled, text_emb, ((1,), (0,)))
    grad_text_emb = dot(scaled, image_emb, ((0,), (0,)))
    grad_pooled = (
        grad_image_emb - image_unit * jnp.sum(image_unit * grad_image_emb, axis=1, keepdims=True)
    ) / image_norm
    grad_block = (grad_pooled / patches).astype(jnp.bfloat16)
    grad_text_proj = (
        (grad_text_emb - text_unit * jnp.sum(text_unit * grad_text_emb, axis=1, keepdims=True))
        / text_norm
    ).astype(jnp.bfloat16)

    place = lax.axis_index("dp")
    own_block = lax.dynamic_slice_in_dim(grad_block, place * count, count, 0)
    own_text_grad = lax.dynamic_slice_in_dim(grad_text_proj, place * count, count, 0)
    rows = width // lax.axis_size("dp")
    grad_texts = dot(own_text_grad, w_text, ((1,), (1,))).astype(jnp.bfloat16)
    own_features = lax.dynamic_slice_in_dim(texts_all, place * rows, rows, 1)
    grad_w_text = dot(own_features, grad_text_proj, ((0,), (0,)))
    own_columns = lax.dynamic_slice_in_dim(grad_block, place * rows, rows, 1)
    grad_w_out = dot(act_sum_all, own_columns.astype(jnp.float32), ((0,), (0,)), HIGHEST)

    grad_act = dot(own_block, w_out, ((1,), (1,)))
    total = products[0] * grad_act[0:1]
    for i in range(1, count):
        total = total + products[i] * grad_act[i : i + 1]
    grad_w_in = lax.psum_scatter(total, "dp", scatter_dimension=0, tiled=True)
    return (grad_w_in, grad_w_out, grad_w_text, grad_texts)


def solution(mesh):
    placed = (
        P("dp", None, "mp"),
        P(),
        P(None, "mp"),
        P("mp"),
        P("mp", None),
        P("dp", None),
        P(),
        P(),
        P(),
        P(),
    )
    return jax.shard_map(
        shards,
        mesh=mesh,
        in_specs=placed,
        out_specs=(P("dp", "mp"), P("mp", "dp"), P("dp", None), P("dp", None)),
        check_vma=False,
    )
```

```python
import jax
import jax.numpy as jnp
from jax import lax
from jax.experimental import pallas as pl
from jax.experimental.pallas import tpu as pltpu
from jax.sharding import PartitionSpec as P

sqrt_two_pi = 0.7978845608028654
cubic_term = 0.044715
epsilon = 1e-06

NX, NH, NZ, NM = 4, 2, 8, 4
D = 1152
HID = 1076
PATCH = 729
OWN = D // 4
TILE = 256
TILES = 3
ROWS = 18
PAIR = 48
GROUPS_A = ((0, 640),)
GROUPS_B = ((640, 512),)
AHEAD = 3
PADDED = 1088
BATCH = 128
HALF = 64

f32 = jnp.float32
b16 = jnp.bfloat16
MESH = pl.DeviceIdType.MESH


def mm(a, b):
    return lax.dot_general(a, b, (((1,), (0,)), ((), ())), preferred_element_type=f32)


def mm_nt(a, b):
    return lax.dot_general(a, b, (((1,), (1,)), ((), ())), preferred_element_type=f32)


def mm_tn(a, b):
    return lax.dot_general(a, b, (((0,), (0,)), ((), ())), preferred_element_type=f32)


class Refs:
    def __init__(self, values):
        for name, value in values.items():
            setattr(self, name, Refs(value) if isinstance(value, dict) else value)


def iota(shape, axis):
    return lax.broadcasted_iota(jnp.int32, shape, axis)


def three_parts(values):
    high = values.astype(b16)
    rest = values - high.astype(f32)
    middle = rest.astype(b16)
    low = (rest - middle.astype(f32)).astype(b16)
    return high, middle, low


def gelu_and_slope(values):
    squared = values * values
    tanh_part = jnp.tanh(values * (sqrt_two_pi + (sqrt_two_pi * cubic_term) * squared))
    half = 0.5 + 0.5 * tanh_part
    bend = (1.0 - tanh_part * tanh_part) * (
        0.5 * sqrt_two_pi + (1.5 * sqrt_two_pi * cubic_term) * squared
    )
    return values * half, half + values * bend


def kernel(
    images,
    gain_row,
    bias_in,
    bias_text,
    texts,
    scale_ref,
    shift_ref,
    w_in_hbm,
    w_out_hbm,
    w_text_hbm,
    out_in,
    out_out,
    out_text,
    out_texts,
    s,
):
    s = Refs(s)
    w_in, w_tail, w_out, w_text = s.w_in, s.w_tail, s.w_out, s.w_text
    full, normed, slopes, product = s.full, s.normed, s.slopes, s.product
    act_sum, image_sum, grad_act, parts = s.act_sum, s.image_sum, s.grad_act, s.parts

    dp = lax.axis_index("dp")
    mp = lax.axis_index("mp")
    x = dp // (NH * NZ)
    yh = (dp // NZ) % NH
    z = dp % NZ
    slot = yh * (NX * NZ) + x * NZ + z
    yl = mp // 2
    core = mp % 2
    mp_chip = (1 - yl) * 2 + core
    mp_core = yl * 2 + (1 - core)
    mp_far = (1 - yl) * 2 + (1 - core)
    chip, other, far = (dp, mp_chip), (dp, mp_core), (dp, mp_far)

    def at_z(d):
        return ((x * NH + yh) * NZ + (z + d) % NZ, mp)

    def at_x(d):
        return ((((x + d) % NX) * NH + yh) * NZ + z, mp)

    def at_yh():
        return ((x * NH + (1 - yh)) * NZ + z, mp)

    def remote(src, dst, send_sem, recv_sem, device):
        return pltpu.make_async_remote_copy(
            src_ref=src,
            dst_ref=dst,
            send_sem=send_sem,
            recv_sem=recv_sem,
            device_id=device,
            device_id_type=MESH,
        )

    sent = []

    def send(src, dst, send_sem, recv_sem, device):
        copy = remote(src, dst, send_sem, recv_sem, device)
        copy.start()
        sent.append(copy)

    def arrived(dst, send_sem, recv_sem, device):
        remote(dst, dst, send_sem, recv_sem, device).wait_recv()

    loads = [
        pltpu.make_async_copy(w_in_hbm, w_in, s.load_sem.at[0]),
        pltpu.make_async_copy(w_out_hbm, w_out, s.load_sem.at[1]),
        pltpu.make_async_copy(w_text_hbm, w_text, s.load_sem.at[2]),
    ]
    for load in loads:
        load.start()

    barrier = pltpu.get_barrier_semaphore()
    partners = [chip, other, far, at_yh()]
    partners += [at_z(d) for d in range(1, NZ)] + [at_x(d) for d in range(1, NX)]
    for partner in partners:
        pl.semaphore_signal(barrier, inc=1, device_id=partner, device_id_type=MESH)

    for i in range(2):
        for j in range(TILES):
            begin = j * TILE
            width = min(TILE, PATCH - begin)
            if width < TILE:
                full[i * TILES + j, mp] = jnp.zeros((OWN, TILE), b16)
            full[i * TILES + j, mp, :, 0:width] = images[i, :, begin : begin + width]
    s.texts.buf[yh, x, z] = texts[...].astype(f32)

    pl.semaphore_wait(barrier, len(partners))

    class Gather:
        def __init__(self, refs):
            self.buf, self.send_sem, self.recv_sem = refs.buf, refs.send, refs.recv

        def copies(self, stage):
            if stage == 0:
                return [
                    (d, self.buf.at[yh, x, z], self.buf.at[yh, x, (z + NZ - d) % NZ], at_z(d))
                    for d in range(1, NZ)
                ]
            if stage == 1:
                return [
                    (7 + d, self.buf.at[yh, x], self.buf.at[yh, (x + NX - d) % NX], at_x(d))
                    for d in range(1, NX)
                ]
            return [(0, self.buf.at[yh], self.buf.at[1 - yh], at_yh())]

        def start(self, stage):
            for n, own, _, device in self.copies(stage):
                remote(own, own, self.send_sem.at[n], self.recv_sem.at[n], device).start()

        def wait(self, stage):
            for n, _, landed, device in self.copies(stage):
                arrived(landed, self.send_sem.at[n], self.recv_sem.at[n], device)

        def drain(self):
            for stage in range(3):
                for n, own, _, device in self.copies(stage):
                    remote(own, own, self.send_sem.at[n], self.recv_sem.at[n], device).wait_send()

    def tile_copy(k, t):
        source = full.at[t, mp_chip if k == 2 else mp]
        return remote(source, source, s.img.send.at[k, t], s.img.recv.at[k, t], chip if k == 0 else other)

    text_gather = Gather(s.texts)
    for t in range(AHEAD):
        tile_copy(0, t).start()
        tile_copy(1, t).start()
    text_gather.start(0)

    product[...] = jnp.zeros_like(product)
    act_sum[...] = jnp.zeros_like(act_sum)
    image_sum[...] = jnp.zeros_like(image_sum)
    grad_act[...] = jnp.zeros_like(grad_act)
    diagonal = iota((128, 128), 0) == iota((128, 128), 1)
    row_pad = s.row_pad
    for row, column, width in ((gain_row, s.gain_col, D), (bias_in, s.bias_col, HID)):
        row_pad[...] = jnp.zeros_like(row_pad)
        row_pad[:, 0:width] = row[...].reshape(1, width)
        for k in range(D // 128):
            span = slice(128 * k, 128 * k + 128)
            picked = jnp.sum(jnp.where(diagonal, row_pad[:, span], 0.0), axis=1, keepdims=True)
            column[span, :] = jnp.broadcast_to(picked, (128, 128))
    whole = HID // TILE * TILE
    chunks = [(begin, TILE) for begin in range(0, whole, TILE)] + [(whole, PADDED - whole)]
    loads[0].wait()
    tail = (iota((PADDED - whole, HID - whole), 0) == iota((PADDED - whole, HID - whole), 1)).astype(
        b16
    )
    w_tail[...] = mm(tail, w_in[whole:HID, :]).astype(b16)

    def add_product(t):
        i = t // TILES
        for begin, width in chunks:
            span = slice(begin, begin + width)
            product[i, :, span] += mm_nt(normed[t], slopes[t, span, :])

    def work_on(t):
        i = t // TILES
        j = t % TILES
        for h in range(TILE // 128):
            lanes = slice(128 * h, 128 * h + 128)
            total = jnp.zeros((1, 128), f32)
            for m in range(NM):
                total += jnp.sum(full[t, m, :, lanes].astype(f32), axis=0, keepdims=True)
            mean = total * (1.0 / D)
            total = jnp.zeros((1, 128), f32)
            for m in range(NM):
                centered = full[t, m, :, lanes].astype(f32) - mean
                total += jnp.sum(centered * centered, axis=0, keepdims=True)
            factor = lax.rsqrt(total * (1.0 / D) + epsilon)
            for m in range(NM):
                rows = slice(OWN * m, OWN * m + OWN)
                centered = full[t, m, :, lanes].astype(f32) - mean
                normed[t, rows, lanes] = (centered * factor * s.gain_col[rows, :]).astype(b16)
        valid = (iota((8, TILE), 1) + j * TILE < PATCH).astype(b16)
        image_sum[i] += mm_nt(valid, full[t].reshape(D, TILE))
        for begin, width in chunks:
            span = slice(begin, begin + width)
            bias = s.bias_col[span, :]
            weight = w_in[span, :] if begin < whole else w_tail[...]
            before = mm(weight, normed[t]) + jnp.concatenate([bias, bias], axis=1)
            act, slope = gelu_and_slope(before)
            slopes[t, span, :] = slope.astype(b16)
            act_sum[i, :, span] += mm_nt(valid, act.astype(b16))

    def project_texts():
        loads[2].wait()
        for r in range(2):
            s.text_rows[HALF * r : HALF * r + HALF, :] = (
                s.texts.buf[:, :, :, r, :].reshape(HALF, D).astype(b16)
            )
        projected = mm(s.text_rows[...], w_text[...]) + bias_text[...].reshape(1, D)
        norm = jnp.sqrt(jnp.sum(projected * projected, axis=1, keepdims=True) + epsilon)
        unit = projected / norm
        s.text_norm[...] = jnp.broadcast_to(norm, (BATCH, 128))
        s.text_unit[...] = unit
        s.text_emb[...] = unit.astype(b16)

    def tile_step(t, carry):
        arrived(full.at[t, mp_chip], s.img.send.at[0, t], s.img.recv.at[0, t], chip)
        tile_copy(2, t).start()

        @pl.when(t < 2 * TILES - AHEAD)
        def _():
            tile_copy(0, t + AHEAD).start()
            tile_copy(1, t + AHEAD).start()

        @pl.when(t > 0)
        def _():
            add_product(t - 1)

        @pl.when(t == 1)
        def _():
            text_gather.wait(0)
            text_gather.start(1)

        @pl.when(t == 3)
        def _():
            text_gather.wait(1)
            text_gather.start(2)

        @pl.when(t == 5)
        def _():
            text_gather.wait(2)
            project_texts()

        arrived(full.at[t, mp_core], s.img.send.at[1, t], s.img.recv.at[1, t], other)
        arrived(full.at[t, mp_far], s.img.send.at[2, t], s.img.recv.at[2, t], other)
        work_on(t)
        return carry

    lax.fori_loop(0, 2 * TILES, tile_step, 0)

    loads[1].wait()
    row = iota((8, HID), 0)
    split = three_parts(act_sum[0, :, 0:HID]) + three_parts(act_sum[1, :, 0:HID])
    stacked = jnp.zeros((8, HID), f32)
    for k in range(6):
        stacked = jnp.where(row == k, split[k].astype(f32), stacked)
    shares = mm(stacked.astype(b16), w_out[...])
    row = iota((8, D), 0)
    share_0 = jnp.sum(jnp.where(row < 3, shares, 0.0), axis=0, keepdims=True)
    share_1 = jnp.sum(jnp.where((row >= 3) & (row < 6), shares, 0.0), axis=0, keepdims=True)
    first = iota((2, D), 0) == 0
    parts[mp] = jnp.where(first, share_0, share_1)
    group = (chip, other, far)
    for k, partner in enumerate(group):
        own = parts.at[mp]
        send(own, own, s.part.send.at[k], s.part.recv.at[k], partner)
    add_product(2 * TILES - 1)
    for k, source in enumerate((mp_chip, mp_core, mp_far)):
        arrived(parts.at[source], s.part.send.at[k], s.part.recv.at[k], group[k])
    block = parts[0] + parts[1] + parts[2] + parts[3]
    pooled = (jnp.where(first, image_sum[0, 0:2, :], image_sum[1, 0:2, :]) + block) * (1.0 / PATCH)
    pool_gather = Gather(s.pool)
    mine = jnp.where(core == 0, pooled[0:1, :], pooled[1:2, :])
    pooled_high = mine.astype(b16)
    pooled_rest = (mine - pooled_high.astype(f32)).astype(b16)
    rows = (pooled_high.astype(f32), pooled_rest.astype(f32), act_sum[0, 0:1, :], act_sum[1, 0:1, :])
    order = iota((4, D), 0)
    packed = jnp.broadcast_to(rows[0], (4, D))
    for k in range(1, 4):
        packed = jnp.where(order == k, rows[k], packed)
    s.pool.buf[yh, x, z] = packed.astype(b16)
    pool_gather.start(0)

    scale = scale_ref[0]
    shift = shift_ref[0]

    def block_gradient(values):
        norm = jnp.sqrt(jnp.sum(values * values, axis=1, keepdims=True) + epsilon)
        unit = values / norm
        emb = unit.astype(b16)
        logits = scale * mm_nt(emb, s.text_emb[...]) + shift
        if values.shape[0] == 2:
            matches = iota((2, BATCH), 1) == iota((2, BATCH), 0) * HALF + slot
        else:
            matches = iota((BATCH, BATCH), 0) == iota((BATCH, BATCH), 1)
        signs = jnp.where(matches, 1.0, -1.0)
        coef = -signs * jax.nn.sigmoid(-signs * logits)
        weights = (scale * coef).astype(b16)
        grad_emb = mm(weights, s.text_emb[...])
        along = jnp.sum(unit * grad_emb, axis=1, keepdims=True)
        grad_pooled = (grad_emb - unit * along) / norm
        return (grad_pooled * (1.0 / PATCH)).astype(b16), weights, emb

    own_block, _, _ = block_gradient(pooled)
    grad_act[:, 0:HID] = mm_nt(own_block, w_out[...])

    near_z = (at_z(1), at_z(NZ - 1))
    near_x = (at_x(1), at_x(NX - 1))

    def add_into(target, index, begin, count, received):
        for r in range(0, count, 48):
            there = slice(begin + r, begin + r + 48)
            target[index, there, :] = (
                target[index, there, :].astype(f32) + received[r : r + 48, :].astype(f32)
            ).astype(b16)

    class Ring:
        def __init__(self, refs, place, size, near, steps):
            self.buf = refs.buf
            self.recv = refs.right, refs.left
            self.sems = refs.send, refs.recv
            self.place, self.size, self.near, self.steps = place, size, near, steps

        def wait(self, way, k):
            n = way * self.steps[0] + k - 1
            there = self.recv[way].at[k - 1]
            arrived(there, self.sems[0].at[n], self.sems[1].at[n], self.near[way])
            return there

        def step(self, k):
            for way in range(2):
                if k > self.steps[way]:
                    continue
                away = self.steps[way] + 1 - k
                chunk = (self.place + (self.size - away if way else away)) % self.size
                if k > 1:
                    add_into(self.buf, chunk, 0, self.buf.shape[1], self.wait(way, k - 1))
                n = way * self.steps[0] + k - 1
                send(
                    self.buf.at[chunk],
                    self.recv[way].at[k - 1],
                    self.sems[0].at[n],
                    self.sems[1].at[n],
                    self.near[way],
                )

        def finish(self):
            for way in range(2):
                self.wait(way, self.steps[way])

        def total(self, rows):
            value = self.buf[self.place, rows, :].astype(f32)
            for way in range(2):
                value += self.recv[way][self.steps[way] - 1, rows, :].astype(f32)
            return value

    class Group:
        def __init__(self, refs, begin, width):
            self.refs, self.begin, self.width = refs, begin, width
            self.span = slice(begin, begin + width)

        def send_pair(self, ring):
            ring.finish()
            value = ring.total(slice(0, PAIR))
            for h in range(NH):
                self.refs.pair.buf[h] = value[24 * h : 24 * h + 24, :]
            sems = self.refs.pair.send.at[0], self.refs.pair.recv.at[0]
            send(self.refs.pair.buf.at[1 - yh], self.refs.pair.right, *sems, at_yh())

        def result(self):
            sems = self.refs.pair.send.at[0], self.refs.pair.recv.at[0]
            arrived(self.refs.pair.right, *sems, at_yh())
            width = min(self.width, HID - self.begin)
            value = self.refs.pair.buf[yh] + self.refs.pair.right[...]
            out_in[:, self.begin : self.begin + width] = value[0:ROWS, 0:width]

    class GroupA(Group):
        def __init__(self, refs, begin, width, steps):
            super().__init__(refs, begin, width)
            self.z = Ring(refs.ring, z, NZ, near_z, steps)
            self.q1, self.q2, self.q3 = (x + 1) % NX, (x + 2) % NX, (x + 3) % NX

        def combine(self, q):
            for r in range(OWN // 48):
                rows = pl.ds(pl.multiple_of(q * OWN + 48 * r, 16), 48)
                self.refs.stage.buf[q, 48 * r : 48 * r + 48, :] = (
                    product[0, rows, self.span] * grad_act[0:1, self.span]
                    + product[1, rows, self.span] * grad_act[1:2, self.span]
                ).astype(b16)

        def pieces(self, way, k):
            n = way * 3 + k
            return (
                (self.refs.stage.left if way else self.refs.stage.right).at[k],
                self.refs.stage.send.at[n],
                self.refs.stage.recv.at[n],
                near_x[way],
            )

        def send_half(self, q, half, way, k):
            send(self.refs.stage.buf.at[q, pl.ds(144 * half, 144)], *self.pieces(way, k))

        def wait_half(self, way, k):
            arrived(*self.pieces(way, k))

        def first(self):
            self.combine(self.q2)
            self.send_half(self.q2, 0, 0, 0)
            self.send_half(self.q2, 1, 1, 0)

        def second(self):
            self.combine(self.q1)
            self.send_half(self.q1, 1, 0, 1)
            self.combine(self.q3)
            self.send_half(self.q3, 0, 1, 1)

        def third(self):
            self.wait_half(0, 0)
            add_into(self.refs.stage.buf, self.q1, 0, 144, self.refs.stage.right.at[0])
            self.send_half(self.q1, 0, 0, 2)
            self.wait_half(1, 0)
            add_into(self.refs.stage.buf, self.q3, 144, 144, self.refs.stage.left.at[0])
            self.send_half(self.q3, 1, 1, 2)

        def finish_x(self):
            total = self.refs.sum
            for k in range(1, 3):
                self.wait_half(0, k)
                self.wait_half(1, k)
            for half in range(2):
                for r in range(0, 144, 48):
                    there = slice(144 * half + r, 144 * half + r + 48)
                    here = slice(r, r + 48)
                    total[there, :] = (
                        self.refs.stage.buf[x, there, :].astype(f32)
                        + self.refs.stage.right[2 - half, here, :].astype(f32)
                        + self.refs.stage.left[1 + half, here, :].astype(f32)
                    )
            total[OWN : OWN + 8, :] = jnp.zeros((8, self.width), f32)
            for k in range(NZ):
                both = [
                    total[h * (NZ * ROWS) + k * ROWS : h * (NZ * ROWS) + k * ROWS + 24, :]
                    for h in range(NH)
                ]
                self.refs.ring.buf[k] = jnp.concatenate(both, axis=0).astype(b16)

    class GroupB(Group):
        def __init__(self, refs, begin, width, steps):
            super().__init__(refs, begin, width)
            self.z = Ring(refs.stage, z, NZ, near_z, steps)
            self.x = Ring(refs.ring, x, NX, near_x, (2, 1) if steps[0] > steps[1] else (1, 2))

        def pack(self):
            pack = self.refs.pack
            weight_0, weight_1 = grad_act[0:1, self.span], grad_act[1:2, self.span]
            for k in range(NZ):
                for g in range(NX * NH):
                    begin = g * (NZ * ROWS) + k * ROWS
                    source = slice(begin, begin + ROWS)
                    pack[g * ROWS : g * ROWS + ROWS, :] = (
                        product[0, source, self.span] * weight_0
                        + product[1, source, self.span] * weight_1
                    )
                self.refs.stage.buf[k] = pack[...].astype(b16)

        def finish_z(self):
            self.z.finish()
            total = self.refs.sum
            for r in range(0, 144, 48):
                total[r : r + 48, :] = self.z.total(slice(r, r + 48))
            total[144:152, :] = jnp.zeros((8, self.width), f32)
            for k in range(NX):
                both = [
                    total[(k * NH + h) * ROWS : (k * NH + h) * ROWS + 24, :] for h in range(NH)
                ]
                self.refs.ring.buf[k] = jnp.concatenate(both, axis=0).astype(b16)

    a = GroupA(s.a, *GROUPS_A[0], (3, 4))
    b = GroupB(s.b, *GROUPS_B[0], (4, 3))

    pairs = Refs({})

    def pairs_1():
        halves = []
        for buf in (s.pool.buf, s.pool_other):
            both = [buf[:, :, :, r, :].reshape(HALF, D).astype(f32) for r in range(2)]
            halves.append(both[0] + both[1])
        lower = jnp.where(core == 0, halves[0], halves[1])
        upper = jnp.where(core == 0, halves[1], halves[0])
        all_pooled = jnp.concatenate([lower, upper], axis=0)
        block, weights, emb = block_gradient(all_pooled)
        pick = (iota((D, ROWS), 0) == iota((D, ROWS), 1) + dp * ROWS).astype(b16)
        pairs.columns = mm(block, pick).astype(b16)
        pairs.features = mm(s.text_rows[...], pick).astype(b16)
        pairs.weights, pairs.emb = weights, emb

    def pairs_2():
        grad_text = mm_tn(pairs.weights, pairs.emb)
        unit = s.text_unit[...]
        along = jnp.sum(unit * grad_text, axis=1, keepdims=True)
        pairs.proj = ((grad_text - unit * along) / s.text_norm[:, 0:1]).astype(b16)

    def pairs_3():
        acts = jnp.concatenate(
            [s.pool.buf[:, :, :, 2 + r, 0:HID].reshape(HALF, HID) for r in range(2)], axis=0
        )
        out_out[...] = mm_tn(pairs.columns, acts)

    def pairs_4():
        out_text[...] = mm_tn(pairs.features, pairs.proj)
        chosen = (iota((2, BATCH), 1) == iota((2, BATCH), 0) * HALF + slot).astype(b16)
        own_text = mm(chosen, pairs.proj).astype(b16)
        out_texts[...] = mm_nt(own_text, w_text[...]).astype(b16)

    a.first()
    b.pack()
    b.z.step(1)
    a.second()
    pool_gather.wait(0)
    pool_gather.start(1)
    a.third()
    b.z.step(2)
    a.combine(x)
    b.z.step(3)
    pool_gather.wait(1)
    pool_gather.start(2)
    a.finish_x()
    a.z.step(1)
    b.z.step(4)
    a.z.step(2)
    b.finish_z()
    b.x.step(1)
    a.z.step(3)
    pool_gather.wait(2)
    core_sems = s.core.send.at[0], s.core.recv.at[0]
    send(s.pool.buf, s.pool_other, *core_sems, other)
    b.x.step(2)
    a.z.step(4)
    arrived(s.pool_other, *core_sems, other)
    pairs_1()
    b.send_pair(b.x)
    pairs_2()
    a.send_pair(a.z)
    pairs_3()
    pairs_4()
    b.result()
    a.result()
    for copy in sent:
        copy.wait_send()
    for gather in (text_gather, pool_gather):
        gather.drain()

    def drain_tiles(t, carry):
        for k in range(3):
            tile_copy(k, t).wait_send()
        return carry

    lax.fori_loop(0, 2 * TILES, drain_tiles, 0)


def hand_on(*refs):
    sems = refs[8]
    copies = [pltpu.make_async_copy(refs[k], refs[4 + k], sems.at[k]) for k in range(4)]
    for copy in copies:
        copy.start()
    for copy in copies:
        copy.wait()


def shards(images, ln_gain, w_in, b_in, w_out, texts, w_text, b_text, logit_scale, logit_bias):
    vmem = pl.BlockSpec(memory_space=pltpu.VMEM)
    smem = pl.BlockSpec(memory_space=pltpu.SMEM)
    hbm = pl.BlockSpec(memory_space=pl.ANY)
    dma = pltpu.SemaphoreType.DMA
    V = pltpu.VMEM
    def with_sems(count, **buffers):
        return dict(send=dma(count), recv=dma(count), **buffers)

    def ring(kind, shape, steps, width):
        return with_sems(
            (sum(steps),),
            buf=V(shape + (width,), kind),
            right=V((steps[0],) + shape[1:] + (width,), kind),
            left=V((steps[1],) + shape[1:] + (width,), kind),
        )

    def pair(width):
        return with_sems((1,), buf=V((NH, 24, width), f32), right=V((24, width), f32))

    refs = dict(
        w_in=V((HID, D), b16),
        w_tail=V((PADDED - HID // TILE * TILE, D), b16),
        w_out=V((HID, D), b16),
        w_text=V((D, D), b16),
        gain_col=V((D, 128), f32),
        bias_col=V((D, 128), f32),
        row_pad=V((1, D), f32),
        full=V((2 * TILES, NM, OWN, TILE), b16),
        normed=V((2 * TILES, D, TILE), b16),
        slopes=V((2 * TILES, PADDED, TILE), b16),
        act_sum=V((2, 8, D), f32),
        image_sum=V((2, 8, D), f32),
        product=V((2, D, D), f32),
        parts=V((NM, 2, D), f32),
        pool_other=V((NH, NX, NZ, 4, D), b16),
        text_rows=V((BATCH, D), b16),
        text_emb=V((BATCH, D), b16),
        text_unit=V((BATCH, D), f32),
        text_norm=V((BATCH, 128), f32),
        grad_act=V((2, D), f32),
        load_sem=dma((3,)),
        img=with_sems((3, 2 * TILES)),
        part=with_sems((3,)),
        core=with_sems((1,)),
        texts=with_sems((11,), buf=V((NH, NX, NZ, 2, D), f32)),
        pool=with_sems((11,), buf=V((NH, NX, NZ, 4, D), b16)),
    )
    width = GROUPS_A[0][1]
    stage = with_sems(
        (6,),
        buf=V((NX, OWN, width), b16),
        right=V((3, 144, width), b16),
        left=V((3, 144, width), b16),
    )
    refs.update(
        a=dict(
            stage=stage,
            sum=V((OWN + 8, width), f32),
            ring=ring(b16, (NZ, PAIR), (3, 4), width),
            pair=pair(width),
        )
    )
    width = GROUPS_B[0][1]
    refs.update(
        b=dict(
            pack=V((144, width), f32),
            stage=ring(b16, (NZ, 144), (4, 3), width),
            sum=V((152, width), f32),
            ring=ring(b16, (NX, PAIR), (2, 1), width),
            pair=pair(width),
        )
    )
    out_shape = [
        jax.ShapeDtypeStruct((ROWS, HID), f32),
        jax.ShapeDtypeStruct((ROWS, HID), f32),
        jax.ShapeDtypeStruct((ROWS, D), f32),
        jax.ShapeDtypeStruct((2, D), b16),
    ]
    results = pl.pallas_call(
        kernel,
        out_shape=out_shape,
        in_specs=[vmem] * 5 + [smem] * 2 + [hbm] * 3,
        out_specs=[vmem] * 4,
        scratch_shapes=[refs],
        compiler_params=pltpu.CompilerParams(
            collective_id=0, has_side_effects=True, vmem_limit_bytes=58 << 20
        ),
    )(
        images.transpose(0, 2, 1),
        ln_gain,
        b_in,
        b_text,
        texts,
        logit_scale,
        logit_bias,
        w_in.T,
        w_out,
        w_text,
    )
    grad_in, grad_out, grad_text, grad_texts = pl.pallas_call(
        hand_on,
        out_shape=out_shape,
        in_specs=[hbm] * 4,
        out_specs=[hbm] * 4,
        scratch_shapes=[dma((4,))],
        compiler_params=pltpu.CompilerParams(vmem_limit_bytes=58 << 20),
    )(*results)
    return grad_in, grad_out.T, grad_text, grad_texts


def solution(mesh):
    placed = (
        P("dp", None, "mp"),
        P(),
        P(None, "mp"),
        P("mp"),
        P("mp", None),
        P("dp", None),
        P(),
        P(),
        P(),
        P(),
    )
    return jax.shard_map(
        shards,
        mesh=mesh,
        in_specs=placed,
        out_specs=(P("dp", "mp"), P("mp", "dp"), P("dp", None), P("dp", None)),
        check_vma=False,
    )
```

```python
import jax
import jax.numpy as jnp
from jax import lax
from jax.experimental import pallas as pl
from jax.experimental.pallas import tpu as pltpu
from jax.sharding import PartitionSpec as P

sqrt_two_pi = 0.7978845608028654
cubic_term = 0.044715
epsilon = 1e-06

NX, NH, NZ, NM = 4, 2, 8, 4
D = 1152
HID = 1076
PATCH = 729
OWN = D // 4
TILE = 256
TILES = 3
ROWS = 18
PAIR = 48
GROUPS_A = ((0, 384), (384, 256))
GROUPS_B = ((640, 256), (896, 256))
AHEAD = 3
PADDED = 1088
BATCH = 128
HALF = 64

f32 = jnp.float32
b16 = jnp.bfloat16
MESH = pl.DeviceIdType.MESH


def mm(a, b):
    return lax.dot_general(a, b, (((1,), (0,)), ((), ())), preferred_element_type=f32)


def mm_nt(a, b):
    return lax.dot_general(a, b, (((1,), (1,)), ((), ())), preferred_element_type=f32)


def mm_tn(a, b):
    return lax.dot_general(a, b, (((0,), (0,)), ((), ())), preferred_element_type=f32)


class Refs:
    def __init__(self, values):
        for name, value in values.items():
            if isinstance(value, (tuple, list)):
                value = [Refs(part) for part in value]
            setattr(self, name, Refs(value) if isinstance(value, dict) else value)


def iota(shape, axis):
    return lax.broadcasted_iota(jnp.int32, shape, axis)


def three_parts(values):
    high = values.astype(b16)
    rest = values - high.astype(f32)
    middle = rest.astype(b16)
    low = (rest - middle.astype(f32)).astype(b16)
    return high, middle, low


def gelu_and_slope(values):
    squared = values * values
    tanh_part = jnp.tanh(values * (sqrt_two_pi + (sqrt_two_pi * cubic_term) * squared))
    half = 0.5 + 0.5 * tanh_part
    bend = (1.0 - tanh_part * tanh_part) * (
        0.5 * sqrt_two_pi + (1.5 * sqrt_two_pi * cubic_term) * squared
    )
    return values * half, half + values * bend


def kernel(
    images,
    gain_row,
    bias_in,
    bias_text,
    texts,
    scale_ref,
    shift_ref,
    w_in_hbm,
    w_out_hbm,
    w_text_hbm,
    out_in,
    out_out,
    out_text,
    out_texts,
    s,
):
    s = Refs(s)
    w_in, w_tail, w_out, w_text = s.w_in, s.w_tail, s.w_out, s.w_text
    full, normed, slopes, product = s.full, s.normed, s.slopes, s.product
    act_sum, image_sum, grad_act, parts = s.act_sum, s.image_sum, s.grad_act, s.parts

    dp = lax.axis_index("dp")
    mp = lax.axis_index("mp")
    x = dp // (NH * NZ)
    yh = (dp // NZ) % NH
    z = dp % NZ
    slot = (x * NZ + z) * NH + yh
    yl = mp // 2
    core = mp % 2
    mp_chip = (1 - yl) * 2 + core
    mp_core = yl * 2 + (1 - core)
    mp_far = (1 - yl) * 2 + (1 - core)
    chip, other, far = (dp, mp_chip), (dp, mp_core), (dp, mp_far)

    def at_z(d):
        return ((x * NH + yh) * NZ + (z + d) % NZ, mp)

    def at_x(d):
        return ((((x + d) % NX) * NH + yh) * NZ + z, mp)

    def at_yh():
        return ((x * NH + (1 - yh)) * NZ + z, mp)

    def remote(src, dst, send_sem, recv_sem, device):
        return pltpu.make_async_remote_copy(
            src_ref=src,
            dst_ref=dst,
            send_sem=send_sem,
            recv_sem=recv_sem,
            device_id=device,
            device_id_type=MESH,
        )

    sent = []

    def send(src, dst, send_sem, recv_sem, device):
        copy = remote(src, dst, send_sem, recv_sem, device)
        copy.start()
        sent.append(copy)

    def arrived(dst, send_sem, recv_sem, device):
        remote(dst, dst, send_sem, recv_sem, device).wait_recv()

    loads = [
        pltpu.make_async_copy(w_in_hbm, w_in, s.load_sem.at[0]),
        pltpu.make_async_copy(w_out_hbm, w_out, s.load_sem.at[1]),
        pltpu.make_async_copy(w_text_hbm, w_text, s.load_sem.at[2]),
    ]
    for load in loads:
        load.start()

    barrier = pltpu.get_barrier_semaphore()
    partners = [chip, other, far, at_yh()]
    partners += [at_z(d) for d in range(1, NZ)] + [at_x(d) for d in range(1, NX)]
    for partner in partners:
        pl.semaphore_signal(barrier, inc=1, device_id=partner, device_id_type=MESH)

    for i in range(2):
        for j in range(TILES):
            begin = j * TILE
            width = min(TILE, PATCH - begin)
            if width < TILE:
                full[i * TILES + j, mp] = jnp.zeros((OWN, TILE), b16)
            full[i * TILES + j, mp, :, 0:width] = images[i, :, begin : begin + width]
    s.texts.buf[x, z, yh] = texts[...].astype(f32)

    pl.semaphore_wait(barrier, len(partners))

    class Gather:
        def __init__(self, refs):
            self.buf, self.send_sem, self.recv_sem = refs.buf, refs.send, refs.recv

        def start(self, stage):
            for n, own, _, device in self.copies(stage):
                remote(own, own, self.send_sem.at[n], self.recv_sem.at[n], device).start()

        def wait(self, stage):
            for n, _, landed, device in self.copies(stage):
                arrived(landed, self.send_sem.at[n], self.recv_sem.at[n], device)

        def drain(self, stages):
            for stage in range(stages):
                for n, own, _, device in self.copies(stage):
                    remote(own, own, self.send_sem.at[n], self.recv_sem.at[n], device).wait_send()

    class TextGather(Gather):
        def copies(self, stage):
            at = self.buf.at
            if stage == 0:
                return [(0, at[x, z, yh], at[x, z, 1 - yh], at_yh())]
            if stage == 1:
                return [(d, at[x, z], at[x, (z + NZ - d) % NZ], at_z(d)) for d in range(1, NZ)]
            return [(7 + d, at[x], at[(x + NX - d) % NX], at_x(d)) for d in range(1, NX)]

    class PoolGather(Gather):
        def copies(self, stage):
            at = self.buf.at
            if stage == 0:
                return [
                    (d, at[x, yh, z], at[x, yh, (z + NZ - d) % NZ], at_z(d)) for d in range(1, NZ)
                ]
            if stage == 1:
                return [(0, at[x, yh], at[x, 1 - yh], at_yh())]
            before, after = (x + NX - 1) % NX, (x + 1) % NX
            if stage == 2:
                return [(8, at[x], at[before], at_x(1)), (9, at[x], at[after], at_x(NX - 1))]
            far = (x + 2) % NX
            return [
                (10, at[before, 0], at[far, 0], at_x(1)),
                (11, at[after, 1], at[far, 1], at_x(NX - 1)),
            ]

    def tile_copy(k, t):
        source = full.at[t, mp_chip if k == 2 else mp]
        return remote(source, source, s.img.send.at[k, t], s.img.recv.at[k, t], chip if k == 0 else other)

    text_gather = TextGather(s.texts)
    for t in range(AHEAD):
        tile_copy(0, t).start()
        tile_copy(1, t).start()
    text_gather.start(0)

    product[...] = jnp.zeros_like(product)
    act_sum[...] = jnp.zeros_like(act_sum)
    image_sum[...] = jnp.zeros_like(image_sum)
    grad_act[...] = jnp.zeros_like(grad_act)
    diagonal = iota((128, 128), 0) == iota((128, 128), 1)
    row_pad = s.row_pad
    for row, column, width in ((gain_row, s.gain_col, D), (bias_in, s.bias_col, HID)):
        row_pad[...] = jnp.zeros_like(row_pad)
        row_pad[:, 0:width] = row[...].reshape(1, width)
        for k in range(D // 128):
            span = slice(128 * k, 128 * k + 128)
            picked = jnp.sum(jnp.where(diagonal, row_pad[:, span], 0.0), axis=1, keepdims=True)
            column[span, :] = jnp.broadcast_to(picked, (128, 128))
    whole = HID // TILE * TILE
    chunks = [(begin, TILE) for begin in range(0, whole, TILE)] + [(whole, PADDED - whole)]
    loads[0].wait()
    tail = (iota((PADDED - whole, HID - whole), 0) == iota((PADDED - whole, HID - whole), 1)).astype(
        b16
    )
    w_tail[...] = mm(tail, w_in[whole:HID, :]).astype(b16)

    def add_product(t):
        i = t // TILES
        for begin, width in chunks:
            span = slice(begin, begin + width)
            product[i, :, span] += mm_nt(normed[t], slopes[t, span, :])

    def work_on(t):
        i = t // TILES
        j = t % TILES
        for h in range(TILE // 128):
            lanes = slice(128 * h, 128 * h + 128)
            total = jnp.zeros((1, 128), f32)
            for m in range(NM):
                total += jnp.sum(full[t, m, :, lanes].astype(f32), axis=0, keepdims=True)
            mean = total * (1.0 / D)
            total = jnp.zeros((1, 128), f32)
            for m in range(NM):
                centered = full[t, m, :, lanes].astype(f32) - mean
                total += jnp.sum(centered * centered, axis=0, keepdims=True)
            factor = lax.rsqrt(total * (1.0 / D) + epsilon)
            for m in range(NM):
                rows = slice(OWN * m, OWN * m + OWN)
                centered = full[t, m, :, lanes].astype(f32) - mean
                normed[t, rows, lanes] = (centered * factor * s.gain_col[rows, :]).astype(b16)
        valid = (iota((8, TILE), 1) + j * TILE < PATCH).astype(b16)
        image_sum[i] += mm_nt(valid, full[t].reshape(D, TILE))
        for begin, width in chunks:
            span = slice(begin, begin + width)
            bias = s.bias_col[span, :]
            weight = w_in[span, :] if begin < whole else w_tail[...]
            before = mm(weight, normed[t]) + jnp.concatenate([bias, bias], axis=1)
            act, slope = gelu_and_slope(before)
            slopes[t, span, :] = slope.astype(b16)
            act_sum[i, :, span] += mm_nt(valid, act.astype(b16))

    def project_texts():
        loads[2].wait()
        for r in range(2):
            s.text_rows[HALF * r : HALF * r + HALF, :] = (
                s.texts.buf[:, :, :, r, :].reshape(HALF, D).astype(b16)
            )
        projected = mm(s.text_rows[...], w_text[...]) + bias_text[...].reshape(1, D)
        norm = jnp.sqrt(jnp.sum(projected * projected, axis=1, keepdims=True) + epsilon)
        unit = projected / norm
        s.text_norm[...] = jnp.broadcast_to(norm, (BATCH, 128))
        s.text_unit[...] = unit
        s.text_emb[...] = unit.astype(b16)

    def tile_step(t, carry):
        arrived(full.at[t, mp_chip], s.img.send.at[0, t], s.img.recv.at[0, t], chip)
        tile_copy(2, t).start()

        @pl.when(t < 2 * TILES - AHEAD)
        def _():
            tile_copy(0, t + AHEAD).start()
            tile_copy(1, t + AHEAD).start()

        @pl.when(t > 0)
        def _():
            add_product(t - 1)

        @pl.when(t == 1)
        def _():
            text_gather.wait(0)
            text_gather.start(1)

        @pl.when(t == 3)
        def _():
            text_gather.wait(1)
            text_gather.start(2)

        @pl.when(t == 5)
        def _():
            text_gather.wait(2)
            project_texts()

        arrived(full.at[t, mp_core], s.img.send.at[1, t], s.img.recv.at[1, t], other)
        arrived(full.at[t, mp_far], s.img.send.at[2, t], s.img.recv.at[2, t], other)
        work_on(t)
        return carry

    lax.fori_loop(0, 2 * TILES, tile_step, 0)

    loads[1].wait()
    row = iota((8, HID), 0)
    split = three_parts(act_sum[0, :, 0:HID]) + three_parts(act_sum[1, :, 0:HID])
    stacked = jnp.zeros((8, HID), f32)
    for k in range(6):
        stacked = jnp.where(row == k, split[k].astype(f32), stacked)
    shares = mm(stacked.astype(b16), w_out[...])
    row = iota((8, D), 0)
    share_0 = jnp.sum(jnp.where(row < 3, shares, 0.0), axis=0, keepdims=True)
    share_1 = jnp.sum(jnp.where((row >= 3) & (row < 6), shares, 0.0), axis=0, keepdims=True)
    first = iota((2, D), 0) == 0
    parts[mp] = jnp.where(first, share_0, share_1)
    group = (chip, other, far)
    for k, partner in enumerate(group):
        own = parts.at[mp]
        send(own, own, s.part.send.at[k], s.part.recv.at[k], partner)
    add_product(2 * TILES - 1)
    for k, source in enumerate((mp_chip, mp_core, mp_far)):
        arrived(parts.at[source], s.part.send.at[k], s.part.recv.at[k], group[k])
    block = parts[0] + parts[1] + parts[2] + parts[3]
    pooled = (jnp.where(first, image_sum[0, 0:2, :], image_sum[1, 0:2, :]) + block) * (1.0 / PATCH)
    pool_gather = PoolGather(s.pool)
    mine = jnp.where(core == 0, pooled[0:1, :], pooled[1:2, :])
    pooled_high = mine.astype(b16)
    pooled_rest = (mine - pooled_high.astype(f32)).astype(b16)
    rows = (pooled_high.astype(f32), pooled_rest.astype(f32), act_sum[0, 0:1, :], act_sum[1, 0:1, :])
    order = iota((4, D), 0)
    packed = jnp.broadcast_to(rows[0], (4, D))
    for k in range(1, 4):
        packed = jnp.where(order == k, rows[k], packed)
    s.pool.buf[x, yh, z] = packed.astype(b16)
    pool_gather.start(0)

    scale = scale_ref[0]
    shift = shift_ref[0]

    def block_gradient(values):
        norm = jnp.sqrt(jnp.sum(values * values, axis=1, keepdims=True) + epsilon)
        unit = values / norm
        emb = unit.astype(b16)
        logits = scale * mm_nt(emb, s.text_emb[...]) + shift
        if values.shape[0] == 2:
            matches = iota((2, BATCH), 1) == iota((2, BATCH), 0) * HALF + slot
        else:
            at = iota((BATCH, BATCH), 0)
            matches = (at & 112) + ((at & 7) << 1) + ((at >> 3) & 1) == iota((BATCH, BATCH), 1)
        signs = jnp.where(matches, 1.0, -1.0)
        coef = -signs * jax.nn.sigmoid(-signs * logits)
        weights = (scale * coef).astype(b16)
        grad_emb = mm(weights, s.text_emb[...])
        along = jnp.sum(unit * grad_emb, axis=1, keepdims=True)
        grad_pooled = (grad_emb - unit * along) / norm
        return (grad_pooled * (1.0 / PATCH)).astype(b16), weights, emb

    own_block, _, _ = block_gradient(pooled)
    grad_act[:, 0:HID] = mm_nt(own_block, w_out[...])

    near_z = (at_z(1), at_z(NZ - 1))
    near_x = (at_x(1), at_x(NX - 1))

    def add_into(target, index, begin, count, received):
        for r in range(0, count, 48):
            there = slice(begin + r, begin + r + 48)
            target[index, there, :] = (
                target[index, there, :].astype(f32) + received[r : r + 48, :].astype(f32)
            ).astype(b16)

    class Ring:
        def __init__(self, refs, place, size, near, steps):
            self.buf = refs.buf
            self.recv = refs.right, refs.left
            self.sems = refs.send, refs.recv
            self.place, self.size, self.near, self.steps = place, size, near, steps

        def wait(self, way, k):
            n = way * self.steps[0] + k - 1
            there = self.recv[way].at[k - 1]
            arrived(there, self.sems[0].at[n], self.sems[1].at[n], self.near[way])
            return there

        def step(self, k):
            for way in range(2):
                if k > self.steps[way]:
                    continue
                away = self.steps[way] + 1 - k
                chunk = (self.place + (self.size - away if way else away)) % self.size
                if k > 1:
                    add_into(self.buf, chunk, 0, self.buf.shape[1], self.wait(way, k - 1))
                n = way * self.steps[0] + k - 1
                send(
                    self.buf.at[chunk],
                    self.recv[way].at[k - 1],
                    self.sems[0].at[n],
                    self.sems[1].at[n],
                    self.near[way],
                )

        def finish(self):
            for way in range(2):
                self.wait(way, self.steps[way])

        def total(self, rows):
            value = self.buf[self.place, rows, :].astype(f32)
            for way in range(2):
                value += self.recv[way][self.steps[way] - 1, rows, :].astype(f32)
            return value

    class Group:
        def __init__(self, refs, begin, width):
            self.refs, self.begin, self.width = refs, begin, width
            self.span = slice(begin, begin + width)

        def send_pair(self):
            value = self.last_total()
            for h in range(NH):
                self.refs.pair.buf[h] = value[24 * h : 24 * h + 24, :]
            sems = self.refs.pair.send.at[0], self.refs.pair.recv.at[0]
            send(self.refs.pair.buf.at[1 - yh], self.refs.pair.right, *sems, at_yh())

        def result(self):
            sems = self.refs.pair.send.at[0], self.refs.pair.recv.at[0]
            arrived(self.refs.pair.right, *sems, at_yh())
            width = min(self.width, HID - self.begin)
            value = self.refs.pair.buf[yh] + self.refs.pair.right[...]
            out_in[:, self.begin : self.begin + width] = value[0:ROWS, 0:width]

    class GroupA(Group):
        def __init__(self, refs, begin, width, steps):
            super().__init__(refs, begin, width)
            self.z = Ring(refs.ring, z, NZ, near_z, steps)
            self.q1, self.q2, self.q3 = (x + 1) % NX, (x + 2) % NX, (x + 3) % NX

        def combine(self, q):
            for r in range(OWN // 48):
                rows = pl.ds(pl.multiple_of(q * OWN + 48 * r, 16), 48)
                self.refs.stage.buf[q, 48 * r : 48 * r + 48, :] = (
                    product[0, rows, self.span] * grad_act[0:1, self.span]
                    + product[1, rows, self.span] * grad_act[1:2, self.span]
                ).astype(b16)

        def pieces(self, way, k):
            n = way * 3 + k
            return (
                (self.refs.stage.left if way else self.refs.stage.right).at[k],
                self.refs.stage.send.at[n],
                self.refs.stage.recv.at[n],
                near_x[way],
            )

        def send_half(self, q, half, way, k):
            send(self.refs.stage.buf.at[q, pl.ds(144 * half, 144)], *self.pieces(way, k))

        def wait_half(self, way, k):
            arrived(*self.pieces(way, k))

        def first(self):
            self.combine(self.q2)
            self.send_half(self.q2, 0, 0, 0)
            self.send_half(self.q2, 1, 1, 0)

        def second(self):
            self.combine(self.q1)
            self.send_half(self.q1, 1, 0, 1)
            self.combine(self.q3)
            self.send_half(self.q3, 0, 1, 1)

        def third(self):
            self.wait_half(0, 0)
            add_into(self.refs.stage.buf, self.q1, 0, 144, self.refs.stage.right.at[0])
            self.send_half(self.q1, 0, 0, 2)
            self.wait_half(1, 0)
            add_into(self.refs.stage.buf, self.q3, 144, 144, self.refs.stage.left.at[0])
            self.send_half(self.q3, 1, 1, 2)

        def finish_x(self):
            total = self.refs.sum
            for k in range(1, 3):
                self.wait_half(0, k)
                self.wait_half(1, k)
            for half in range(2):
                for r in range(0, 144, 48):
                    there = slice(144 * half + r, 144 * half + r + 48)
                    here = slice(r, r + 48)
                    total[there, :] = (
                        self.refs.stage.buf[x, there, :].astype(f32)
                        + self.refs.stage.right[2 - half, here, :].astype(f32)
                        + self.refs.stage.left[1 + half, here, :].astype(f32)
                    )
            total[OWN : OWN + 8, :] = jnp.zeros((8, self.width), f32)
            for k in range(NZ):
                both = [
                    total[h * (NZ * ROWS) + k * ROWS : h * (NZ * ROWS) + k * ROWS + 24, :]
                    for h in range(NH)
                ]
                self.refs.ring.buf[k] = jnp.concatenate(both, axis=0).astype(b16)

        def last_total(self):
            self.z.finish()
            return self.z.total(slice(0, PAIR))

    class GroupB(Group):
        def __init__(self, refs, begin, width, steps):
            super().__init__(refs, begin, width)
            self.z = Ring(refs.stage, z, NZ, near_z, steps)

        def pack(self):
            pack = self.refs.pack
            weight_0, weight_1 = grad_act[0:1, self.span], grad_act[1:2, self.span]
            for k in range(NZ):
                for g in range(NX * NH):
                    begin = g * (NZ * ROWS) + k * ROWS
                    source = slice(begin, begin + ROWS)
                    pack[g * ROWS : g * ROWS + ROWS, :] = (
                        product[0, source, self.span] * weight_0
                        + product[1, source, self.span] * weight_1
                    )
                self.refs.stage.buf[k] = pack[...].astype(b16)

        def finish_z(self):
            self.z.finish()
            total = self.refs.sum
            for r in range(0, 144, 48):
                total[r : r + 48, :] = self.z.total(slice(r, r + 48))
            total[144:152, :] = jnp.zeros((8, self.width), f32)
            for k in range(NX):
                both = [
                    total[(k * NH + h) * ROWS : (k * NH + h) * ROWS + 24, :] for h in range(NH)
                ]
                self.refs.ring.buf[k] = jnp.concatenate(both, axis=0).astype(b16)

        def send_x(self):
            refs = self.refs.ring
            for d in range(1, NX):
                source, sems = refs.buf.at[(x + d) % NX], (refs.send.at[d - 1], refs.recv.at[d - 1])
                send(source, refs.right.at[d - 1], *sems, at_x(d))

        def last_total(self):
            refs = self.refs.ring
            value = refs.buf[x].astype(f32)
            for d in range(1, NX):
                arrived(refs.right.at[d - 1], refs.send.at[d - 1], refs.recv.at[d - 1], at_x(d))
                value += refs.right[d - 1].astype(f32)
            return value

    a1 = GroupA(s.a[0], *GROUPS_A[0], (3, 4))
    a2 = GroupA(s.a[1], *GROUPS_A[1], (4, 3))
    b1 = GroupB(s.b[0], *GROUPS_B[0], (4, 3))
    b2 = GroupB(s.b[1], *GROUPS_B[1], (3, 4))

    pairs = Refs({})

    def pairs_1():
        halves = []
        for buf in (s.pool.buf, s.pool_other):
            both = [buf[:, :, :, r, :].reshape(HALF, D).astype(f32) for r in range(2)]
            halves.append(both[0] + both[1])
        lower = jnp.where(core == 0, halves[0], halves[1])
        upper = jnp.where(core == 0, halves[1], halves[0])
        all_pooled = jnp.concatenate([lower, upper], axis=0)
        block, weights, emb = block_gradient(all_pooled)
        pick = (iota((D, ROWS), 0) == iota((D, ROWS), 1) + dp * ROWS).astype(b16)
        pairs.columns = mm(block, pick).astype(b16)
        pairs.features = mm(s.text_rows[...], pick).astype(b16)
        pairs.weights, pairs.emb = weights, emb

    def pairs_2():
        grad_text = mm_tn(pairs.weights, pairs.emb)
        unit = s.text_unit[...]
        along = jnp.sum(unit * grad_text, axis=1, keepdims=True)
        pairs.proj = ((grad_text - unit * along) / s.text_norm[:, 0:1]).astype(b16)

    def pairs_3():
        acts = jnp.concatenate(
            [s.pool.buf[:, :, :, 2 + r, 0:HID].reshape(HALF, HID) for r in range(2)], axis=0
        )
        out_out[...] = mm_tn(pairs.columns, acts)

    def pairs_4():
        out_text[...] = mm_tn(pairs.features, pairs.proj)
        chosen = (iota((2, BATCH), 1) == iota((2, BATCH), 0) * HALF + slot).astype(b16)
        own_text = mm(chosen, pairs.proj).astype(b16)
        out_texts[...] = mm_nt(own_text, w_text[...]).astype(b16)

    a1.first()
    a2.first()
    b1.pack()
    b1.z.step(1)
    a1.second()
    b2.pack()
    b2.z.step(1)
    a2.second()
    pool_gather.wait(0)
    pool_gather.start(1)
    a1.third()
    b1.z.step(2)
    a2.third()
    b2.z.step(2)
    a1.combine(x)
    a2.combine(x)
    b1.z.step(3)
    pool_gather.wait(1)
    pool_gather.start(2)
    b2.z.step(3)
    a1.finish_x()
    a1.z.step(1)
    b1.z.step(4)
    a2.finish_x()
    a2.z.step(1)
    b2.z.step(4)
    a1.z.step(2)
    a2.z.step(2)
    b1.finish_z()
    b1.send_x()
    pool_gather.wait(2)
    pool_gather.start(3)
    b2.finish_z()
    b2.send_x()
    a1.z.step(3)
    a2.z.step(3)
    b1.send_pair()
    a1.z.step(4)
    b2.send_pair()
    a2.z.step(4)
    pool_gather.wait(3)
    core_sems = s.core.send.at[0], s.core.recv.at[0]
    send(s.pool.buf, s.pool_other, *core_sems, other)
    a1.send_pair()
    a2.send_pair()
    arrived(s.pool_other, *core_sems, other)
    pairs_1()
    pairs_2()
    pairs_3()
    pairs_4()
    for group in (b1, b2, a1, a2):
        group.result()
    for copy in sent:
        copy.wait_send()
    text_gather.drain(3)
    pool_gather.drain(4)

    def drain_tiles(t, carry):
        for k in range(3):
            tile_copy(k, t).wait_send()
        return carry

    lax.fori_loop(0, 2 * TILES, drain_tiles, 0)


def hand_on(*refs):
    for k in range(4):
        refs[4 + k][...] = refs[k][...]


def shards(images, ln_gain, w_in, b_in, w_out, texts, w_text, b_text, logit_scale, logit_bias):
    vmem = pl.BlockSpec(memory_space=pltpu.VMEM)
    smem = pl.BlockSpec(memory_space=pltpu.SMEM)
    hbm = pl.BlockSpec(memory_space=pl.ANY)
    dma = pltpu.SemaphoreType.DMA
    V = pltpu.VMEM
    def with_sems(count, **buffers):
        return dict(send=dma(count), recv=dma(count), **buffers)

    def ring(kind, shape, steps, width):
        return with_sems(
            (sum(steps),),
            buf=V(shape + (width,), kind),
            right=V((steps[0],) + shape[1:] + (width,), kind),
            left=V((steps[1],) + shape[1:] + (width,), kind),
        )

    def pair(width):
        return with_sems((1,), buf=V((NH, 24, width), f32), right=V((24, width), f32))

    refs = dict(
        w_in=V((HID, D), b16),
        w_tail=V((PADDED - HID // TILE * TILE, D), b16),
        w_out=V((HID, D), b16),
        w_text=V((D, D), b16),
        gain_col=V((D, 128), f32),
        bias_col=V((D, 128), f32),
        row_pad=V((1, D), f32),
        full=V((2 * TILES, NM, OWN, TILE), b16),
        normed=V((2 * TILES, D, TILE), b16),
        slopes=V((2 * TILES, PADDED, TILE), b16),
        act_sum=V((2, 8, D), f32),
        image_sum=V((2, 8, D), f32),
        product=V((2, D, D), f32),
        parts=V((NM, 2, D), f32),
        pool_other=V((NX, NH, NZ, 4, D), b16),
        text_rows=V((BATCH, D), b16),
        text_emb=V((BATCH, D), b16),
        text_unit=V((BATCH, D), f32),
        text_norm=V((BATCH, 128), f32),
        grad_act=V((2, D), f32),
        load_sem=dma((3,)),
        img=with_sems((3, 2 * TILES)),
        part=with_sems((3,)),
        core=with_sems((1,)),
        texts=with_sems((11,), buf=V((NX, NZ, NH, 2, D), f32)),
        pool=with_sems((12,), buf=V((NX, NH, NZ, 4, D), b16)),
    )
    def group_a(width, steps):
        stage = with_sems(
            (6,),
            buf=V((NX, OWN, width), b16),
            right=V((3, 144, width), b16),
            left=V((3, 144, width), b16),
        )
        return dict(
            stage=stage,
            sum=V((OWN + 8, width), f32),
            ring=ring(b16, (NZ, PAIR), steps, width),
            pair=pair(width),
        )

    def group_b(width, steps):
        return dict(
            pack=V((144, width), f32),
            stage=ring(b16, (NZ, 144), steps, width),
            sum=V((152, width), f32),
            ring=with_sems(
                (NX - 1,), buf=V((NX, PAIR, width), b16), right=V((NX - 1, PAIR, width), b16)
            ),
            pair=pair(width),
        )

    refs.update(
        a=[group_a(GROUPS_A[0][1], (3, 4)), group_a(GROUPS_A[1][1], (4, 3))],
        b=[group_b(GROUPS_B[0][1], (4, 3)), group_b(GROUPS_B[1][1], (3, 4))],
    )
    out_shape = [
        jax.ShapeDtypeStruct((ROWS, HID), f32),
        jax.ShapeDtypeStruct((ROWS, HID), f32),
        jax.ShapeDtypeStruct((ROWS, D), f32),
        jax.ShapeDtypeStruct((2, D), b16),
    ]
    results = pl.pallas_call(
        kernel,
        out_shape=out_shape,
        in_specs=[vmem] * 5 + [smem] * 2 + [hbm] * 3,
        out_specs=[vmem] * 4,
        scratch_shapes=[refs],
        compiler_params=pltpu.CompilerParams(
            collective_id=0, has_side_effects=True, vmem_limit_bytes=58 << 20
        ),
    )(
        images.transpose(0, 2, 1),
        ln_gain,
        b_in,
        b_text,
        texts,
        logit_scale,
        logit_bias,
        w_in.T,
        w_out,
        w_text,
    )
    grad_in, grad_out, grad_text, grad_texts = pl.pallas_call(
        hand_on,
        out_shape=out_shape,
        in_specs=[vmem] * 4,
        out_specs=[vmem] * 4,
        compiler_params=pltpu.CompilerParams(vmem_limit_bytes=58 << 20),
    )(*results)
    return grad_in, grad_out.T, grad_text, grad_texts


def solution(mesh):
    placed = (
        P("dp", None, "mp"),
        P(),
        P(None, "mp"),
        P("mp"),
        P("mp", None),
        P("dp", None),
        P(),
        P(),
        P(),
        P(),
    )
    return jax.shard_map(
        shards,
        mesh=mesh,
        in_specs=placed,
        out_specs=(P("dp", "mp"), P("mp", "dp"), P("dp", None), P("dp", None)),
        check_vma=False,
    )
```

```python
import jax
import jax.numpy as jnp
from jax import lax
from jax.experimental import pallas as pl
from jax.experimental.pallas import tpu as pltpu
from jax.sharding import PartitionSpec as P

sqrt_two_pi = 0.7978845608028654
cubic_term = 0.044715
epsilon = 1e-06

NX, NH, NZ, NM = 4, 2, 8, 4
D = 1152
HID = 1076
PATCH = 729
OWN = D // 4
TILE = 256
TILES = 3
ROWS = 18
PAIR = 48
GROUPS_A = ((0, 384), (384, 256))
GROUPS_B = ((640, 256), (896, 256))
AHEAD = 3
PADDED = 1088
BATCH = 128
HALF = 64

f32 = jnp.float32
b16 = jnp.bfloat16
MESH = pl.DeviceIdType.MESH


def mm(a, b):
    return lax.dot_general(a, b, (((1,), (0,)), ((), ())), preferred_element_type=f32)


def mm_nt(a, b):
    return lax.dot_general(a, b, (((1,), (1,)), ((), ())), preferred_element_type=f32)


def mm_tn(a, b):
    return lax.dot_general(a, b, (((0,), (0,)), ((), ())), preferred_element_type=f32)


class Refs:
    def __init__(self, values):
        for name, value in values.items():
            if isinstance(value, (tuple, list)):
                value = [Refs(part) for part in value]
            setattr(self, name, Refs(value) if isinstance(value, dict) else value)


def iota(shape, axis):
    return lax.broadcasted_iota(jnp.int32, shape, axis)


def three_parts(values):
    high = values.astype(b16)
    rest = values - high.astype(f32)
    middle = rest.astype(b16)
    low = (rest - middle.astype(f32)).astype(b16)
    return high, middle, low


def gelu_and_slope(values):
    squared = values * values
    tanh_part = jnp.tanh(values * (sqrt_two_pi + (sqrt_two_pi * cubic_term) * squared))
    half = 0.5 + 0.5 * tanh_part
    bend = (1.0 - tanh_part * tanh_part) * (
        0.5 * sqrt_two_pi + (1.5 * sqrt_two_pi * cubic_term) * squared
    )
    return values * half, half + values * bend


def kernel(
    images,
    gain_row,
    bias_in,
    bias_text,
    texts,
    scale_ref,
    shift_ref,
    w_in_hbm,
    w_out_hbm,
    w_text_hbm,
    out_in,
    out_out,
    out_text,
    out_texts,
    s,
):
    s = Refs(s)
    w_in, w_pad, w_out, w_text = s.w_in, s.w_pad, s.w_out, s.w_text
    full, normed, slopes, product = s.full, s.normed, s.slopes, s.product
    act_sum, image_sum, grad_act, parts = s.act_sum, s.image_sum, s.grad_act, s.parts
    act_lanes, before = s.act_lanes, s.before

    dp = lax.axis_index("dp")
    mp = lax.axis_index("mp")
    x = dp // (NH * NZ)
    yh = (dp // NZ) % NH
    z = dp % NZ
    slot = (x * NZ + z) * NH + yh
    yl = mp // 2
    core = mp % 2
    mp_chip = (1 - yl) * 2 + core
    mp_core = yl * 2 + (1 - core)
    mp_far = (1 - yl) * 2 + (1 - core)
    chip, other, far = (dp, mp_chip), (dp, mp_core), (dp, mp_far)

    def at_z(d):
        return ((x * NH + yh) * NZ + (z + d) % NZ, mp)

    def at_x(d):
        return ((((x + d) % NX) * NH + yh) * NZ + z, mp)

    def at_yh():
        return ((x * NH + (1 - yh)) * NZ + z, mp)

    def remote(src, dst, send_sem, recv_sem, device):
        return pltpu.make_async_remote_copy(
            src_ref=src,
            dst_ref=dst,
            send_sem=send_sem,
            recv_sem=recv_sem,
            device_id=device,
            device_id_type=MESH,
        )

    sent = []

    def send(src, dst, send_sem, recv_sem, device):
        copy = remote(src, dst, send_sem, recv_sem, device)
        copy.start()
        sent.append(copy)

    def arrived(dst, send_sem, recv_sem, device):
        remote(dst, dst, send_sem, recv_sem, device).wait_recv()

    loads = [
        pltpu.make_async_copy(w_in_hbm, w_in, s.load_sem.at[0]),
        pltpu.make_async_copy(w_out_hbm, w_out, s.load_sem.at[1]),
        pltpu.make_async_copy(w_text_hbm, w_text, s.load_sem.at[2]),
    ]
    for load in loads:
        load.start()

    barrier = pltpu.get_barrier_semaphore()
    partners = [chip, other, far, at_yh()]
    partners += [at_z(d) for d in range(1, NZ)] + [at_x(d) for d in range(1, NX)]
    for partner in partners:
        pl.semaphore_signal(barrier, inc=1, device_id=partner, device_id_type=MESH)

    for i in range(2):
        for j in range(TILES):
            begin = j * TILE
            width = min(TILE, PATCH - begin)
            if width < TILE:
                full[i * TILES + j, mp] = jnp.zeros((OWN, TILE), b16)
            full[i * TILES + j, mp, :, 0:width] = images[i, :, begin : begin + width]
    s.texts.buf[x, z, yh] = texts[...].astype(f32)

    pl.semaphore_wait(barrier, len(partners))

    class Gather:
        def __init__(self, refs):
            self.buf, self.send_sem, self.recv_sem = refs.buf, refs.send, refs.recv

        def start(self, stage):
            for n, own, _, device in self.copies(stage):
                remote(own, own, self.send_sem.at[n], self.recv_sem.at[n], device).start()

        def wait(self, stage):
            for n, _, landed, device in self.copies(stage):
                arrived(landed, self.send_sem.at[n], self.recv_sem.at[n], device)

        def drain(self, stages):
            for stage in range(stages):
                for n, own, _, device in self.copies(stage):
                    remote(own, own, self.send_sem.at[n], self.recv_sem.at[n], device).wait_send()

    class TextGather(Gather):
        def copies(self, stage):
            at = self.buf.at
            if stage == 0:
                return [(0, at[x, z, yh], at[x, z, 1 - yh], at_yh())]
            if stage == 1:
                return [(d, at[x, z], at[x, (z + NZ - d) % NZ], at_z(d)) for d in range(1, NZ)]
            return [(7 + d, at[x], at[(x + NX - d) % NX], at_x(d)) for d in range(1, NX)]

    class PoolGather(Gather):
        def copies(self, stage):
            at = self.buf.at
            if stage == 0:
                return [
                    (d, at[x, yh, z], at[x, yh, (z + NZ - d) % NZ], at_z(d)) for d in range(1, NZ)
                ]
            if stage == 1:
                return [(0, at[x, yh], at[x, 1 - yh], at_yh())]
            before, after = (x + NX - 1) % NX, (x + 1) % NX
            if stage == 2:
                return [(8, at[x], at[before], at_x(1)), (9, at[x], at[after], at_x(NX - 1))]
            far = (x + 2) % NX
            return [
                (10, at[before, 0], at[far, 0], at_x(1)),
                (11, at[after, 1], at[far, 1], at_x(NX - 1)),
            ]

    def tile_copy(k, t):
        source = full.at[t, mp_chip if k == 2 else mp]
        return remote(source, source, s.img.send.at[k, t], s.img.recv.at[k, t], chip if k == 0 else other)

    text_gather = TextGather(s.texts)
    for t in range(AHEAD):
        tile_copy(0, t).start()
        tile_copy(1, t).start()
    text_gather.start(0)

    product[:, :, PADDED:D] = jnp.zeros((2, D, D - PADDED), f32)
    act_lanes[...] = jnp.zeros_like(act_lanes)
    act_sum[...] = jnp.zeros_like(act_sum)
    image_sum[...] = jnp.zeros_like(image_sum)
    grad_act[...] = jnp.zeros_like(grad_act)
    diagonal = iota((128, 128), 0) == iota((128, 128), 1)
    row_pad = s.row_pad
    for row, column, width in ((gain_row, s.gain_col, D), (bias_in, s.bias_col, HID)):
        row_pad[...] = jnp.zeros_like(row_pad)
        row_pad[:, 0:width] = row[...].reshape(1, width)
        for k in range(D // 128):
            span = slice(128 * k, 128 * k + 128)
            picked = jnp.sum(jnp.where(diagonal, row_pad[:, span], 0.0), axis=1, keepdims=True)
            column[span, :] = jnp.broadcast_to(picked, (128, 128))
    whole = HID // TILE * TILE
    chunks = [(begin, TILE) for begin in range(0, whole, TILE)] + [(whole, PADDED - whole)]
    loads[0].wait()
    tail = (iota((PADDED - whole, HID - whole), 0) == iota((PADDED - whole, HID - whole), 1)).astype(
        b16
    )
    w_pad[0:whole, :] = w_in[0:whole, :]
    w_pad[whole:PADDED, :] = mm(tail, w_in[whole:HID, :]).astype(b16)

    def multiply(i):
        for begin, width in chunks:
            span = slice(begin, begin + width)
            product[i, :, span] = mm_nt(normed[i], slopes[i, span, :])

    def work_on(t):
        i = t // TILES
        j = t % TILES
        patches = pl.ds(pl.multiple_of(j * TILE, TILE), TILE)
        for h in range(TILE // 128):
            lanes = slice(128 * h, 128 * h + 128)
            total = jnp.zeros((1, 128), f32)
            for m in range(NM):
                total += jnp.sum(full[t, m, :, lanes].astype(f32), axis=0, keepdims=True)
            mean = total * (1.0 / D)
            total = jnp.zeros((1, 128), f32)
            for m in range(NM):
                centered = full[t, m, :, lanes].astype(f32) - mean
                total += jnp.sum(centered * centered, axis=0, keepdims=True)
            factor = lax.rsqrt(total * (1.0 / D) + epsilon)
            for m in range(NM):
                rows = slice(OWN * m, OWN * m + OWN)
                centered = full[t, m, :, lanes].astype(f32) - mean
                there = pl.ds(pl.multiple_of(j * TILE + 128 * h, 128), 128)
                normed[i, rows, there] = (centered * factor * s.gain_col[rows, :]).astype(b16)
        image_sum[i] += mm_nt(jnp.ones((8, TILE), b16), full[t].reshape(D, TILE))
        before[...] = mm(w_pad[...], normed[i, :, patches])
        valid = (iota((1, TILE), 1) + j * TILE < PATCH).astype(f32)
        for begin, width in chunks:
            span = slice(begin, begin + width)
            bias = s.bias_col[span, :]
            act, slope = gelu_and_slope(before[span, :] + jnp.concatenate([bias, bias], axis=1))
            slopes[i, span, patches] = slope.astype(b16)
            act = act * valid
            act_lanes[i, span, :] += act[:, 0:128] + act[:, 128:TILE]

    def project_texts():
        loads[2].wait()
        for r in range(2):
            s.text_rows[HALF * r : HALF * r + HALF, :] = (
                s.texts.buf[:, :, :, r, :].reshape(HALF, D).astype(b16)
            )
        projected = mm(s.text_rows[...], w_text[...]) + bias_text[...].reshape(1, D)
        norm = jnp.sqrt(jnp.sum(projected * projected, axis=1, keepdims=True) + epsilon)
        unit = projected / norm
        s.text_norm[...] = jnp.broadcast_to(norm, (BATCH, 128))
        s.text_unit[...] = unit
        s.text_emb[...] = unit.astype(b16)

    def tile_step(t, carry):
        arrived(full.at[t, mp_chip], s.img.send.at[0, t], s.img.recv.at[0, t], chip)
        tile_copy(2, t).start()

        @pl.when(t < 2 * TILES - AHEAD)
        def _():
            tile_copy(0, t + AHEAD).start()
            tile_copy(1, t + AHEAD).start()

        @pl.when(t == TILES)
        def _():
            multiply(0)

        @pl.when(t == 1)
        def _():
            text_gather.wait(0)
            text_gather.start(1)

        @pl.when(t == 3)
        def _():
            text_gather.wait(1)
            text_gather.start(2)

        @pl.when(t == 5)
        def _():
            text_gather.wait(2)
            project_texts()

        arrived(full.at[t, mp_core], s.img.send.at[1, t], s.img.recv.at[1, t], other)
        arrived(full.at[t, mp_far], s.img.send.at[2, t], s.img.recv.at[2, t], other)
        work_on(t)
        return carry

    lax.fori_loop(0, 2 * TILES, tile_step, 0)

    loads[1].wait()
    ones = jnp.ones((8, 128), b16)
    for i in range(2):
        high, middle, low = three_parts(act_lanes[i])
        act_sum[i, :, 0:PADDED] = mm_nt(ones, high) + mm_nt(ones, middle) + mm_nt(ones, low)
    row = iota((8, HID), 0)
    split = three_parts(act_sum[0, :, 0:HID]) + three_parts(act_sum[1, :, 0:HID])
    stacked = jnp.zeros((8, HID), f32)
    for k in range(6):
        stacked = jnp.where(row == k, split[k].astype(f32), stacked)
    shares = mm(stacked.astype(b16), w_out[...])
    row = iota((8, D), 0)
    share_0 = jnp.sum(jnp.where(row < 3, shares, 0.0), axis=0, keepdims=True)
    share_1 = jnp.sum(jnp.where((row >= 3) & (row < 6), shares, 0.0), axis=0, keepdims=True)
    first = iota((2, D), 0) == 0
    parts[mp] = jnp.where(first, share_0, share_1)
    group = (chip, other, far)
    for k, partner in enumerate(group):
        own = parts.at[mp]
        send(own, own, s.part.send.at[k], s.part.recv.at[k], partner)
    multiply(1)
    for k, source in enumerate((mp_chip, mp_core, mp_far)):
        arrived(parts.at[source], s.part.send.at[k], s.part.recv.at[k], group[k])
    block = parts[0] + parts[1] + parts[2] + parts[3]
    pooled = (jnp.where(first, image_sum[0, 0:2, :], image_sum[1, 0:2, :]) + block) * (1.0 / PATCH)
    pool_gather = PoolGather(s.pool)
    mine = jnp.where(core == 0, pooled[0:1, :], pooled[1:2, :])
    pooled_high = mine.astype(b16)
    pooled_rest = (mine - pooled_high.astype(f32)).astype(b16)
    rows = (pooled_high.astype(f32), pooled_rest.astype(f32), act_sum[0, 0:1, :], act_sum[1, 0:1, :])
    order = iota((4, D), 0)
    packed = jnp.broadcast_to(rows[0], (4, D))
    for k in range(1, 4):
        packed = jnp.where(order == k, rows[k], packed)
    s.pool.buf[x, yh, z] = packed.astype(b16)
    pool_gather.start(0)

    scale = scale_ref[0]
    shift = shift_ref[0]

    def block_gradient(values):
        norm = jnp.sqrt(jnp.sum(values * values, axis=1, keepdims=True) + epsilon)
        unit = values / norm
        emb = unit.astype(b16)
        logits = scale * mm_nt(emb, s.text_emb[...]) + shift
        if values.shape[0] == 2:
            matches = iota((2, BATCH), 1) == iota((2, BATCH), 0) * HALF + slot
        else:
            at = iota((BATCH, BATCH), 0)
            matches = (at & 112) + ((at & 7) << 1) + ((at >> 3) & 1) == iota((BATCH, BATCH), 1)
        signs = jnp.where(matches, 1.0, -1.0)
        coef = -signs * jax.nn.sigmoid(-signs * logits)
        weights = (scale * coef).astype(b16)
        grad_emb = mm(weights, s.text_emb[...])
        along = jnp.sum(unit * grad_emb, axis=1, keepdims=True)
        grad_pooled = (grad_emb - unit * along) / norm
        return (grad_pooled * (1.0 / PATCH)).astype(b16), weights, emb

    own_block, _, _ = block_gradient(pooled)
    grad_act[:, 0:HID] = mm_nt(own_block, w_out[...])
    pool_gather.wait(0)
    pool_gather.start(1)

    near_z = (at_z(1), at_z(NZ - 1))
    near_x = (at_x(1), at_x(NX - 1))

    def add_into(target, index, begin, count, received):
        for r in range(0, count, 48):
            there = slice(begin + r, begin + r + 48)
            target[index, there, :] = (
                target[index, there, :].astype(f32) + received[r : r + 48, :].astype(f32)
            ).astype(b16)

    class Ring:
        def __init__(self, refs, place, size, near, steps):
            self.buf = refs.buf
            self.recv = refs.right, refs.left
            self.sems = refs.send, refs.recv
            self.place, self.size, self.near, self.steps = place, size, near, steps

        def wait(self, way, k):
            n = way * self.steps[0] + k - 1
            there = self.recv[way].at[k - 1]
            arrived(there, self.sems[0].at[n], self.sems[1].at[n], self.near[way])
            return there

        def step(self, k):
            for way in range(2):
                if k > self.steps[way]:
                    continue
                away = self.steps[way] + 1 - k
                chunk = (self.place + (self.size - away if way else away)) % self.size
                if k > 1:
                    add_into(self.buf, chunk, 0, self.buf.shape[1], self.wait(way, k - 1))
                n = way * self.steps[0] + k - 1
                send(
                    self.buf.at[chunk],
                    self.recv[way].at[k - 1],
                    self.sems[0].at[n],
                    self.sems[1].at[n],
                    self.near[way],
                )

        def finish(self):
            for way in range(2):
                self.wait(way, self.steps[way])

        def total(self, rows):
            value = self.buf[self.place, rows, :].astype(f32)
            for way in range(2):
                value += self.recv[way][self.steps[way] - 1, rows, :].astype(f32)
            return value

    class Group:
        def __init__(self, refs, begin, width):
            self.refs, self.begin, self.width = refs, begin, width
            self.span = slice(begin, begin + width)

        def send_pair(self):
            value = self.last_total()
            for h in range(NH):
                self.refs.pair.buf[h] = value[24 * h : 24 * h + 24, :]
            sems = self.refs.pair.send.at[0], self.refs.pair.recv.at[0]
            send(self.refs.pair.buf.at[1 - yh], self.refs.pair.right, *sems, at_yh())

        def result(self):
            sems = self.refs.pair.send.at[0], self.refs.pair.recv.at[0]
            arrived(self.refs.pair.right, *sems, at_yh())
            width = min(self.width, HID - self.begin)
            value = self.refs.pair.buf[yh] + self.refs.pair.right[...]
            out_in[:, self.begin : self.begin + width] = value[0:ROWS, 0:width]

    class GroupA(Group):
        def __init__(self, refs, begin, width, steps):
            super().__init__(refs, begin, width)
            self.z = Ring(refs.ring, z, NZ, near_z, steps)
            self.q1, self.q2, self.q3 = (x + 1) % NX, (x + 2) % NX, (x + 3) % NX

        def combine(self, q):
            for r in range(OWN // 48):
                rows = pl.ds(pl.multiple_of(q * OWN + 48 * r, 16), 48)
                self.refs.stage.buf[q, 48 * r : 48 * r + 48, :] = (
                    product[0, rows, self.span] * grad_act[0:1, self.span]
                    + product[1, rows, self.span] * grad_act[1:2, self.span]
                ).astype(b16)

        def pieces(self, way, k):
            n = way * 3 + k
            return (
                (self.refs.stage.left if way else self.refs.stage.right).at[k],
                self.refs.stage.send.at[n],
                self.refs.stage.recv.at[n],
                near_x[way],
            )

        def send_half(self, q, half, way, k):
            send(self.refs.stage.buf.at[q, pl.ds(144 * half, 144)], *self.pieces(way, k))

        def wait_half(self, way, k):
            arrived(*self.pieces(way, k))

        def first(self):
            self.combine(self.q2)
            self.send_half(self.q2, 0, 0, 0)
            self.send_half(self.q2, 1, 1, 0)

        def second(self):
            self.combine(self.q1)
            self.send_half(self.q1, 1, 0, 1)
            self.combine(self.q3)
            self.send_half(self.q3, 0, 1, 1)

        def third(self):
            self.wait_half(0, 0)
            add_into(self.refs.stage.buf, self.q1, 0, 144, self.refs.stage.right.at[0])
            self.send_half(self.q1, 0, 0, 2)
            self.wait_half(1, 0)
            add_into(self.refs.stage.buf, self.q3, 144, 144, self.refs.stage.left.at[0])
            self.send_half(self.q3, 1, 1, 2)

        def finish_x(self):
            total = self.refs.sum
            for k in range(1, 3):
                self.wait_half(0, k)
                self.wait_half(1, k)
            for half in range(2):
                for r in range(0, 144, 48):
                    there = slice(144 * half + r, 144 * half + r + 48)
                    here = slice(r, r + 48)
                    total[there, :] = (
                        self.refs.stage.buf[x, there, :].astype(f32)
                        + self.refs.stage.right[2 - half, here, :].astype(f32)
                        + self.refs.stage.left[1 + half, here, :].astype(f32)
                    )
            total[OWN : OWN + 8, :] = jnp.zeros((8, self.width), f32)
            for k in range(NZ):
                both = [
                    total[h * (NZ * ROWS) + k * ROWS : h * (NZ * ROWS) + k * ROWS + 24, :]
                    for h in range(NH)
                ]
                self.refs.ring.buf[k] = jnp.concatenate(both, axis=0).astype(b16)

        def last_total(self):
            self.z.finish()
            return self.z.total(slice(0, PAIR))

    class GroupB(Group):
        def __init__(self, refs, begin, width, steps):
            super().__init__(refs, begin, width)
            self.z = Ring(refs.stage, z, NZ, near_z, steps)

        def pack(self):
            pack = self.refs.pack
            weight_0, weight_1 = grad_act[0:1, self.span], grad_act[1:2, self.span]
            for k in range(NZ):
                for g in range(NX * NH):
                    begin = g * (NZ * ROWS) + k * ROWS
                    source = slice(begin, begin + ROWS)
                    pack[g * ROWS : g * ROWS + ROWS, :] = (
                        product[0, source, self.span] * weight_0
                        + product[1, source, self.span] * weight_1
                    )
                self.refs.stage.buf[k] = pack[...].astype(b16)

        def finish_z(self):
            self.z.finish()
            total = self.refs.sum
            for r in range(0, 144, 48):
                total[r : r + 48, :] = self.z.total(slice(r, r + 48))
            total[144:152, :] = jnp.zeros((8, self.width), f32)
            for k in range(NX):
                both = [
                    total[(k * NH + h) * ROWS : (k * NH + h) * ROWS + 24, :] for h in range(NH)
                ]
                self.refs.ring.buf[k] = jnp.concatenate(both, axis=0).astype(b16)

        def send_x(self):
            refs = self.refs.ring
            for d in range(1, NX):
                source, sems = refs.buf.at[(x + d) % NX], (refs.send.at[d - 1], refs.recv.at[d - 1])
                send(source, refs.right.at[d - 1], *sems, at_x(d))

        def last_total(self):
            refs = self.refs.ring
            value = refs.buf[x].astype(f32)
            for d in range(1, NX):
                arrived(refs.right.at[d - 1], refs.send.at[d - 1], refs.recv.at[d - 1], at_x(d))
                value += refs.right[d - 1].astype(f32)
            return value

    a1 = GroupA(s.a[0], *GROUPS_A[0], (3, 4))
    a2 = GroupA(s.a[1], *GROUPS_A[1], (4, 3))
    b1 = GroupB(s.b[0], *GROUPS_B[0], (4, 3))
    b2 = GroupB(s.b[1], *GROUPS_B[1], (3, 4))

    pairs = Refs({})

    def pairs_1():
        halves = []
        for buf in (s.pool.buf, s.pool_other):
            both = [buf[:, :, :, r, :].reshape(HALF, D).astype(f32) for r in range(2)]
            halves.append(both[0] + both[1])
        lower = jnp.where(core == 0, halves[0], halves[1])
        upper = jnp.where(core == 0, halves[1], halves[0])
        all_pooled = jnp.concatenate([lower, upper], axis=0)
        block, weights, emb = block_gradient(all_pooled)
        pick = (iota((D, ROWS), 0) == iota((D, ROWS), 1) + dp * ROWS).astype(b16)
        pairs.columns = mm(block, pick).astype(b16)
        pairs.features = mm(s.text_rows[...], pick).astype(b16)
        pairs.weights, pairs.emb = weights, emb

    def pairs_2():
        grad_text = mm_tn(pairs.weights, pairs.emb)
        unit = s.text_unit[...]
        along = jnp.sum(unit * grad_text, axis=1, keepdims=True)
        pairs.proj = ((grad_text - unit * along) / s.text_norm[:, 0:1]).astype(b16)

    def pairs_3():
        for r in range(2):
            s.acts[HALF * r : HALF * r + HALF, :] = s.pool.buf[:, :, :, 2 + r, :].reshape(HALF, D)

    def pairs_4():
        out_out[...] = mm_tn(pairs.columns, s.acts[:, 0:HID])
        out_text[...] = mm_tn(pairs.features, pairs.proj)
        chosen = (iota((2, BATCH), 1) == iota((2, BATCH), 0) * HALF + slot).astype(b16)
        own_text = mm(chosen, pairs.proj).astype(b16)
        out_texts[...] = mm_nt(own_text, w_text[...]).astype(b16)

    a1.first()
    a2.first()
    b1.pack()
    b1.z.step(1)
    a1.second()
    b2.pack()
    b2.z.step(1)
    a2.second()
    a1.third()
    b1.z.step(2)
    a2.third()
    b2.z.step(2)
    pool_gather.wait(1)
    pool_gather.start(2)
    a1.combine(x)
    a2.combine(x)
    b1.z.step(3)
    b2.z.step(3)
    a1.finish_x()
    a1.z.step(1)
    b1.z.step(4)
    a2.finish_x()
    a2.z.step(1)
    pool_gather.wait(2)
    pool_gather.start(3)
    b2.z.step(4)
    a1.z.step(2)
    a2.z.step(2)
    b1.finish_z()
    b1.send_x()
    b2.finish_z()
    b2.send_x()
    pool_gather.wait(3)
    core_sems = s.core.send.at[0], s.core.recv.at[0]
    send(s.pool.buf, s.pool_other, *core_sems, other)
    a1.z.step(3)
    a2.z.step(3)
    pairs_3()
    b1.send_pair()
    a1.z.step(4)
    b2.send_pair()
    a2.z.step(4)
    arrived(s.pool_other, *core_sems, other)
    pairs_1()
    a1.send_pair()
    a2.send_pair()
    pairs_2()
    pairs_4()
    for group in (b1, b2, a1, a2):
        group.result()
    for copy in sent:
        copy.wait_send()
    text_gather.drain(3)
    pool_gather.drain(4)

    def drain_tiles(t, carry):
        for k in range(3):
            tile_copy(k, t).wait_send()
        return carry

    lax.fori_loop(0, 2 * TILES, drain_tiles, 0)


def hand_on(*refs):
    for k in range(4):
        refs[4 + k][...] = refs[k][...]


def shards(images, ln_gain, w_in, b_in, w_out, texts, w_text, b_text, logit_scale, logit_bias):
    vmem = pl.BlockSpec(memory_space=pltpu.VMEM)
    smem = pl.BlockSpec(memory_space=pltpu.SMEM)
    hbm = pl.BlockSpec(memory_space=pl.ANY)
    dma = pltpu.SemaphoreType.DMA
    V = pltpu.VMEM
    def with_sems(count, **buffers):
        return dict(send=dma(count), recv=dma(count), **buffers)

    def ring(kind, shape, steps, width):
        return with_sems(
            (sum(steps),),
            buf=V(shape + (width,), kind),
            right=V((steps[0],) + shape[1:] + (width,), kind),
            left=V((steps[1],) + shape[1:] + (width,), kind),
        )

    def pair(width):
        return with_sems((1,), buf=V((NH, 24, width), f32), right=V((24, width), f32))

    refs = dict(
        w_in=V((HID, D), b16),
        w_pad=V((PADDED, D), b16),
        before=V((PADDED, TILE), f32),
        act_lanes=V((2, PADDED, 128), f32),
        w_out=V((HID, D), b16),
        w_text=V((D, D), b16),
        gain_col=V((D, 128), f32),
        bias_col=V((D, 128), f32),
        row_pad=V((1, D), f32),
        full=V((2 * TILES, NM, OWN, TILE), b16),
        normed=V((2, D, TILES * TILE), b16),
        slopes=V((2, PADDED, TILES * TILE), b16),
        act_sum=V((2, 8, D), f32),
        image_sum=V((2, 8, D), f32),
        product=V((2, D, D), f32),
        parts=V((NM, 2, D), f32),
        pool_other=V((NX, NH, NZ, 4, D), b16),
        acts=V((BATCH, D), b16),
        text_rows=V((BATCH, D), b16),
        text_emb=V((BATCH, D), b16),
        text_unit=V((BATCH, D), f32),
        text_norm=V((BATCH, 128), f32),
        grad_act=V((2, D), f32),
        load_sem=dma((3,)),
        img=with_sems((3, 2 * TILES)),
        part=with_sems((3,)),
        core=with_sems((1,)),
        texts=with_sems((11,), buf=V((NX, NZ, NH, 2, D), f32)),
        pool=with_sems((12,), buf=V((NX, NH, NZ, 4, D), b16)),
    )
    def group_a(width, steps):
        stage = with_sems(
            (6,),
            buf=V((NX, OWN, width), b16),
            right=V((3, 144, width), b16),
            left=V((3, 144, width), b16),
        )
        return dict(
            stage=stage,
            sum=V((OWN + 8, width), f32),
            ring=ring(b16, (NZ, PAIR), steps, width),
            pair=pair(width),
        )

    def group_b(width, steps):
        return dict(
            pack=V((144, width), f32),
            stage=ring(b16, (NZ, 144), steps, width),
            sum=V((152, width), f32),
            ring=with_sems(
                (NX - 1,), buf=V((NX, PAIR, width), b16), right=V((NX - 1, PAIR, width), b16)
            ),
            pair=pair(width),
        )

    refs.update(
        a=[group_a(GROUPS_A[0][1], (3, 4)), group_a(GROUPS_A[1][1], (4, 3))],
        b=[group_b(GROUPS_B[0][1], (4, 3)), group_b(GROUPS_B[1][1], (3, 4))],
    )
    out_shape = [
        jax.ShapeDtypeStruct((ROWS, HID), f32),
        jax.ShapeDtypeStruct((ROWS, HID), f32),
        jax.ShapeDtypeStruct((ROWS, D), f32),
        jax.ShapeDtypeStruct((2, D), b16),
    ]
    results = pl.pallas_call(
        kernel,
        out_shape=out_shape,
        in_specs=[vmem] * 5 + [smem] * 2 + [hbm] * 3,
        out_specs=[vmem] * 4,
        scratch_shapes=[refs],
        compiler_params=pltpu.CompilerParams(
            collective_id=0, has_side_effects=True, vmem_limit_bytes=58 << 20
        ),
    )(
        images.transpose(0, 2, 1),
        ln_gain,
        b_in,
        b_text,
        texts,
        logit_scale,
        logit_bias,
        w_in.T,
        w_out,
        w_text,
    )
    grad_in, grad_out, grad_text, grad_texts = pl.pallas_call(
        hand_on,
        out_shape=out_shape,
        in_specs=[vmem] * 4,
        out_specs=[vmem] * 4,
        compiler_params=pltpu.CompilerParams(vmem_limit_bytes=58 << 20),
    )(*results)
    return grad_in, grad_out.T, grad_text, grad_texts


def solution(mesh):
    placed = (
        P("dp", None, "mp"),
        P(),
        P(None, "mp"),
        P("mp"),
        P("mp", None),
        P("dp", None),
        P(),
        P(),
        P(),
        P(),
    )
    return jax.shard_map(
        shards,
        mesh=mesh,
        in_specs=placed,
        out_specs=(P("dp", "mp"), P("mp", "dp"), P("dp", None), P("dp", None)),
        check_vma=False,
    )
```

```python
import jax
import jax.numpy as jnp
from jax import lax
from jax.experimental import pallas as pl
from jax.experimental.pallas import tpu as pltpu
from jax.sharding import PartitionSpec as P

sqrt_two_pi = 0.7978845608028654
cubic_term = 0.044715
epsilon = 1e-06

NX, NH, NZ, NM = 4, 2, 8, 4
D = 1152
HID = 1076
PATCH = 729
OWN = D // 4
TILE = 256
TILES = 3
ROWS = 18
PAIR = 48
GROUPS_A = ((0, 384), (384, 256))
GROUPS_B = ((640, 256), (896, 256))
AHEAD = 3
PADDED = 1088
BATCH = 128
HALF = 64

f32 = jnp.float32
b16 = jnp.bfloat16
MESH = pl.DeviceIdType.MESH


def mm(a, b):
    return lax.dot_general(a, b, (((1,), (0,)), ((), ())), preferred_element_type=f32)


def mm_nt(a, b):
    return lax.dot_general(a, b, (((1,), (1,)), ((), ())), preferred_element_type=f32)


def mm_tn(a, b):
    return lax.dot_general(a, b, (((0,), (0,)), ((), ())), preferred_element_type=f32)


class Refs:
    def __init__(self, values):
        for name, value in values.items():
            if isinstance(value, (tuple, list)):
                value = [Refs(part) for part in value]
            setattr(self, name, Refs(value) if isinstance(value, dict) else value)


def iota(shape, axis):
    return lax.broadcasted_iota(jnp.int32, shape, axis)


def three_parts(values):
    high = values.astype(b16)
    rest = values - high.astype(f32)
    middle = rest.astype(b16)
    low = (rest - middle.astype(f32)).astype(b16)
    return high, middle, low


def gelu_and_slope(values):
    squared = values * values
    tanh_part = jnp.tanh(values * (sqrt_two_pi + (sqrt_two_pi * cubic_term) * squared))
    half = 0.5 + 0.5 * tanh_part
    bend = (1.0 - tanh_part * tanh_part) * (
        0.5 * sqrt_two_pi + (1.5 * sqrt_two_pi * cubic_term) * squared
    )
    return values * half, half + values * bend


def kernel(
    images_hbm,
    gain_hbm,
    bias_hbm,
    shift_hbm,
    texts_hbm,
    scale_ref,
    shift_ref,
    w_in_hbm,
    w_out_hbm,
    w_text_hbm,
    out_in,
    out_out,
    out_text,
    out_texts,
    s,
):
    s = Refs(s)
    w_in, w_tail, w_out, w_text = s.w_in, s.w_tail, s.w_out, s.w_text
    images, texts = s.images, s.own_texts
    gain_row, bias_in, bias_text = s.gain_row, s.bias_in, s.bias_text
    full, normed, slopes, product = s.full, s.normed, s.slopes, s.product
    act_sum, image_sum, grad_act, parts = s.act_sum, s.image_sum, s.grad_act, s.parts

    dp = lax.axis_index("dp")
    mp = lax.axis_index("mp")
    x = dp // (NH * NZ)
    yh = (dp // NZ) % NH
    z = dp % NZ
    slot = (x * NZ + z) * NH + yh
    yl = mp // 2
    core = mp % 2
    mp_chip = (1 - yl) * 2 + core
    mp_core = yl * 2 + (1 - core)
    mp_far = (1 - yl) * 2 + (1 - core)
    chip, other, far = (dp, mp_chip), (dp, mp_core), (dp, mp_far)

    def at_z(d):
        return ((x * NH + yh) * NZ + (z + d) % NZ, mp)

    def at_x(d):
        return ((((x + d) % NX) * NH + yh) * NZ + z, mp)

    def at_yh():
        return ((x * NH + (1 - yh)) * NZ + z, mp)

    def remote(src, dst, send_sem, recv_sem, device):
        return pltpu.make_async_remote_copy(
            src_ref=src,
            dst_ref=dst,
            send_sem=send_sem,
            recv_sem=recv_sem,
            device_id=device,
            device_id_type=MESH,
        )

    sent = []

    def send(src, dst, send_sem, recv_sem, device):
        copy = remote(src, dst, send_sem, recv_sem, device)
        copy.start()
        sent.append(copy)

    def arrived(dst, send_sem, recv_sem, device):
        remote(dst, dst, send_sem, recv_sem, device).wait_recv()

    sources = (w_in_hbm, w_out_hbm, w_text_hbm, images_hbm, texts_hbm, gain_hbm, bias_hbm, shift_hbm)
    targets = (w_in, w_out, w_text, images, texts, gain_row, bias_in, bias_text)
    loads = [
        pltpu.make_async_copy(source, target, s.load_sem.at[k])
        for k, (source, target) in enumerate(zip(sources, targets))
    ]
    for k in (3, 4, 5, 6, 0, 2, 7, 1):
        loads[k].start()

    barrier = pltpu.get_barrier_semaphore()
    partners = [chip, other, far, at_yh()]
    partners += [at_z(d) for d in range(1, NZ)] + [at_x(d) for d in range(1, NX)]
    for partner in partners:
        pl.semaphore_signal(barrier, inc=1, device_id=partner, device_id_type=MESH)

    loads[3].wait()
    for i in range(2):
        for j in range(TILES):
            begin = j * TILE
            width = min(TILE, PATCH - begin)
            if width < TILE:
                full[i * TILES + j, mp] = jnp.zeros((OWN, TILE), b16)
            full[i * TILES + j, mp, :, 0:width] = images[i, :, begin : begin + width]
    loads[4].wait()
    s.texts.buf[x, z, yh] = texts[...].astype(f32)

    pl.semaphore_wait(barrier, len(partners))

    class Gather:
        def __init__(self, refs):
            self.buf, self.send_sem, self.recv_sem = refs.buf, refs.send, refs.recv

        def start(self, stage):
            for n, own, _, device in self.copies(stage):
                remote(own, own, self.send_sem.at[n], self.recv_sem.at[n], device).start()

        def wait(self, stage):
            for n, _, landed, device in self.copies(stage):
                arrived(landed, self.send_sem.at[n], self.recv_sem.at[n], device)

        def drain(self, stages):
            for stage in range(stages):
                for n, own, _, device in self.copies(stage):
                    remote(own, own, self.send_sem.at[n], self.recv_sem.at[n], device).wait_send()

    class TextGather(Gather):
        def copies(self, stage):
            at = self.buf.at
            if stage == 0:
                return [(0, at[x, z, yh], at[x, z, 1 - yh], at_yh())]
            if stage == 1:
                return [(d, at[x, z], at[x, (z + NZ - d) % NZ], at_z(d)) for d in range(1, NZ)]
            return [(7 + d, at[x], at[(x + NX - d) % NX], at_x(d)) for d in range(1, NX)]

    class PoolGather(Gather):
        def copies(self, stage):
            at = self.buf.at
            if stage == 0:
                return [
                    (d, at[x, yh, z], at[x, yh, (z + NZ - d) % NZ], at_z(d)) for d in range(1, NZ)
                ]
            if stage == 1:
                return [(0, at[x, yh], at[x, 1 - yh], at_yh())]
            before, after = (x + NX - 1) % NX, (x + 1) % NX
            if stage == 2:
                return [(8, at[x], at[before], at_x(1)), (9, at[x], at[after], at_x(NX - 1))]
            far = (x + 2) % NX
            return [
                (10, at[before, 0], at[far, 0], at_x(1)),
                (11, at[after, 1], at[far, 1], at_x(NX - 1)),
            ]

    def tile_copy(k, t):
        source = full.at[t, mp_chip if k == 2 else mp]
        return remote(source, source, s.img.send.at[k, t], s.img.recv.at[k, t], chip if k == 0 else other)

    text_gather = TextGather(s.texts)
    for t in range(AHEAD):
        tile_copy(0, t).start()
        tile_copy(1, t).start()
    text_gather.start(0)

    product[...] = jnp.zeros_like(product)
    act_sum[...] = jnp.zeros_like(act_sum)
    image_sum[...] = jnp.zeros_like(image_sum)
    grad_act[...] = jnp.zeros_like(grad_act)
    loads[5].wait()
    loads[6].wait()
    diagonal = iota((128, 128), 0) == iota((128, 128), 1)
    row_pad = s.row_pad
    for row, column, width in ((gain_row, s.gain_col, D), (bias_in, s.bias_col, HID)):
        row_pad[...] = jnp.zeros_like(row_pad)
        row_pad[:, 0:width] = row[...].reshape(1, width)
        for k in range(D // 128):
            span = slice(128 * k, 128 * k + 128)
            picked = jnp.sum(jnp.where(diagonal, row_pad[:, span], 0.0), axis=1, keepdims=True)
            column[span, :] = jnp.broadcast_to(picked, (128, 128))
    whole = HID // TILE * TILE
    chunks = [(begin, TILE) for begin in range(0, whole, TILE)] + [(whole, PADDED - whole)]
    loads[0].wait()
    tail = (iota((PADDED - whole, HID - whole), 0) == iota((PADDED - whole, HID - whole), 1)).astype(
        b16
    )
    w_tail[...] = mm(tail, w_in[whole:HID, :]).astype(b16)

    def add_product(t):
        i = t // TILES
        for begin, width in chunks:
            span = slice(begin, begin + width)
            product[i, :, span] += mm_nt(normed[t], slopes[t, span, :])

    def work_on(t):
        i = t // TILES
        j = t % TILES
        for h in range(TILE // 128):
            lanes = slice(128 * h, 128 * h + 128)
            total = jnp.zeros((1, 128), f32)
            for m in range(NM):
                total += jnp.sum(full[t, m, :, lanes].astype(f32), axis=0, keepdims=True)
            mean = total * (1.0 / D)
            total = jnp.zeros((1, 128), f32)
            for m in range(NM):
                centered = full[t, m, :, lanes].astype(f32) - mean
                total += jnp.sum(centered * centered, axis=0, keepdims=True)
            factor = lax.rsqrt(total * (1.0 / D) + epsilon)
            for m in range(NM):
                rows = slice(OWN * m, OWN * m + OWN)
                centered = full[t, m, :, lanes].astype(f32) - mean
                normed[t, rows, lanes] = (centered * factor * s.gain_col[rows, :]).astype(b16)
        valid = (iota((8, TILE), 1) + j * TILE < PATCH).astype(b16)
        image_sum[i] += mm_nt(valid, full[t].reshape(D, TILE))
        for begin, width in chunks:
            span = slice(begin, begin + width)
            bias = s.bias_col[span, :]
            weight = w_in[span, :] if begin < whole else w_tail[...]
            before = mm(weight, normed[t]) + jnp.concatenate([bias, bias], axis=1)
            act, slope = gelu_and_slope(before)
            slopes[t, span, :] = slope.astype(b16)
            act_sum[i, :, span] += mm_nt(valid, act.astype(b16))

    def project_texts():
        loads[2].wait()
        loads[7].wait()
        for r in range(2):
            s.text_rows[HALF * r : HALF * r + HALF, :] = (
                s.texts.buf[:, :, :, r, :].reshape(HALF, D).astype(b16)
            )
        projected = mm(s.text_rows[...], w_text[...]) + bias_text[...].reshape(1, D)
        norm = jnp.sqrt(jnp.sum(projected * projected, axis=1, keepdims=True) + epsilon)
        unit = projected / norm
        s.text_norm[...] = jnp.broadcast_to(norm, (BATCH, 128))
        s.text_unit[...] = unit
        s.text_emb[...] = unit.astype(b16)

    def pass_on(t):
        arrived(full.at[t, mp_chip], s.img.send.at[0, t], s.img.recv.at[0, t], chip)
        tile_copy(2, t).start()

    def tile_step(t, carry):
        @pl.when(t < 2 * TILES - 1)
        def _():
            pass_on(t + 1)

        @pl.when(t < 2 * TILES - AHEAD)
        def _():
            tile_copy(0, t + AHEAD).start()
            tile_copy(1, t + AHEAD).start()

        @pl.when(t == 0)
        def _():
            text_gather.wait(0)
            text_gather.start(1)

        @pl.when(t == 2)
        def _():
            text_gather.wait(1)
            text_gather.start(2)

        @pl.when(t == 4)
        def _():
            text_gather.wait(2)
            project_texts()

        @pl.when(t > 0)
        def _():
            add_product(t - 1)

        arrived(full.at[t, mp_core], s.img.send.at[1, t], s.img.recv.at[1, t], other)
        arrived(full.at[t, mp_far], s.img.send.at[2, t], s.img.recv.at[2, t], other)
        work_on(t)
        return carry

    pass_on(0)
    lax.fori_loop(0, 2 * TILES, tile_step, 0)

    loads[1].wait()
    row = iota((8, HID), 0)
    split = three_parts(act_sum[0, :, 0:HID]) + three_parts(act_sum[1, :, 0:HID])
    stacked = jnp.zeros((8, HID), f32)
    for k in range(6):
        stacked = jnp.where(row == k, split[k].astype(f32), stacked)
    shares = mm(stacked.astype(b16), w_out[...])
    row = iota((8, D), 0)
    share_0 = jnp.sum(jnp.where(row < 3, shares, 0.0), axis=0, keepdims=True)
    share_1 = jnp.sum(jnp.where((row >= 3) & (row < 6), shares, 0.0), axis=0, keepdims=True)
    first = iota((2, D), 0) == 0
    parts[mp] = jnp.where(first, share_0, share_1)
    group = (chip, other, far)
    for k, partner in enumerate(group):
        own = parts.at[mp]
        send(own, own, s.part.send.at[k], s.part.recv.at[k], partner)
    add_product(2 * TILES - 1)
    for k, source in enumerate((mp_chip, mp_core, mp_far)):
        arrived(parts.at[source], s.part.send.at[k], s.part.recv.at[k], group[k])
    block = parts[0] + parts[1] + parts[2] + parts[3]
    pooled = (jnp.where(first, image_sum[0, 0:2, :], image_sum[1, 0:2, :]) + block) * (1.0 / PATCH)
    pool_gather = PoolGather(s.pool)
    mine = jnp.where(core == 0, pooled[0:1, :], pooled[1:2, :])
    pooled_high = mine.astype(b16)
    pooled_rest = (mine - pooled_high.astype(f32)).astype(b16)
    rows = (pooled_high.astype(f32), pooled_rest.astype(f32), act_sum[0, 0:1, :], act_sum[1, 0:1, :])
    order = iota((4, D), 0)
    packed = jnp.broadcast_to(rows[0], (4, D))
    for k in range(1, 4):
        packed = jnp.where(order == k, rows[k], packed)
    s.pool.buf[x, yh, z] = packed.astype(b16)
    pool_gather.start(0)

    scale = scale_ref[0]
    shift = shift_ref[0]

    def block_gradient(values):
        norm = jnp.sqrt(jnp.sum(values * values, axis=1, keepdims=True) + epsilon)
        unit = values / norm
        emb = unit.astype(b16)
        logits = scale * mm_nt(emb, s.text_emb[...]) + shift
        if values.shape[0] == 2:
            matches = iota((2, BATCH), 1) == iota((2, BATCH), 0) * HALF + slot
        else:
            at = iota((BATCH, BATCH), 0)
            matches = (at & 112) + ((at & 7) << 1) + ((at >> 3) & 1) == iota((BATCH, BATCH), 1)
        signs = jnp.where(matches, 1.0, -1.0)
        coef = -signs * jax.nn.sigmoid(-signs * logits)
        weights = (scale * coef).astype(b16)
        grad_emb = mm(weights, s.text_emb[...])
        along = jnp.sum(unit * grad_emb, axis=1, keepdims=True)
        grad_pooled = (grad_emb - unit * along) / norm
        return (grad_pooled * (1.0 / PATCH)).astype(b16), weights, emb

    own_block, _, _ = block_gradient(pooled)
    grad_act[:, 0:HID] = mm_nt(own_block, w_out[...])
    pool_gather.wait(0)
    pool_gather.start(1)

    near_z = (at_z(1), at_z(NZ - 1))
    near_x = (at_x(1), at_x(NX - 1))

    def add_into(target, index, begin, count, received):
        for r in range(0, count, 48):
            there = slice(begin + r, begin + r + 48)
            target[index, there, :] = (
                target[index, there, :].astype(f32) + received[r : r + 48, :].astype(f32)
            ).astype(b16)

    class Ring:
        def __init__(self, refs, place, size, near, steps):
            self.buf = refs.buf
            self.recv = refs.right, refs.left
            self.sems = refs.send, refs.recv
            self.place, self.size, self.near, self.steps = place, size, near, steps

        def wait(self, way, k):
            n = way * self.steps[0] + k - 1
            there = self.recv[way].at[k - 1]
            arrived(there, self.sems[0].at[n], self.sems[1].at[n], self.near[way])
            return there

        def step(self, k):
            for way in range(2):
                if k > self.steps[way]:
                    continue
                away = self.steps[way] + 1 - k
                chunk = (self.place + (self.size - away if way else away)) % self.size
                if k > 1:
                    add_into(self.buf, chunk, 0, self.buf.shape[1], self.wait(way, k - 1))
                n = way * self.steps[0] + k - 1
                send(
                    self.buf.at[chunk],
                    self.recv[way].at[k - 1],
                    self.sems[0].at[n],
                    self.sems[1].at[n],
                    self.near[way],
                )

        def finish(self):
            for way in range(2):
                self.wait(way, self.steps[way])

        def total(self, rows):
            value = self.buf[self.place, rows, :].astype(f32)
            for way in range(2):
                value += self.recv[way][self.steps[way] - 1, rows, :].astype(f32)
            return value

    class Group:
        def __init__(self, refs, begin, width):
            self.refs, self.begin, self.width = refs, begin, width
            self.span = slice(begin, begin + width)

        def send_pair(self):
            value = self.last_total()
            for h in range(NH):
                self.refs.pair.buf[h] = value[24 * h : 24 * h + 24, :]
            sems = self.refs.pair.send.at[0], self.refs.pair.recv.at[0]
            send(self.refs.pair.buf.at[1 - yh], self.refs.pair.right, *sems, at_yh())

        def result(self):
            sems = self.refs.pair.send.at[0], self.refs.pair.recv.at[0]
            arrived(self.refs.pair.right, *sems, at_yh())
            width = min(self.width, HID - self.begin)
            value = self.refs.pair.buf[yh] + self.refs.pair.right[...]
            out_in[:, self.begin : self.begin + width] = value[0:ROWS, 0:width]

    class GroupA(Group):
        def __init__(self, refs, begin, width, steps):
            super().__init__(refs, begin, width)
            self.z = Ring(refs.ring, z, NZ, near_z, steps)
            self.q1, self.q2, self.q3 = (x + 1) % NX, (x + 2) % NX, (x + 3) % NX

        def combine(self, q):
            for r in range(OWN // 48):
                rows = pl.ds(pl.multiple_of(q * OWN + 48 * r, 16), 48)
                self.refs.stage.buf[q, 48 * r : 48 * r + 48, :] = (
                    product[0, rows, self.span] * grad_act[0:1, self.span]
                    + product[1, rows, self.span] * grad_act[1:2, self.span]
                ).astype(b16)

        def pieces(self, way, k):
            n = way * 3 + k
            return (
                (self.refs.stage.left if way else self.refs.stage.right).at[k],
                self.refs.stage.send.at[n],
                self.refs.stage.recv.at[n],
                near_x[way],
            )

        def send_half(self, q, half, way, k):
            send(self.refs.stage.buf.at[q, pl.ds(144 * half, 144)], *self.pieces(way, k))

        def wait_half(self, way, k):
            arrived(*self.pieces(way, k))

        def first(self):
            self.combine(self.q2)
            self.send_half(self.q2, 0, 0, 0)
            self.send_half(self.q2, 1, 1, 0)

        def second(self):
            self.combine(self.q1)
            self.send_half(self.q1, 1, 0, 1)
            self.combine(self.q3)
            self.send_half(self.q3, 0, 1, 1)

        def third(self):
            self.wait_half(0, 0)
            add_into(self.refs.stage.buf, self.q1, 0, 144, self.refs.stage.right.at[0])
            self.send_half(self.q1, 0, 0, 2)
            self.wait_half(1, 0)
            add_into(self.refs.stage.buf, self.q3, 144, 144, self.refs.stage.left.at[0])
            self.send_half(self.q3, 1, 1, 2)

        def finish_x(self):
            total = self.refs.sum
            for k in range(1, 3):
                self.wait_half(0, k)
                self.wait_half(1, k)
            for half in range(2):
                for r in range(0, 144, 48):
                    there = slice(144 * half + r, 144 * half + r + 48)
                    here = slice(r, r + 48)
                    total[there, :] = (
                        self.refs.stage.buf[x, there, :].astype(f32)
                        + self.refs.stage.right[2 - half, here, :].astype(f32)
                        + self.refs.stage.left[1 + half, here, :].astype(f32)
                    )
            total[OWN : OWN + 8, :] = jnp.zeros((8, self.width), f32)
            for k in range(NZ):
                both = [
                    total[h * (NZ * ROWS) + k * ROWS : h * (NZ * ROWS) + k * ROWS + 24, :]
                    for h in range(NH)
                ]
                self.refs.ring.buf[k] = jnp.concatenate(both, axis=0).astype(b16)

        def last_total(self):
            self.z.finish()
            return self.z.total(slice(0, PAIR))

    class GroupB(Group):
        def __init__(self, refs, begin, width, steps):
            super().__init__(refs, begin, width)
            self.z = Ring(refs.stage, z, NZ, near_z, steps)

        def pack(self):
            pack = self.refs.pack
            weight_0, weight_1 = grad_act[0:1, self.span], grad_act[1:2, self.span]
            for k in range(NZ):
                for g in range(NX * NH):
                    begin = g * (NZ * ROWS) + k * ROWS
                    source = slice(begin, begin + ROWS)
                    pack[g * ROWS : g * ROWS + ROWS, :] = (
                        product[0, source, self.span] * weight_0
                        + product[1, source, self.span] * weight_1
                    )
                self.refs.stage.buf[k] = pack[...].astype(b16)

        def finish_z(self):
            self.z.finish()
            total = self.refs.sum
            for r in range(0, 144, 48):
                total[r : r + 48, :] = self.z.total(slice(r, r + 48))
            total[144:152, :] = jnp.zeros((8, self.width), f32)
            for k in range(NX):
                both = [
                    total[(k * NH + h) * ROWS : (k * NH + h) * ROWS + 24, :] for h in range(NH)
                ]
                self.refs.ring.buf[k] = jnp.concatenate(both, axis=0).astype(b16)

        def send_x(self):
            refs = self.refs.ring
            for d in range(1, NX):
                source, sems = refs.buf.at[(x + d) % NX], (refs.send.at[d - 1], refs.recv.at[d - 1])
                send(source, refs.right.at[d - 1], *sems, at_x(d))

        def last_total(self):
            refs = self.refs.ring
            value = refs.buf[x].astype(f32)
            for d in range(1, NX):
                arrived(refs.right.at[d - 1], refs.send.at[d - 1], refs.recv.at[d - 1], at_x(d))
                value += refs.right[d - 1].astype(f32)
            return value

    a1 = GroupA(s.a[0], *GROUPS_A[0], (3, 4))
    a2 = GroupA(s.a[1], *GROUPS_A[1], (4, 3))
    b1 = GroupB(s.b[0], *GROUPS_B[0], (4, 3))
    b2 = GroupB(s.b[1], *GROUPS_B[1], (3, 4))

    pairs = Refs({})

    def pairs_1():
        halves = []
        for buf in (s.pool.buf, s.pool_other):
            both = [buf[:, :, :, r, :].reshape(HALF, D).astype(f32) for r in range(2)]
            halves.append(both[0] + both[1])
        lower = jnp.where(core == 0, halves[0], halves[1])
        upper = jnp.where(core == 0, halves[1], halves[0])
        all_pooled = jnp.concatenate([lower, upper], axis=0)
        block, weights, emb = block_gradient(all_pooled)
        pick = (iota((D, ROWS), 0) == iota((D, ROWS), 1) + dp * ROWS).astype(b16)
        pairs.columns = mm(block, pick).astype(b16)
        pairs.features = mm(s.text_rows[...], pick).astype(b16)
        pairs.weights, pairs.emb = weights, emb

    def pairs_2():
        grad_text = mm_tn(pairs.weights, pairs.emb)
        unit = s.text_unit[...]
        along = jnp.sum(unit * grad_text, axis=1, keepdims=True)
        pairs.proj = ((grad_text - unit * along) / s.text_norm[:, 0:1]).astype(b16)

    def pairs_3():
        for r in range(2):
            s.acts[HALF * r : HALF * r + HALF, :] = s.pool.buf[:, :, :, 2 + r, :].reshape(HALF, D)

    def pairs_4():
        out_out[...] = mm_tn(pairs.columns, s.acts[:, 0:HID])
        out_text[...] = mm_tn(pairs.features, pairs.proj)
        chosen = (iota((2, BATCH), 1) == iota((2, BATCH), 0) * HALF + slot).astype(b16)
        own_text = mm(chosen, pairs.proj).astype(b16)
        out_texts[...] = mm_nt(own_text, w_text[...]).astype(b16)

    a1.first()
    a2.first()
    b1.pack()
    b1.z.step(1)
    a1.second()
    b2.pack()
    b2.z.step(1)
    a2.second()
    a1.third()
    b1.z.step(2)
    a2.third()
    b2.z.step(2)
    pool_gather.wait(1)
    pool_gather.start(2)
    a1.combine(x)
    a2.combine(x)
    b1.z.step(3)
    b2.z.step(3)
    a1.finish_x()
    a1.z.step(1)
    b1.z.step(4)
    a2.finish_x()
    a2.z.step(1)
    pool_gather.wait(2)
    pool_gather.start(3)
    b2.z.step(4)
    a1.z.step(2)
    a2.z.step(2)
    b1.finish_z()
    b1.send_x()
    b2.finish_z()
    b2.send_x()
    pool_gather.wait(3)
    core_sems = s.core.send.at[0], s.core.recv.at[0]
    send(s.pool.buf, s.pool_other, *core_sems, other)
    a1.z.step(3)
    a2.z.step(3)
    pairs_3()
    b1.send_pair()
    a1.z.step(4)
    b2.send_pair()
    a2.z.step(4)
    arrived(s.pool_other, *core_sems, other)
    pairs_1()
    a1.send_pair()
    a2.send_pair()
    pairs_2()
    pairs_4()
    for group in (b1, b2, a1, a2):
        group.result()
    for copy in sent:
        copy.wait_send()
    text_gather.drain(3)
    pool_gather.drain(4)

    def drain_tiles(t, carry):
        for k in range(3):
            tile_copy(k, t).wait_send()
        return carry

    lax.fori_loop(0, 2 * TILES, drain_tiles, 0)


def hand_on(*refs):
    for k in range(4):
        refs[4 + k][...] = refs[k][...]


def shards(images, ln_gain, w_in, b_in, w_out, texts, w_text, b_text, logit_scale, logit_bias):
    vmem = pl.BlockSpec(memory_space=pltpu.VMEM)
    smem = pl.BlockSpec(memory_space=pltpu.SMEM)
    hbm = pl.BlockSpec(memory_space=pl.ANY)
    dma = pltpu.SemaphoreType.DMA
    V = pltpu.VMEM
    def with_sems(count, **buffers):
        return dict(send=dma(count), recv=dma(count), **buffers)

    def ring(kind, shape, steps, width):
        return with_sems(
            (sum(steps),),
            buf=V(shape + (width,), kind),
            right=V((steps[0],) + shape[1:] + (width,), kind),
            left=V((steps[1],) + shape[1:] + (width,), kind),
        )

    def pair(width):
        return with_sems((1,), buf=V((NH, 24, width), f32), right=V((24, width), f32))

    refs = dict(
        w_in=V((HID, D), b16),
        w_tail=V((PADDED - HID // TILE * TILE, D), b16),
        w_out=V((HID, D), b16),
        w_text=V((D, D), b16),
        gain_col=V((D, 128), f32),
        bias_col=V((D, 128), f32),
        row_pad=V((1, D), f32),
        full=V((2 * TILES, NM, OWN, TILE), b16),
        normed=V((2 * TILES, D, TILE), b16),
        slopes=V((2 * TILES, PADDED, TILE), b16),
        act_sum=V((2, 8, D), f32),
        image_sum=V((2, 8, D), f32),
        product=V((2, D, D), f32),
        parts=V((NM, 2, D), f32),
        pool_other=V((NX, NH, NZ, 4, D), b16),
        acts=V((BATCH, D), b16),
        text_rows=V((BATCH, D), b16),
        text_emb=V((BATCH, D), b16),
        text_unit=V((BATCH, D), f32),
        text_norm=V((BATCH, 128), f32),
        grad_act=V((2, D), f32),
        load_sem=dma((8,)),
        images=V((2, OWN, PATCH), b16),
        own_texts=V((2, D), b16),
        gain_row=V((D,), f32),
        bias_in=V((HID,), f32),
        bias_text=V((D,), f32),
        img=with_sems((3, 2 * TILES)),
        part=with_sems((3,)),
        core=with_sems((1,)),
        texts=with_sems((11,), buf=V((NX, NZ, NH, 2, D), f32)),
        pool=with_sems((12,), buf=V((NX, NH, NZ, 4, D), b16)),
    )
    def group_a(width, steps):
        stage = with_sems(
            (6,),
            buf=V((NX, OWN, width), b16),
            right=V((3, 144, width), b16),
            left=V((3, 144, width), b16),
        )
        return dict(
            stage=stage,
            sum=V((OWN + 8, width), f32),
            ring=ring(b16, (NZ, PAIR), steps, width),
            pair=pair(width),
        )

    def group_b(width, steps):
        return dict(
            pack=V((144, width), f32),
            stage=ring(b16, (NZ, 144), steps, width),
            sum=V((152, width), f32),
            ring=with_sems(
                (NX - 1,), buf=V((NX, PAIR, width), b16), right=V((NX - 1, PAIR, width), b16)
            ),
            pair=pair(width),
        )

    refs.update(
        a=[group_a(GROUPS_A[0][1], (3, 4)), group_a(GROUPS_A[1][1], (4, 3))],
        b=[group_b(GROUPS_B[0][1], (4, 3)), group_b(GROUPS_B[1][1], (3, 4))],
    )
    out_shape = [
        jax.ShapeDtypeStruct((ROWS, HID), f32),
        jax.ShapeDtypeStruct((ROWS, HID), f32),
        jax.ShapeDtypeStruct((ROWS, D), f32),
        jax.ShapeDtypeStruct((2, D), b16),
    ]
    results = pl.pallas_call(
        kernel,
        out_shape=out_shape,
        in_specs=[hbm] * 5 + [smem] * 2 + [hbm] * 3,
        out_specs=[vmem] * 4,
        scratch_shapes=[refs],
        compiler_params=pltpu.CompilerParams(
            collective_id=0, has_side_effects=True, vmem_limit_bytes=58 << 20
        ),
    )(
        images.transpose(0, 2, 1),
        ln_gain,
        b_in,
        b_text,
        texts,
        logit_scale,
        logit_bias,
        w_in.T,
        w_out,
        w_text,
    )
    grad_in, grad_out, grad_text, grad_texts = pl.pallas_call(
        hand_on,
        out_shape=out_shape,
        in_specs=[vmem] * 4,
        out_specs=[vmem] * 4,
        compiler_params=pltpu.CompilerParams(vmem_limit_bytes=58 << 20),
    )(*results)
    return grad_in, grad_out.T, grad_text, grad_texts


def solution(mesh):
    placed = (
        P("dp", None, "mp"),
        P(),
        P(None, "mp"),
        P("mp"),
        P("mp", None),
        P("dp", None),
        P(),
        P(),
        P(),
        P(),
    )
    return jax.shard_map(
        shards,
        mesh=mesh,
        in_specs=placed,
        out_specs=(P("dp", "mp"), P("mp", "dp"), P("dp", None), P("dp", None)),
        check_vma=False,
    )
```

```python
import jax
import jax.numpy as jnp
from jax import lax
from jax.experimental import pallas as pl
from jax.experimental.pallas import tpu as pltpu
from jax.sharding import PartitionSpec as P

sqrt_two_pi = 0.7978845608028654
cubic_term = 0.044715
epsilon = 1e-06

NX, NH, NZ, NM = 4, 2, 8, 4
D = 1152
HID = 1076
PATCH = 729
OWN = D // 4
TILE = 256
TILES = 3
ROWS = 18
PAIR = 48
GROUPS_A = ((0, 384), (384, 256))
GROUPS_B = ((640, 256), (896, 256))
PADDED = 1088
BATCH = 128
HALF = 64

f32 = jnp.float32
b16 = jnp.bfloat16
MESH = pl.DeviceIdType.MESH


def mm(a, b):
    return lax.dot_general(a, b, (((1,), (0,)), ((), ())), preferred_element_type=f32)


def mm_nt(a, b):
    return lax.dot_general(a, b, (((1,), (1,)), ((), ())), preferred_element_type=f32)


def mm_tn(a, b):
    return lax.dot_general(a, b, (((0,), (0,)), ((), ())), preferred_element_type=f32)


class Refs:
    def __init__(self, values):
        for name, value in values.items():
            if isinstance(value, (tuple, list)):
                value = [Refs(part) for part in value]
            setattr(self, name, Refs(value) if isinstance(value, dict) else value)


def iota(shape, axis):
    return lax.broadcasted_iota(jnp.int32, shape, axis)


def three_parts(values):
    high = values.astype(b16)
    rest = values - high.astype(f32)
    middle = rest.astype(b16)
    low = (rest - middle.astype(f32)).astype(b16)
    return high, middle, low


def gelu_and_slope(values):
    squared = values * values
    tanh_part = jnp.tanh(values * (sqrt_two_pi + (sqrt_two_pi * cubic_term) * squared))
    half = 0.5 + 0.5 * tanh_part
    bend = (1.0 - tanh_part * tanh_part) * (
        0.5 * sqrt_two_pi + (1.5 * sqrt_two_pi * cubic_term) * squared
    )
    return values * half, half + values * bend


def kernel(
    images_hbm,
    gain_hbm,
    bias_hbm,
    shift_hbm,
    texts_hbm,
    scale_ref,
    shift_ref,
    w_in_hbm,
    w_out_hbm,
    w_text_hbm,
    out_in,
    out_out,
    out_text,
    out_texts,
    s,
):
    s = Refs(s)
    w_in, w_tail, w_out, w_text = s.w_in, s.w_tail, s.w_out, s.w_text
    images, texts = s.images, s.own_texts
    gain_row, bias_in, bias_text = s.gain_row, s.bias_in, s.bias_text
    full, normed, slopes, product = s.full, s.normed, s.slopes, s.product
    act_sum, image_sum, grad_act, parts = s.act_sum, s.image_sum, s.grad_act, s.parts

    dp = lax.axis_index("dp")
    mp = lax.axis_index("mp")
    x = dp // (NH * NZ)
    yh = (dp // NZ) % NH
    z = dp % NZ
    slot = (x * NZ + z) * NH + yh
    yl = mp // 2
    core = mp % 2
    mp_chip = (1 - yl) * 2 + core
    mp_core = yl * 2 + (1 - core)
    mp_far = (1 - yl) * 2 + (1 - core)
    chip, other, far = (dp, mp_chip), (dp, mp_core), (dp, mp_far)

    def at_z(d):
        return ((x * NH + yh) * NZ + (z + d) % NZ, mp)

    def at_x(d):
        return ((((x + d) % NX) * NH + yh) * NZ + z, mp)

    def at_yh():
        return ((x * NH + (1 - yh)) * NZ + z, mp)

    def remote(src, dst, send_sem, recv_sem, device):
        return pltpu.make_async_remote_copy(
            src_ref=src,
            dst_ref=dst,
            send_sem=send_sem,
            recv_sem=recv_sem,
            device_id=device,
            device_id_type=MESH,
        )

    sent = []

    def send(src, dst, send_sem, recv_sem, device):
        copy = remote(src, dst, send_sem, recv_sem, device)
        copy.start()
        sent.append(copy)

    def arrived(dst, send_sem, recv_sem, device):
        remote(dst, dst, send_sem, recv_sem, device).wait_recv()

    sources = (w_in_hbm, w_out_hbm, w_text_hbm, images_hbm, texts_hbm, gain_hbm, bias_hbm, shift_hbm)
    targets = (w_in, w_out, w_text, images, texts, gain_row, bias_in, bias_text)
    loads = [
        pltpu.make_async_copy(source, target, s.load_sem.at[k])
        for k, (source, target) in enumerate(zip(sources, targets))
    ]
    for k in (3, 4, 5, 6, 0):
        loads[k].start()

    barrier = pltpu.get_barrier_semaphore()
    partners = [chip, other, far, at_yh()]
    partners += [at_z(d) for d in range(1, NZ)] + [at_x(d) for d in range(1, NX)]
    for partner in partners:
        pl.semaphore_signal(barrier, inc=1, device_id=partner, device_id_type=MESH)

    loads[3].wait()
    for i in range(2):
        for j in range(TILES):
            begin = j * TILE
            width = min(TILE, PATCH - begin)
            if width < TILE:
                full[i * TILES + j, mp] = jnp.zeros((OWN, TILE), b16)
            full[i * TILES + j, mp, :, 0:width] = images[i, :, begin : begin + width]
    loads[4].wait()
    s.texts.buf[x, z, yh] = texts[...].astype(f32)

    pl.semaphore_wait(barrier, len(partners))

    class Gather:
        def __init__(self, refs):
            self.buf, self.send_sem, self.recv_sem = refs.buf, refs.send, refs.recv

        def start(self, stage):
            for n, own, _, device in self.copies(stage):
                remote(own, own, self.send_sem.at[n], self.recv_sem.at[n], device).start()

        def wait(self, stage):
            for n, _, landed, device in self.copies(stage):
                arrived(landed, self.send_sem.at[n], self.recv_sem.at[n], device)

        def drain(self, stages):
            for stage in range(stages):
                for n, own, _, device in self.copies(stage):
                    remote(own, own, self.send_sem.at[n], self.recv_sem.at[n], device).wait_send()

    class TextGather(Gather):
        def copies(self, stage):
            at = self.buf.at
            if stage == 0:
                return [(0, at[x, z, yh], at[x, z, 1 - yh], at_yh())]
            if stage == 1:
                return [(d, at[x, z], at[x, (z + NZ - d) % NZ], at_z(d)) for d in range(1, NZ)]
            return [(7 + d, at[x], at[(x + NX - d) % NX], at_x(d)) for d in range(1, NX)]

    class PoolGather(Gather):
        def copies(self, stage):
            at = self.buf.at
            if stage == 0:
                return [
                    (d, at[x, yh, z], at[x, yh, (z + NZ - d) % NZ], at_z(d)) for d in range(1, NZ)
                ]
            if stage == 1:
                return [(0, at[x, yh], at[x, 1 - yh], at_yh())]
            before, after = (x + NX - 1) % NX, (x + 1) % NX
            if stage == 2:
                return [(8, at[x], at[before], at_x(1)), (9, at[x], at[after], at_x(NX - 1))]
            far = (x + 2) % NX
            return [
                (10, at[before, 0], at[far, 0], at_x(1)),
                (11, at[after, 1], at[far, 1], at_x(NX - 1)),
            ]

    def tile_copy(k, t):
        source = full.at[t, mp_chip if k == 2 else mp]
        return remote(source, source, s.img.send.at[k, t], s.img.recv.at[k, t], chip if k == 0 else other)

    for k in (2, 7, 1):
        loads[k].start()
    text_gather = TextGather(s.texts)
    for t in range(2 * TILES):
        tile_copy(0, t).start()
        tile_copy(1, t).start()
    text_gather.start(0)

    product[...] = jnp.zeros_like(product)
    act_sum[...] = jnp.zeros_like(act_sum)
    image_sum[...] = jnp.zeros_like(image_sum)
    grad_act[...] = jnp.zeros_like(grad_act)
    loads[5].wait()
    loads[6].wait()
    diagonal = iota((128, 128), 0) == iota((128, 128), 1)
    row_pad = s.row_pad
    for row, column, width in ((gain_row, s.gain_col, D), (bias_in, s.bias_col, HID)):
        row_pad[...] = jnp.zeros_like(row_pad)
        row_pad[:, 0:width] = row[...].reshape(1, width)
        for k in range(D // 128):
            span = slice(128 * k, 128 * k + 128)
            picked = jnp.sum(jnp.where(diagonal, row_pad[:, span], 0.0), axis=1, keepdims=True)
            column[span, :] = jnp.broadcast_to(picked, (128, 128))
    whole = HID // TILE * TILE
    chunks = [(begin, TILE) for begin in range(0, whole, TILE)] + [(whole, PADDED - whole)]
    loads[0].wait()
    tail = (iota((PADDED - whole, HID - whole), 0) == iota((PADDED - whole, HID - whole), 1)).astype(
        b16
    )
    w_tail[...] = mm(tail, w_in[whole:HID, :]).astype(b16)

    def add_product(t):
        i = t // TILES
        for begin, width in chunks:
            span = slice(begin, begin + width)
            product[i, :, span] += mm_nt(normed[t], slopes[t, span, :])

    def work_on(t):
        i = t // TILES
        j = t % TILES
        for h in range(TILE // 128):
            lanes = slice(128 * h, 128 * h + 128)
            total = jnp.zeros((1, 128), f32)
            for m in range(NM):
                total += jnp.sum(full[t, m, :, lanes].astype(f32), axis=0, keepdims=True)
            mean = total * (1.0 / D)
            total = jnp.zeros((1, 128), f32)
            for m in range(NM):
                centered = full[t, m, :, lanes].astype(f32) - mean
                total += jnp.sum(centered * centered, axis=0, keepdims=True)
            factor = lax.rsqrt(total * (1.0 / D) + epsilon)
            for m in range(NM):
                rows = slice(OWN * m, OWN * m + OWN)
                centered = full[t, m, :, lanes].astype(f32) - mean
                normed[t, rows, lanes] = (centered * factor * s.gain_col[rows, :]).astype(b16)
        valid = (iota((8, TILE), 1) + j * TILE < PATCH).astype(b16)
        image_sum[i] += mm_nt(valid, full[t].reshape(D, TILE))
        for begin, width in chunks:
            span = slice(begin, begin + width)
            bias = s.bias_col[span, :]
            weight = w_in[span, :] if begin < whole else w_tail[...]
            before = mm(weight, normed[t]) + jnp.concatenate([bias, bias], axis=1)
            act, slope = gelu_and_slope(before)
            slopes[t, span, :] = slope.astype(b16)
            act_sum[i, :, span] += mm_nt(valid, act.astype(b16))

    def project_texts():
        loads[2].wait()
        loads[7].wait()
        for r in range(2):
            s.text_rows[HALF * r : HALF * r + HALF, :] = (
                s.texts.buf[:, :, :, r, :].reshape(HALF, D).astype(b16)
            )
        projected = mm(s.text_rows[...], w_text[...]) + bias_text[...].reshape(1, D)
        norm = jnp.sqrt(jnp.sum(projected * projected, axis=1, keepdims=True) + epsilon)
        unit = projected / norm
        s.text_norm[...] = jnp.broadcast_to(norm, (BATCH, 128))
        s.text_unit[...] = unit
        s.text_emb[...] = unit.astype(b16)

    def tile_step(t, carry):
        arrived(full.at[t, mp_chip], s.img.send.at[0, t], s.img.recv.at[0, t], chip)
        tile_copy(2, t).start()

        @pl.when(t > 0)
        def _():
            add_product(t - 1)

        @pl.when(t == 0)
        def _():
            text_gather.wait(0)
            text_gather.start(1)

        @pl.when(t == 2)
        def _():
            text_gather.wait(1)
            text_gather.start(2)

        @pl.when(t == 4)
        def _():
            text_gather.wait(2)
            project_texts()

        arrived(full.at[t, mp_core], s.img.send.at[1, t], s.img.recv.at[1, t], other)
        arrived(full.at[t, mp_far], s.img.send.at[2, t], s.img.recv.at[2, t], other)
        work_on(t)
        return carry

    lax.fori_loop(0, 2 * TILES, tile_step, 0)

    loads[1].wait()
    row = iota((8, HID), 0)
    split = three_parts(act_sum[0, :, 0:HID]) + three_parts(act_sum[1, :, 0:HID])
    stacked = jnp.zeros((8, HID), f32)
    for k in range(6):
        stacked = jnp.where(row == k, split[k].astype(f32), stacked)
    shares = mm(stacked.astype(b16), w_out[...])
    row = iota((8, D), 0)
    share_0 = jnp.sum(jnp.where(row < 3, shares, 0.0), axis=0, keepdims=True)
    share_1 = jnp.sum(jnp.where((row >= 3) & (row < 6), shares, 0.0), axis=0, keepdims=True)
    first = iota((2, D), 0) == 0
    parts[mp] = jnp.where(first, share_0, share_1)
    group = (chip, other, far)
    for k, partner in enumerate(group):
        own = parts.at[mp]
        send(own, own, s.part.send.at[k], s.part.recv.at[k], partner)
    add_product(2 * TILES - 1)
    for k, source in enumerate((mp_chip, mp_core, mp_far)):
        arrived(parts.at[source], s.part.send.at[k], s.part.recv.at[k], group[k])
    block = parts[0] + parts[1] + parts[2] + parts[3]
    pooled = (jnp.where(first, image_sum[0, 0:2, :], image_sum[1, 0:2, :]) + block) * (1.0 / PATCH)
    pool_gather = PoolGather(s.pool)
    mine = jnp.where(core == 0, pooled[0:1, :], pooled[1:2, :])
    pooled_high = mine.astype(b16)
    pooled_rest = (mine - pooled_high.astype(f32)).astype(b16)
    rows = (pooled_high.astype(f32), pooled_rest.astype(f32), act_sum[0, 0:1, :], act_sum[1, 0:1, :])
    order = iota((4, D), 0)
    packed = jnp.broadcast_to(rows[0], (4, D))
    for k in range(1, 4):
        packed = jnp.where(order == k, rows[k], packed)
    s.pool.buf[x, yh, z] = packed.astype(b16)
    pool_gather.start(0)

    scale = scale_ref[0]
    shift = shift_ref[0]

    def block_gradient(values):
        norm = jnp.sqrt(jnp.sum(values * values, axis=1, keepdims=True) + epsilon)
        unit = values / norm
        emb = unit.astype(b16)
        logits = scale * mm_nt(emb, s.text_emb[...]) + shift
        if values.shape[0] == 2:
            matches = iota((2, BATCH), 1) == iota((2, BATCH), 0) * HALF + slot
        else:
            at = iota((BATCH, BATCH), 0)
            matches = (at & 112) + ((at & 7) << 1) + ((at >> 3) & 1) == iota((BATCH, BATCH), 1)
        signs = jnp.where(matches, 1.0, -1.0)
        coef = -signs * jax.nn.sigmoid(-signs * logits)
        weights = (scale * coef).astype(b16)
        grad_emb = mm(weights, s.text_emb[...])
        along = jnp.sum(unit * grad_emb, axis=1, keepdims=True)
        grad_pooled = (grad_emb - unit * along) / norm
        return (grad_pooled * (1.0 / PATCH)).astype(b16), weights, emb

    own_block, _, _ = block_gradient(pooled)
    grad_act[:, 0:HID] = mm_nt(own_block, w_out[...])

    near_z = (at_z(1), at_z(NZ - 1))
    near_x = (at_x(1), at_x(NX - 1))

    def add_into(target, index, begin, count, received):
        for r in range(0, count, 48):
            there = slice(begin + r, begin + r + 48)
            target[index, there, :] = (
                target[index, there, :].astype(f32) + received[r : r + 48, :].astype(f32)
            ).astype(b16)

    class Ring:
        def __init__(self, refs, place, size, near, steps):
            self.buf = refs.buf
            self.recv = refs.right, refs.left
            self.sems = refs.send, refs.recv
            self.place, self.size, self.near, self.steps = place, size, near, steps

        def wait(self, way, k):
            n = way * self.steps[0] + k - 1
            there = self.recv[way].at[k - 1]
            arrived(there, self.sems[0].at[n], self.sems[1].at[n], self.near[way])
            return there

        def step(self, k):
            for way in range(2):
                if k > self.steps[way]:
                    continue
                away = self.steps[way] + 1 - k
                chunk = (self.place + (self.size - away if way else away)) % self.size
                if k > 1:
                    add_into(self.buf, chunk, 0, self.buf.shape[1], self.wait(way, k - 1))
                n = way * self.steps[0] + k - 1
                send(
                    self.buf.at[chunk],
                    self.recv[way].at[k - 1],
                    self.sems[0].at[n],
                    self.sems[1].at[n],
                    self.near[way],
                )

        def finish(self):
            for way in range(2):
                self.wait(way, self.steps[way])

        def total(self, rows):
            value = self.buf[self.place, rows, :].astype(f32)
            for way in range(2):
                value += self.recv[way][self.steps[way] - 1, rows, :].astype(f32)
            return value

    class Group:
        def __init__(self, refs, begin, width):
            self.refs, self.begin, self.width = refs, begin, width
            self.span = slice(begin, begin + width)

        def send_pair(self):
            value = self.last_total()
            for h in range(NH):
                self.refs.pair.buf[h] = value[24 * h : 24 * h + 24, :]
            sems = self.refs.pair.send.at[0], self.refs.pair.recv.at[0]
            send(self.refs.pair.buf.at[1 - yh], self.refs.pair.right, *sems, at_yh())

        def result(self):
            sems = self.refs.pair.send.at[0], self.refs.pair.recv.at[0]
            arrived(self.refs.pair.right, *sems, at_yh())
            width = min(self.width, HID - self.begin)
            value = self.refs.pair.buf[yh] + self.refs.pair.right[...]
            out_in[:, self.begin : self.begin + width] = value[0:ROWS, 0:width]

    class GroupA(Group):
        def __init__(self, refs, begin, width, steps):
            super().__init__(refs, begin, width)
            self.z = Ring(refs.ring, z, NZ, near_z, steps)
            self.q1, self.q2, self.q3 = (x + 1) % NX, (x + 2) % NX, (x + 3) % NX

        def combine(self, q):
            for r in range(OWN // 48):
                rows = pl.ds(pl.multiple_of(q * OWN + 48 * r, 16), 48)
                self.refs.stage.buf[q, 48 * r : 48 * r + 48, :] = (
                    product[0, rows, self.span] * grad_act[0:1, self.span]
                    + product[1, rows, self.span] * grad_act[1:2, self.span]
                ).astype(b16)

        def pieces(self, way, k):
            n = way * 3 + k
            return (
                (self.refs.stage.left if way else self.refs.stage.right).at[k],
                self.refs.stage.send.at[n],
                self.refs.stage.recv.at[n],
                near_x[way],
            )

        def send_half(self, q, half, way, k):
            send(self.refs.stage.buf.at[q, pl.ds(144 * half, 144)], *self.pieces(way, k))

        def wait_half(self, way, k):
            arrived(*self.pieces(way, k))

        def first(self):
            self.combine(self.q2)
            self.send_half(self.q2, 0, 0, 0)
            self.send_half(self.q2, 1, 1, 0)

        def second(self):
            self.combine(self.q1)
            self.send_half(self.q1, 1, 0, 1)
            self.combine(self.q3)
            self.send_half(self.q3, 0, 1, 1)

        def third(self):
            self.wait_half(0, 0)
            add_into(self.refs.stage.buf, self.q1, 0, 144, self.refs.stage.right.at[0])
            self.send_half(self.q1, 0, 0, 2)
            self.wait_half(1, 0)
            add_into(self.refs.stage.buf, self.q3, 144, 144, self.refs.stage.left.at[0])
            self.send_half(self.q3, 1, 1, 2)

        def finish_x(self):
            total = self.refs.sum
            for k in range(1, 3):
                self.wait_half(0, k)
                self.wait_half(1, k)
            for half in range(2):
                for r in range(0, 144, 48):
                    there = slice(144 * half + r, 144 * half + r + 48)
                    here = slice(r, r + 48)
                    total[there, :] = (
                        self.refs.stage.buf[x, there, :].astype(f32)
                        + self.refs.stage.right[2 - half, here, :].astype(f32)
                        + self.refs.stage.left[1 + half, here, :].astype(f32)
                    )
            total[OWN : OWN + 8, :] = jnp.zeros((8, self.width), f32)
            for k in range(NZ):
                both = [
                    total[h * (NZ * ROWS) + k * ROWS : h * (NZ * ROWS) + k * ROWS + 24, :]
                    for h in range(NH)
                ]
                self.refs.ring.buf[k] = jnp.concatenate(both, axis=0).astype(b16)

        def last_total(self):
            self.z.finish()
            return self.z.total(slice(0, PAIR))

    class GroupB(Group):
        def __init__(self, refs, begin, width, steps):
            super().__init__(refs, begin, width)
            self.z = Ring(refs.stage, z, NZ, near_z, steps)

        def pack(self):
            pack = self.refs.pack
            weight_0, weight_1 = grad_act[0:1, self.span], grad_act[1:2, self.span]
            for k in range(NZ):
                for g in range(NX * NH):
                    begin = g * (NZ * ROWS) + k * ROWS
                    source = slice(begin, begin + ROWS)
                    pack[g * ROWS : g * ROWS + ROWS, :] = (
                        product[0, source, self.span] * weight_0
                        + product[1, source, self.span] * weight_1
                    )
                self.refs.stage.buf[k] = pack[...].astype(b16)

        def finish_z(self):
            self.z.finish()
            total = self.refs.sum
            for r in range(0, 144, 48):
                total[r : r + 48, :] = self.z.total(slice(r, r + 48))
            total[144:152, :] = jnp.zeros((8, self.width), f32)
            for k in range(NX):
                both = [
                    total[(k * NH + h) * ROWS : (k * NH + h) * ROWS + 24, :] for h in range(NH)
                ]
                self.refs.ring.buf[k] = jnp.concatenate(both, axis=0).astype(b16)

        def send_x(self):
            refs = self.refs.ring
            for d in range(1, NX):
                source, sems = refs.buf.at[(x + d) % NX], (refs.send.at[d - 1], refs.recv.at[d - 1])
                send(source, refs.right.at[d - 1], *sems, at_x(d))

        def last_total(self):
            refs = self.refs.ring
            value = refs.buf[x].astype(f32)
            for d in range(1, NX):
                arrived(refs.right.at[d - 1], refs.send.at[d - 1], refs.recv.at[d - 1], at_x(d))
                value += refs.right[d - 1].astype(f32)
            return value

    a1 = GroupA(s.a[0], *GROUPS_A[0], (3, 4))
    a2 = GroupA(s.a[1], *GROUPS_A[1], (4, 3))
    b1 = GroupB(s.b[0], *GROUPS_B[0], (4, 3))
    b2 = GroupB(s.b[1], *GROUPS_B[1], (3, 4))

    pairs = Refs({})

    def pairs_1():
        halves = []
        for buf in (s.pool.buf, s.pool_other):
            both = [buf[:, :, :, r, :].reshape(HALF, D).astype(f32) for r in range(2)]
            halves.append(both[0] + both[1])
        lower = jnp.where(core == 0, halves[0], halves[1])
        upper = jnp.where(core == 0, halves[1], halves[0])
        all_pooled = jnp.concatenate([lower, upper], axis=0)
        block, weights, emb = block_gradient(all_pooled)
        pick = (iota((D, ROWS), 0) == iota((D, ROWS), 1) + dp * ROWS).astype(b16)
        pairs.columns = mm(block, pick).astype(b16)
        pairs.features = mm(s.text_rows[...], pick).astype(b16)
        pairs.weights, pairs.emb = weights, emb

    def pairs_2():
        grad_text = mm_tn(pairs.weights, pairs.emb)
        unit = s.text_unit[...]
        along = jnp.sum(unit * grad_text, axis=1, keepdims=True)
        pairs.proj = ((grad_text - unit * along) / s.text_norm[:, 0:1]).astype(b16)

    def pairs_3():
        acts = jnp.concatenate(
            [s.pool.buf[:, :, :, 2 + r, 0:HID].reshape(HALF, HID) for r in range(2)], axis=0
        )
        out_out[...] = mm_tn(pairs.columns, acts)

    def pairs_4():
        out_text[...] = mm_tn(pairs.features, pairs.proj)
        chosen = (iota((2, BATCH), 1) == iota((2, BATCH), 0) * HALF + slot).astype(b16)
        own_text = mm(chosen, pairs.proj).astype(b16)
        out_texts[...] = mm_nt(own_text, w_text[...]).astype(b16)

    a1.first()
    a2.first()
    b1.pack()
    b1.z.step(1)
    a1.second()
    b2.pack()
    b2.z.step(1)
    a2.second()
    pool_gather.wait(0)
    pool_gather.start(1)
    a1.third()
    b1.z.step(2)
    a2.third()
    b2.z.step(2)
    a1.combine(x)
    a2.combine(x)
    b1.z.step(3)
    pool_gather.wait(1)
    pool_gather.start(2)
    b2.z.step(3)
    a1.finish_x()
    a1.z.step(1)
    b1.z.step(4)
    a2.finish_x()
    a2.z.step(1)
    b2.z.step(4)
    a1.z.step(2)
    a2.z.step(2)
    b1.finish_z()
    b1.send_x()
    pool_gather.wait(2)
    pool_gather.start(3)
    b2.finish_z()
    b2.send_x()
    a1.z.step(3)
    a2.z.step(3)
    b1.send_pair()
    a1.z.step(4)
    b2.send_pair()
    a2.z.step(4)
    pool_gather.wait(3)
    core_sems = s.core.send.at[0], s.core.recv.at[0]
    send(s.pool.buf, s.pool_other, *core_sems, other)
    a1.send_pair()
    a2.send_pair()
    arrived(s.pool_other, *core_sems, other)
    pairs_1()
    pairs_2()
    pairs_3()
    pairs_4()
    for group in (b1, b2, a1, a2):
        group.result()
    for copy in sent:
        copy.wait_send()
    text_gather.drain(3)
    pool_gather.drain(4)

    def drain_tiles(t, carry):
        for k in range(3):
            tile_copy(k, t).wait_send()
        return carry

    lax.fori_loop(0, 2 * TILES, drain_tiles, 0)


def hand_on(*refs):
    for k in range(4):
        refs[4 + k][...] = refs[k][...]


def shards(images, ln_gain, w_in, b_in, w_out, texts, w_text, b_text, logit_scale, logit_bias):
    vmem = pl.BlockSpec(memory_space=pltpu.VMEM)
    smem = pl.BlockSpec(memory_space=pltpu.SMEM)
    hbm = pl.BlockSpec(memory_space=pl.ANY)
    dma = pltpu.SemaphoreType.DMA
    V = pltpu.VMEM
    def with_sems(count, **buffers):
        return dict(send=dma(count), recv=dma(count), **buffers)

    def ring(kind, shape, steps, width):
        return with_sems(
            (sum(steps),),
            buf=V(shape + (width,), kind),
            right=V((steps[0],) + shape[1:] + (width,), kind),
            left=V((steps[1],) + shape[1:] + (width,), kind),
        )

    def pair(width):
        return with_sems((1,), buf=V((NH, 24, width), f32), right=V((24, width), f32))

    refs = dict(
        w_in=V((HID, D), b16),
        w_tail=V((PADDED - HID // TILE * TILE, D), b16),
        w_out=V((HID, D), b16),
        w_text=V((D, D), b16),
        gain_col=V((D, 128), f32),
        bias_col=V((D, 128), f32),
        row_pad=V((1, D), f32),
        full=V((2 * TILES, NM, OWN, TILE), b16),
        normed=V((2 * TILES, D, TILE), b16),
        slopes=V((2 * TILES, PADDED, TILE), b16),
        act_sum=V((2, 8, D), f32),
        image_sum=V((2, 8, D), f32),
        product=V((2, D, D), f32),
        parts=V((NM, 2, D), f32),
        pool_other=V((NX, NH, NZ, 4, D), b16),
        text_rows=V((BATCH, D), b16),
        text_emb=V((BATCH, D), b16),
        text_unit=V((BATCH, D), f32),
        text_norm=V((BATCH, 128), f32),
        grad_act=V((2, D), f32),
        load_sem=dma((8,)),
        images=V((2, OWN, PATCH), b16),
        own_texts=V((2, D), b16),
        gain_row=V((D,), f32),
        bias_in=V((HID,), f32),
        bias_text=V((D,), f32),
        img=with_sems((3, 2 * TILES)),
        part=with_sems((3,)),
        core=with_sems((1,)),
        texts=with_sems((11,), buf=V((NX, NZ, NH, 2, D), f32)),
        pool=with_sems((12,), buf=V((NX, NH, NZ, 4, D), b16)),
    )
    def group_a(width, steps):
        stage = with_sems(
            (6,),
            buf=V((NX, OWN, width), b16),
            right=V((3, 144, width), b16),
            left=V((3, 144, width), b16),
        )
        return dict(
            stage=stage,
            sum=V((OWN + 8, width), f32),
            ring=ring(b16, (NZ, PAIR), steps, width),
            pair=pair(width),
        )

    def group_b(width, steps):
        return dict(
            pack=V((144, width), f32),
            stage=ring(b16, (NZ, 144), steps, width),
            sum=V((152, width), f32),
            ring=with_sems(
                (NX - 1,), buf=V((NX, PAIR, width), b16), right=V((NX - 1, PAIR, width), b16)
            ),
            pair=pair(width),
        )

    refs.update(
        a=[group_a(GROUPS_A[0][1], (3, 4)), group_a(GROUPS_A[1][1], (4, 3))],
        b=[group_b(GROUPS_B[0][1], (4, 3)), group_b(GROUPS_B[1][1], (3, 4))],
    )
    out_shape = [
        jax.ShapeDtypeStruct((ROWS, HID), f32),
        jax.ShapeDtypeStruct((ROWS, HID), f32),
        jax.ShapeDtypeStruct((ROWS, D), f32),
        jax.ShapeDtypeStruct((2, D), b16),
    ]
    results = pl.pallas_call(
        kernel,
        out_shape=out_shape,
        in_specs=[hbm] * 5 + [smem] * 2 + [hbm] * 3,
        out_specs=[vmem] * 4,
        scratch_shapes=[refs],
        compiler_params=pltpu.CompilerParams(
            collective_id=0, has_side_effects=True, vmem_limit_bytes=58 << 20
        ),
    )(
        images.transpose(0, 2, 1),
        ln_gain,
        b_in,
        b_text,
        texts,
        logit_scale,
        logit_bias,
        w_in.T,
        w_out,
        w_text,
    )
    grad_in, grad_out, grad_text, grad_texts = pl.pallas_call(
        hand_on,
        out_shape=out_shape,
        in_specs=[vmem] * 4,
        out_specs=[vmem] * 4,
        compiler_params=pltpu.CompilerParams(vmem_limit_bytes=58 << 20),
    )(*results)
    return grad_in, grad_out.T, grad_text, grad_texts


def solution(mesh):
    placed = (
        P("dp", None, "mp"),
        P(),
        P(None, "mp"),
        P("mp"),
        P("mp", None),
        P("dp", None),
        P(),
        P(),
        P(),
        P(),
    )
    return jax.shard_map(
        shards,
        mesh=mesh,
        in_specs=placed,
        out_specs=(P("dp", "mp"), P("mp", "dp"), P("dp", None), P("dp", None)),
        check_vma=False,
    )
```

```python
import jax
import jax.numpy as jnp
from jax import lax
from jax.experimental import pallas as pl
from jax.experimental.pallas import tpu as pltpu
from jax.sharding import PartitionSpec as P

sqrt_two_pi = 0.7978845608028654
cubic_term = 0.044715
epsilon = 1e-06

NX, NH, NZ, NM = 4, 2, 8, 4
D = 1152
HID = 1076
PATCH = 729
OWN = D // 4
TILE = 256
TILES = 3
ROWS = 18
PAIR = 48
GROUPS_A = ((0, 384), (384, 256))
GROUPS_B = ((640, 256), (896, 256))
PADDED = 1088
BATCH = 128
HALF = 64

f32 = jnp.float32
b16 = jnp.bfloat16
MESH = pl.DeviceIdType.MESH


def mm(a, b):
    return lax.dot_general(a, b, (((1,), (0,)), ((), ())), preferred_element_type=f32)


def mm_nt(a, b):
    return lax.dot_general(a, b, (((1,), (1,)), ((), ())), preferred_element_type=f32)


def mm_tn(a, b):
    return lax.dot_general(a, b, (((0,), (0,)), ((), ())), preferred_element_type=f32)


class Refs:
    def __init__(self, values):
        for name, value in values.items():
            if isinstance(value, (tuple, list)):
                value = [Refs(part) for part in value]
            setattr(self, name, Refs(value) if isinstance(value, dict) else value)


def iota(shape, axis):
    return lax.broadcasted_iota(jnp.int32, shape, axis)


def three_parts(values):
    high = values.astype(b16)
    rest = values - high.astype(f32)
    middle = rest.astype(b16)
    low = (rest - middle.astype(f32)).astype(b16)
    return high, middle, low


def gelu_and_slope(values):
    squared = values * values
    tanh_part = jnp.tanh(values * (sqrt_two_pi + (sqrt_two_pi * cubic_term) * squared))
    half = 0.5 + 0.5 * tanh_part
    bend = (1.0 - tanh_part * tanh_part) * (
        0.5 * sqrt_two_pi + (1.5 * sqrt_two_pi * cubic_term) * squared
    )
    return values * half, half + values * bend


def kernel(
    images_hbm,
    gain_hbm,
    bias_hbm,
    shift_hbm,
    texts_hbm,
    scale_ref,
    shift_ref,
    w_in_hbm,
    w_out_hbm,
    w_text_hbm,
    out_in,
    out_out,
    out_text,
    out_texts,
    s,
):
    s = Refs(s)
    w_in, w_pad, w_out, w_text = s.w_in, s.w_pad, s.w_out, s.w_text
    images, texts = s.images, s.own_texts
    gain_row, bias_in, bias_text = s.gain_row, s.bias_in, s.bias_text
    full, normed, slopes, product = s.full, s.normed, s.slopes, s.product
    act_sum, image_sum, grad_act, parts = s.act_sum, s.image_sum, s.grad_act, s.parts
    act_lanes, before = s.act_lanes, s.before

    dp = lax.axis_index("dp")
    mp = lax.axis_index("mp")
    x = dp // (NH * NZ)
    yh = (dp // NZ) % NH
    z = dp % NZ
    slot = (x * NZ + z) * NH + yh
    yl = mp // 2
    core = mp % 2
    mp_chip = (1 - yl) * 2 + core
    mp_core = yl * 2 + (1 - core)
    mp_far = (1 - yl) * 2 + (1 - core)
    chip, other, far = (dp, mp_chip), (dp, mp_core), (dp, mp_far)

    def at_z(d):
        return ((x * NH + yh) * NZ + (z + d) % NZ, mp)

    def at_x(d):
        return ((((x + d) % NX) * NH + yh) * NZ + z, mp)

    def at_yh():
        return ((x * NH + (1 - yh)) * NZ + z, mp)

    def remote(src, dst, send_sem, recv_sem, device):
        return pltpu.make_async_remote_copy(
            src_ref=src,
            dst_ref=dst,
            send_sem=send_sem,
            recv_sem=recv_sem,
            device_id=device,
            device_id_type=MESH,
        )

    sent = []

    def send(src, dst, send_sem, recv_sem, device):
        copy = remote(src, dst, send_sem, recv_sem, device)
        copy.start()
        sent.append(copy)

    def arrived(dst, send_sem, recv_sem, device):
        remote(dst, dst, send_sem, recv_sem, device).wait_recv()

    sources = (w_in_hbm, w_out_hbm, w_text_hbm, images_hbm, texts_hbm, gain_hbm, bias_hbm, shift_hbm)
    targets = (w_in, w_out, w_text, images, texts, gain_row, bias_in, bias_text)
    loads = [
        pltpu.make_async_copy(source, target, s.load_sem.at[k])
        for k, (source, target) in enumerate(zip(sources, targets))
    ]
    for k in (3, 4, 5, 6, 0):
        loads[k].start()

    barrier = pltpu.get_barrier_semaphore()
    partners = [chip, other, far, at_yh()]
    partners += [at_z(d) for d in range(1, NZ)] + [at_x(d) for d in range(1, NX)]
    for partner in partners:
        pl.semaphore_signal(barrier, inc=1, device_id=partner, device_id_type=MESH)

    loads[3].wait()
    for i in range(2):
        for j in range(TILES):
            begin = j * TILE
            width = min(TILE, PATCH - begin)
            if width < TILE:
                full[i * TILES + j, mp] = jnp.zeros((OWN, TILE), b16)
            full[i * TILES + j, mp, :, 0:width] = images[i, :, begin : begin + width]
    loads[4].wait()
    s.texts.buf[x, z, yh] = texts[...].astype(f32)

    pl.semaphore_wait(barrier, len(partners))

    class Gather:
        def __init__(self, refs):
            self.buf, self.send_sem, self.recv_sem = refs.buf, refs.send, refs.recv

        def start(self, stage):
            for n, own, _, device in self.copies(stage):
                remote(own, own, self.send_sem.at[n], self.recv_sem.at[n], device).start()

        def wait(self, stage):
            for n, _, landed, device in self.copies(stage):
                arrived(landed, self.send_sem.at[n], self.recv_sem.at[n], device)

        def drain(self, stages):
            for stage in range(stages):
                for n, own, _, device in self.copies(stage):
                    remote(own, own, self.send_sem.at[n], self.recv_sem.at[n], device).wait_send()

    class TextGather(Gather):
        def copies(self, stage):
            at = self.buf.at
            if stage == 0:
                return [(0, at[x, z, yh], at[x, z, 1 - yh], at_yh())]
            if stage == 1:
                return [(d, at[x, z], at[x, (z + NZ - d) % NZ], at_z(d)) for d in range(1, NZ)]
            return [(7 + d, at[x], at[(x + NX - d) % NX], at_x(d)) for d in range(1, NX)]

    class PoolGather(Gather):
        def copies(self, stage):
            at = self.buf.at
            if stage == 0:
                return [
                    (d, at[x, yh, z], at[x, yh, (z + NZ - d) % NZ], at_z(d)) for d in range(1, NZ)
                ]
            if stage == 1:
                return [(0, at[x, yh], at[x, 1 - yh], at_yh())]
            before, after = (x + NX - 1) % NX, (x + 1) % NX
            if stage == 2:
                return [(8, at[x], at[before], at_x(1)), (9, at[x], at[after], at_x(NX - 1))]
            far = (x + 2) % NX
            return [
                (10, at[before, 0], at[far, 0], at_x(1)),
                (11, at[after, 1], at[far, 1], at_x(NX - 1)),
            ]

    def tile_copy(k, t):
        source = full.at[t, mp_chip if k == 2 else mp]
        return remote(source, source, s.img.send.at[k, t], s.img.recv.at[k, t], chip if k == 0 else other)

    for k in (2, 7, 1):
        loads[k].start()
    text_gather = TextGather(s.texts)
    tile_copy(0, 0).start()
    tile_copy(1, 0).start()
    text_gather.start(0)

    product[...] = jnp.zeros_like(product)
    act_lanes[...] = jnp.zeros_like(act_lanes)
    act_sum[...] = jnp.zeros_like(act_sum)
    image_sum[...] = jnp.zeros_like(image_sum)
    grad_act[...] = jnp.zeros_like(grad_act)
    loads[5].wait()
    loads[6].wait()
    tile_copy(0, 1).start()
    tile_copy(1, 1).start()
    diagonal = iota((128, 128), 0) == iota((128, 128), 1)
    row_pad = s.row_pad
    for row, column, width in ((gain_row, s.gain_col, D), (bias_in, s.bias_col, HID)):
        row_pad[...] = jnp.zeros_like(row_pad)
        row_pad[:, 0:width] = row[...].reshape(1, width)
        for k in range(D // 128):
            span = slice(128 * k, 128 * k + 128)
            picked = jnp.sum(jnp.where(diagonal, row_pad[:, span], 0.0), axis=1, keepdims=True)
            column[span, :] = jnp.broadcast_to(picked, (128, 128))
    whole = HID // TILE * TILE
    chunks = [(begin, TILE) for begin in range(0, whole, TILE)] + [(whole, PADDED - whole)]
    loads[0].wait()
    tail = (iota((PADDED - whole, HID - whole), 0) == iota((PADDED - whole, HID - whole), 1)).astype(
        b16
    )
    w_pad[0:whole, :] = w_in[0:whole, :]
    w_pad[whole:PADDED, :] = mm(tail, w_in[whole:HID, :]).astype(b16)

    def add_product(t):
        i = t // TILES
        for begin, width in chunks:
            span = slice(begin, begin + width)
            product[i, :, span] += mm_nt(normed[t], slopes[t, span, :])

    def work_on(t):
        i = t // TILES
        j = t % TILES
        for h in range(TILE // 128):
            lanes = slice(128 * h, 128 * h + 128)
            total = jnp.zeros((1, 128), f32)
            for m in range(NM):
                total += jnp.sum(full[t, m, :, lanes].astype(f32), axis=0, keepdims=True)
            mean = total * (1.0 / D)
            total = jnp.zeros((1, 128), f32)
            for m in range(NM):
                centered = full[t, m, :, lanes].astype(f32) - mean
                total += jnp.sum(centered * centered, axis=0, keepdims=True)
            factor = lax.rsqrt(total * (1.0 / D) + epsilon)
            for m in range(NM):
                rows = slice(OWN * m, OWN * m + OWN)
                centered = full[t, m, :, lanes].astype(f32) - mean
                normed[t, rows, lanes] = (centered * factor * s.gain_col[rows, :]).astype(b16)
        image_sum[i] += mm_nt(jnp.ones((8, TILE), b16), full[t].reshape(D, TILE))
        before[...] = mm(w_pad[...], normed[t])
        valid = (iota((1, TILE), 1) + j * TILE < PATCH).astype(f32)
        for begin, width in chunks:
            span = slice(begin, begin + width)
            bias = s.bias_col[span, :]
            act, slope = gelu_and_slope(before[span, :] + jnp.concatenate([bias, bias], axis=1))
            slopes[t, span, :] = slope.astype(b16)
            act = act * valid
            act_lanes[i, span, :] += act[:, 0:128] + act[:, 128:TILE]

    def project_texts():
        loads[2].wait()
        loads[7].wait()
        for r in range(2):
            s.text_rows[HALF * r : HALF * r + HALF, :] = (
                s.texts.buf[:, :, :, r, :].reshape(HALF, D).astype(b16)
            )
        projected = mm(s.text_rows[...], w_text[...]) + bias_text[...].reshape(1, D)
        norm = jnp.sqrt(jnp.sum(projected * projected, axis=1, keepdims=True) + epsilon)
        unit = projected / norm
        s.text_norm[...] = jnp.broadcast_to(norm, (BATCH, 128))
        s.text_unit[...] = unit
        s.text_emb[...] = unit.astype(b16)

    def tile_step(t, carry):
        arrived(full.at[t, mp_chip], s.img.send.at[0, t], s.img.recv.at[0, t], chip)
        tile_copy(2, t).start()

        @pl.when(t < 2 * TILES - 2)
        def _():
            tile_copy(0, t + 2).start()
            tile_copy(1, t + 2).start()

        @pl.when(t > 0)
        def _():
            add_product(t - 1)

        @pl.when(t == 0)
        def _():
            text_gather.wait(0)
            text_gather.start(1)

        @pl.when(t == 2)
        def _():
            text_gather.wait(1)
            text_gather.start(2)

        @pl.when(t == 4)
        def _():
            text_gather.wait(2)
            project_texts()

        arrived(full.at[t, mp_core], s.img.send.at[1, t], s.img.recv.at[1, t], other)
        arrived(full.at[t, mp_far], s.img.send.at[2, t], s.img.recv.at[2, t], other)
        work_on(t)
        return carry

    lax.fori_loop(0, 2 * TILES, tile_step, 0)

    loads[1].wait()
    ones = jnp.ones((8, 128), b16)
    for i in range(2):
        high, middle, low = three_parts(act_lanes[i])
        act_sum[i, :, 0:PADDED] = mm_nt(ones, high) + mm_nt(ones, middle) + mm_nt(ones, low)
    row = iota((8, HID), 0)
    split = three_parts(act_sum[0, :, 0:HID]) + three_parts(act_sum[1, :, 0:HID])
    stacked = jnp.zeros((8, HID), f32)
    for k in range(6):
        stacked = jnp.where(row == k, split[k].astype(f32), stacked)
    shares = mm(stacked.astype(b16), w_out[...])
    row = iota((8, D), 0)
    share_0 = jnp.sum(jnp.where(row < 3, shares, 0.0), axis=0, keepdims=True)
    share_1 = jnp.sum(jnp.where((row >= 3) & (row < 6), shares, 0.0), axis=0, keepdims=True)
    first = iota((2, D), 0) == 0
    parts[mp] = jnp.where(first, share_0, share_1)
    group = (chip, other, far)
    for k, partner in enumerate(group):
        own = parts.at[mp]
        send(own, own, s.part.send.at[k], s.part.recv.at[k], partner)
    add_product(2 * TILES - 1)
    for k, source in enumerate((mp_chip, mp_core, mp_far)):
        arrived(parts.at[source], s.part.send.at[k], s.part.recv.at[k], group[k])
    block = parts[0] + parts[1] + parts[2] + parts[3]
    pooled = (jnp.where(first, image_sum[0, 0:2, :], image_sum[1, 0:2, :]) + block) * (1.0 / PATCH)
    pool_gather = PoolGather(s.pool)
    mine = jnp.where(core == 0, pooled[0:1, :], pooled[1:2, :])
    pooled_high = mine.astype(b16)
    pooled_rest = (mine - pooled_high.astype(f32)).astype(b16)
    rows = (pooled_high.astype(f32), pooled_rest.astype(f32), act_sum[0, 0:1, :], act_sum[1, 0:1, :])
    order = iota((4, D), 0)
    packed = jnp.broadcast_to(rows[0], (4, D))
    for k in range(1, 4):
        packed = jnp.where(order == k, rows[k], packed)
    s.pool.buf[x, yh, z] = packed.astype(b16)
    pool_gather.start(0)

    scale = scale_ref[0]
    shift = shift_ref[0]

    def block_gradient(values):
        norm = jnp.sqrt(jnp.sum(values * values, axis=1, keepdims=True) + epsilon)
        unit = values / norm
        emb = unit.astype(b16)
        logits = scale * mm_nt(emb, s.text_emb[...]) + shift
        if values.shape[0] == 2:
            matches = iota((2, BATCH), 1) == iota((2, BATCH), 0) * HALF + slot
        else:
            at = iota((BATCH, BATCH), 0)
            matches = (at & 112) + ((at & 7) << 1) + ((at >> 3) & 1) == iota((BATCH, BATCH), 1)
        signs = jnp.where(matches, 1.0, -1.0)
        coef = -signs * jax.nn.sigmoid(-signs * logits)
        weights = (scale * coef).astype(b16)
        grad_emb = mm(weights, s.text_emb[...])
        along = jnp.sum(unit * grad_emb, axis=1, keepdims=True)
        grad_pooled = (grad_emb - unit * along) / norm
        return (grad_pooled * (1.0 / PATCH)).astype(b16), weights, emb

    own_block, _, _ = block_gradient(pooled)
    grad_act[:, 0:HID] = mm_nt(own_block, w_out[...])

    near_z = (at_z(1), at_z(NZ - 1))
    near_x = (at_x(1), at_x(NX - 1))

    def add_into(target, index, begin, count, received):
        for r in range(0, count, 48):
            there = slice(begin + r, begin + r + 48)
            target[index, there, :] = (
                target[index, there, :].astype(f32) + received[r : r + 48, :].astype(f32)
            ).astype(b16)

    class Ring:
        def __init__(self, refs, place, size, near, steps):
            self.buf = refs.buf
            self.recv = refs.right, refs.left
            self.sems = refs.send, refs.recv
            self.place, self.size, self.near, self.steps = place, size, near, steps

        def wait(self, way, k):
            n = way * self.steps[0] + k - 1
            there = self.recv[way].at[k - 1]
            arrived(there, self.sems[0].at[n], self.sems[1].at[n], self.near[way])
            return there

        def step(self, k):
            for way in range(2):
                if k > self.steps[way]:
                    continue
                away = self.steps[way] + 1 - k
                chunk = (self.place + (self.size - away if way else away)) % self.size
                if k > 1:
                    add_into(self.buf, chunk, 0, self.buf.shape[1], self.wait(way, k - 1))
                n = way * self.steps[0] + k - 1
                send(
                    self.buf.at[chunk],
                    self.recv[way].at[k - 1],
                    self.sems[0].at[n],
                    self.sems[1].at[n],
                    self.near[way],
                )

        def finish(self):
            for way in range(2):
                self.wait(way, self.steps[way])

        def total(self, rows):
            value = self.buf[self.place, rows, :].astype(f32)
            for way in range(2):
                value += self.recv[way][self.steps[way] - 1, rows, :].astype(f32)
            return value

    class Group:
        def __init__(self, refs, begin, width):
            self.refs, self.begin, self.width = refs, begin, width
            self.span = slice(begin, begin + width)

        def send_pair(self):
            value = self.last_total()
            for h in range(NH):
                self.refs.pair.buf[h] = value[24 * h : 24 * h + 24, :]
            sems = self.refs.pair.send.at[0], self.refs.pair.recv.at[0]
            send(self.refs.pair.buf.at[1 - yh], self.refs.pair.right, *sems, at_yh())

        def result(self):
            sems = self.refs.pair.send.at[0], self.refs.pair.recv.at[0]
            arrived(self.refs.pair.right, *sems, at_yh())
            width = min(self.width, HID - self.begin)
            value = self.refs.pair.buf[yh] + self.refs.pair.right[...]
            out_in[:, self.begin : self.begin + width] = value[0:ROWS, 0:width]

    class GroupA(Group):
        def __init__(self, refs, begin, width, steps):
            super().__init__(refs, begin, width)
            self.z = Ring(refs.ring, z, NZ, near_z, steps)
            self.q1, self.q2, self.q3 = (x + 1) % NX, (x + 2) % NX, (x + 3) % NX

        def combine(self, q):
            for r in range(OWN // 48):
                rows = pl.ds(pl.multiple_of(q * OWN + 48 * r, 16), 48)
                self.refs.stage.buf[q, 48 * r : 48 * r + 48, :] = (
                    product[0, rows, self.span] * grad_act[0:1, self.span]
                    + product[1, rows, self.span] * grad_act[1:2, self.span]
                ).astype(b16)

        def pieces(self, way, k):
            n = way * 3 + k
            return (
                (self.refs.stage.left if way else self.refs.stage.right).at[k],
                self.refs.stage.send.at[n],
                self.refs.stage.recv.at[n],
                near_x[way],
            )

        def send_half(self, q, half, way, k):
            send(self.refs.stage.buf.at[q, pl.ds(144 * half, 144)], *self.pieces(way, k))

        def wait_half(self, way, k):
            arrived(*self.pieces(way, k))

        def first(self):
            self.combine(self.q2)
            self.send_half(self.q2, 0, 0, 0)
            self.send_half(self.q2, 1, 1, 0)

        def second(self):
            self.combine(self.q1)
            self.send_half(self.q1, 1, 0, 1)
            self.combine(self.q3)
            self.send_half(self.q3, 0, 1, 1)

        def third(self):
            self.wait_half(0, 0)
            add_into(self.refs.stage.buf, self.q1, 0, 144, self.refs.stage.right.at[0])
            self.send_half(self.q1, 0, 0, 2)
            self.wait_half(1, 0)
            add_into(self.refs.stage.buf, self.q3, 144, 144, self.refs.stage.left.at[0])
            self.send_half(self.q3, 1, 1, 2)

        def finish_x(self):
            total = self.refs.sum
            for k in range(1, 3):
                self.wait_half(0, k)
                self.wait_half(1, k)
            for half in range(2):
                for r in range(0, 144, 48):
                    there = slice(144 * half + r, 144 * half + r + 48)
                    here = slice(r, r + 48)
                    total[there, :] = (
                        self.refs.stage.buf[x, there, :].astype(f32)
                        + self.refs.stage.right[2 - half, here, :].astype(f32)
                        + self.refs.stage.left[1 + half, here, :].astype(f32)
                    )
            total[OWN : OWN + 8, :] = jnp.zeros((8, self.width), f32)
            for k in range(NZ):
                both = [
                    total[h * (NZ * ROWS) + k * ROWS : h * (NZ * ROWS) + k * ROWS + 24, :]
                    for h in range(NH)
                ]
                self.refs.ring.buf[k] = jnp.concatenate(both, axis=0).astype(b16)

        def last_total(self):
            self.z.finish()
            return self.z.total(slice(0, PAIR))

    class GroupB(Group):
        def __init__(self, refs, begin, width, steps):
            super().__init__(refs, begin, width)
            self.z = Ring(refs.stage, z, NZ, near_z, steps)

        def pack(self):
            pack = self.refs.pack
            weight_0, weight_1 = grad_act[0:1, self.span], grad_act[1:2, self.span]
            for k in range(NZ):
                for g in range(NX * NH):
                    begin = g * (NZ * ROWS) + k * ROWS
                    source = slice(begin, begin + ROWS)
                    pack[g * ROWS : g * ROWS + ROWS, :] = (
                        product[0, source, self.span] * weight_0
                        + product[1, source, self.span] * weight_1
                    )
                self.refs.stage.buf[k] = pack[...].astype(b16)

        def finish_z(self):
            self.z.finish()
            total = self.refs.sum
            for r in range(0, 144, 48):
                total[r : r + 48, :] = self.z.total(slice(r, r + 48))
            total[144:152, :] = jnp.zeros((8, self.width), f32)
            for k in range(NX):
                both = [
                    total[(k * NH + h) * ROWS : (k * NH + h) * ROWS + 24, :] for h in range(NH)
                ]
                self.refs.ring.buf[k] = jnp.concatenate(both, axis=0).astype(b16)

        def send_x(self):
            refs = self.refs.ring
            for d in range(1, NX):
                source, sems = refs.buf.at[(x + d) % NX], (refs.send.at[d - 1], refs.recv.at[d - 1])
                send(source, refs.right.at[d - 1], *sems, at_x(d))

        def last_total(self):
            refs = self.refs.ring
            value = refs.buf[x].astype(f32)
            for d in range(1, NX):
                arrived(refs.right.at[d - 1], refs.send.at[d - 1], refs.recv.at[d - 1], at_x(d))
                value += refs.right[d - 1].astype(f32)
            return value

    a1 = GroupA(s.a[0], *GROUPS_A[0], (3, 4))
    a2 = GroupA(s.a[1], *GROUPS_A[1], (4, 3))
    b1 = GroupB(s.b[0], *GROUPS_B[0], (4, 3))
    b2 = GroupB(s.b[1], *GROUPS_B[1], (3, 4))

    pairs = Refs({})

    def pairs_1():
        halves = []
        for buf in (s.pool.buf, s.pool_other):
            both = [buf[:, :, :, r, :].reshape(HALF, D).astype(f32) for r in range(2)]
            halves.append(both[0] + both[1])
        lower = jnp.where(core == 0, halves[0], halves[1])
        upper = jnp.where(core == 0, halves[1], halves[0])
        all_pooled = jnp.concatenate([lower, upper], axis=0)
        block, weights, emb = block_gradient(all_pooled)
        pick = (iota((D, ROWS), 0) == iota((D, ROWS), 1) + dp * ROWS).astype(b16)
        pairs.columns = mm(block, pick).astype(b16)
        pairs.features = mm(s.text_rows[...], pick).astype(b16)
        pairs.weights, pairs.emb = weights, emb

    def pairs_2():
        grad_text = mm_tn(pairs.weights, pairs.emb)
        unit = s.text_unit[...]
        along = jnp.sum(unit * grad_text, axis=1, keepdims=True)
        pairs.proj = ((grad_text - unit * along) / s.text_norm[:, 0:1]).astype(b16)

    def pairs_3():
        acts = jnp.concatenate(
            [s.pool.buf[:, :, :, 2 + r, 0:HID].reshape(HALF, HID) for r in range(2)], axis=0
        )
        out_out[...] = mm_tn(pairs.columns, acts)

    def pairs_4():
        out_text[...] = mm_tn(pairs.features, pairs.proj)
        chosen = (iota((2, BATCH), 1) == iota((2, BATCH), 0) * HALF + slot).astype(b16)
        own_text = mm(chosen, pairs.proj).astype(b16)
        out_texts[...] = mm_nt(own_text, w_text[...]).astype(b16)

    a1.first()
    a2.first()
    b1.pack()
    b1.z.step(1)
    a1.second()
    b2.pack()
    b2.z.step(1)
    a2.second()
    pool_gather.wait(0)
    pool_gather.start(1)
    a1.third()
    b1.z.step(2)
    a2.third()
    b2.z.step(2)
    a1.combine(x)
    a2.combine(x)
    b1.z.step(3)
    pool_gather.wait(1)
    pool_gather.start(2)
    b2.z.step(3)
    a1.finish_x()
    a1.z.step(1)
    b1.z.step(4)
    a2.finish_x()
    a2.z.step(1)
    b2.z.step(4)
    a1.z.step(2)
    a2.z.step(2)
    b1.finish_z()
    b1.send_x()
    pool_gather.wait(2)
    pool_gather.start(3)
    b2.finish_z()
    b2.send_x()
    a1.z.step(3)
    a2.z.step(3)
    b1.send_pair()
    a1.z.step(4)
    b2.send_pair()
    a2.z.step(4)
    pool_gather.wait(3)
    core_sems = s.core.send.at[0], s.core.recv.at[0]
    send(s.pool.buf, s.pool_other, *core_sems, other)
    a1.send_pair()
    a2.send_pair()
    arrived(s.pool_other, *core_sems, other)
    pairs_1()
    pairs_2()
    pairs_3()
    pairs_4()
    for group in (b1, b2, a1, a2):
        group.result()
    for copy in sent:
        copy.wait_send()
    text_gather.drain(3)
    pool_gather.drain(4)

    def drain_tiles(t, carry):
        for k in range(3):
            tile_copy(k, t).wait_send()
        return carry

    lax.fori_loop(0, 2 * TILES, drain_tiles, 0)


def hand_on(*refs):
    for k in range(4):
        refs[4 + k][...] = refs[k][...]


def shards(images, ln_gain, w_in, b_in, w_out, texts, w_text, b_text, logit_scale, logit_bias):
    vmem = pl.BlockSpec(memory_space=pltpu.VMEM)
    smem = pl.BlockSpec(memory_space=pltpu.SMEM)
    hbm = pl.BlockSpec(memory_space=pl.ANY)
    dma = pltpu.SemaphoreType.DMA
    V = pltpu.VMEM
    def with_sems(count, **buffers):
        return dict(send=dma(count), recv=dma(count), **buffers)

    def ring(kind, shape, steps, width):
        return with_sems(
            (sum(steps),),
            buf=V(shape + (width,), kind),
            right=V((steps[0],) + shape[1:] + (width,), kind),
            left=V((steps[1],) + shape[1:] + (width,), kind),
        )

    def pair(width):
        return with_sems((1,), buf=V((NH, 24, width), f32), right=V((24, width), f32))

    refs = dict(
        w_in=V((HID, D), b16),
        w_pad=V((PADDED, D), b16),
        before=V((PADDED, TILE), f32),
        act_lanes=V((2, PADDED, 128), f32),
        w_out=V((HID, D), b16),
        w_text=V((D, D), b16),
        gain_col=V((D, 128), f32),
        bias_col=V((D, 128), f32),
        row_pad=V((1, D), f32),
        full=V((2 * TILES, NM, OWN, TILE), b16),
        normed=V((2 * TILES, D, TILE), b16),
        slopes=V((2 * TILES, PADDED, TILE), b16),
        act_sum=V((2, 8, D), f32),
        image_sum=V((2, 8, D), f32),
        product=V((2, D, D), f32),
        parts=V((NM, 2, D), f32),
        pool_other=V((NX, NH, NZ, 4, D), b16),
        text_rows=V((BATCH, D), b16),
        text_emb=V((BATCH, D), b16),
        text_unit=V((BATCH, D), f32),
        text_norm=V((BATCH, 128), f32),
        grad_act=V((2, D), f32),
        load_sem=dma((8,)),
        images=V((2, OWN, PATCH), b16),
        own_texts=V((2, D), b16),
        gain_row=V((D,), f32),
        bias_in=V((HID,), f32),
        bias_text=V((D,), f32),
        img=with_sems((3, 2 * TILES)),
        part=with_sems((3,)),
        core=with_sems((1,)),
        texts=with_sems((11,), buf=V((NX, NZ, NH, 2, D), f32)),
        pool=with_sems((12,), buf=V((NX, NH, NZ, 4, D), b16)),
    )
    def group_a(width, steps):
        stage = with_sems(
            (6,),
            buf=V((NX, OWN, width), b16),
            right=V((3, 144, width), b16),
            left=V((3, 144, width), b16),
        )
        return dict(
            stage=stage,
            sum=V((OWN + 8, width), f32),
            ring=ring(b16, (NZ, PAIR), steps, width),
            pair=pair(width),
        )

    def group_b(width, steps):
        return dict(
            pack=V((144, width), f32),
            stage=ring(b16, (NZ, 144), steps, width),
            sum=V((152, width), f32),
            ring=with_sems(
                (NX - 1,), buf=V((NX, PAIR, width), b16), right=V((NX - 1, PAIR, width), b16)
            ),
            pair=pair(width),
        )

    refs.update(
        a=[group_a(GROUPS_A[0][1], (3, 4)), group_a(GROUPS_A[1][1], (4, 3))],
        b=[group_b(GROUPS_B[0][1], (4, 3)), group_b(GROUPS_B[1][1], (3, 4))],
    )
    out_shape = [
        jax.ShapeDtypeStruct((ROWS, HID), f32),
        jax.ShapeDtypeStruct((ROWS, HID), f32),
        jax.ShapeDtypeStruct((ROWS, D), f32),
        jax.ShapeDtypeStruct((2, D), b16),
    ]
    results = pl.pallas_call(
        kernel,
        out_shape=out_shape,
        in_specs=[hbm] * 5 + [smem] * 2 + [hbm] * 3,
        out_specs=[vmem] * 4,
        scratch_shapes=[refs],
        compiler_params=pltpu.CompilerParams(
            collective_id=0, has_side_effects=True, vmem_limit_bytes=58 << 20
        ),
    )(
        images.transpose(0, 2, 1),
        ln_gain,
        b_in,
        b_text,
        texts,
        logit_scale,
        logit_bias,
        w_in.T,
        w_out,
        w_text,
    )
    grad_in, grad_out, grad_text, grad_texts = pl.pallas_call(
        hand_on,
        out_shape=out_shape,
        in_specs=[vmem] * 4,
        out_specs=[vmem] * 4,
        compiler_params=pltpu.CompilerParams(vmem_limit_bytes=58 << 20),
    )(*results)
    return grad_in, grad_out.T, grad_text, grad_texts


def solution(mesh):
    placed = (
        P("dp", None, "mp"),
        P(),
        P(None, "mp"),
        P("mp"),
        P("mp", None),
        P("dp", None),
        P(),
        P(),
        P(),
        P(),
    )
    return jax.shard_map(
        shards,
        mesh=mesh,
        in_specs=placed,
        out_specs=(P("dp", "mp"), P("mp", "dp"), P("dp", None), P("dp", None)),
        check_vma=False,
    )
```

```python
import jax
import jax.numpy as jnp
from jax import lax
from jax.experimental import pallas as pl
from jax.experimental.pallas import tpu as pltpu
from jax.sharding import PartitionSpec as P

sqrt_two_pi = 0.7978845608028654
cubic_term = 0.044715
epsilon = 1e-06

NX, NH, NZ, NM = 4, 2, 8, 4
D = 1152
HID = 1076
PATCH = 729
OWN = D // 4
TILE = 256
TILES = 3
ROWS = 18
PAIR = 48
GROUPS_A = ((0, 384), (384, 256))
GROUPS_B = ((640, 256), (896, 256))
PADDED = 1088
BATCH = 128
HALF = 64

f32 = jnp.float32
b16 = jnp.bfloat16
MESH = pl.DeviceIdType.MESH


def mm(a, b):
    return lax.dot_general(a, b, (((1,), (0,)), ((), ())), preferred_element_type=f32)


def mm_nt(a, b):
    return lax.dot_general(a, b, (((1,), (1,)), ((), ())), preferred_element_type=f32)


def mm_tn(a, b):
    return lax.dot_general(a, b, (((0,), (0,)), ((), ())), preferred_element_type=f32)


class Refs:
    def __init__(self, values):
        for name, value in values.items():
            if isinstance(value, (tuple, list)):
                value = [Refs(part) for part in value]
            setattr(self, name, Refs(value) if isinstance(value, dict) else value)


def iota(shape, axis):
    return lax.broadcasted_iota(jnp.int32, shape, axis)


def three_parts(values):
    high = values.astype(b16)
    rest = values - high.astype(f32)
    middle = rest.astype(b16)
    low = (rest - middle.astype(f32)).astype(b16)
    return high, middle, low


def gelu_and_slope(values):
    squared = values * values
    tanh_part = jnp.tanh(values * (sqrt_two_pi + (sqrt_two_pi * cubic_term) * squared))
    half = 0.5 + 0.5 * tanh_part
    bend = (1.0 - tanh_part * tanh_part) * (
        0.5 * sqrt_two_pi + (1.5 * sqrt_two_pi * cubic_term) * squared
    )
    return values * half, half + values * bend


def kernel(
    images_hbm,
    gain_hbm,
    bias_hbm,
    shift_hbm,
    texts_hbm,
    scale_ref,
    shift_ref,
    w_in_hbm,
    w_out_hbm,
    w_text_hbm,
    out_in,
    out_out,
    out_text,
    out_texts,
    s,
):
    s = Refs(s)
    w_in, w_pad, w_out, w_text = s.w_in, s.w_pad, s.w_out, s.w_text
    images, texts = s.images, s.own_texts
    gain_row, bias_in, bias_text = s.gain_row, s.bias_in, s.bias_text
    full, normed, slopes, product = s.full, s.normed, s.slopes, s.product
    act_sum, image_sum, grad_act, parts = s.act_sum, s.image_sum, s.grad_act, s.parts
    act_lanes, before = s.act_lanes, s.before

    dp = lax.axis_index("dp")
    mp = lax.axis_index("mp")
    x = dp // (NH * NZ)
    yh = (dp // NZ) % NH
    z = dp % NZ
    slot = (x * NZ + z) * NH + yh
    yl = mp // 2
    core = mp % 2
    mp_chip = (1 - yl) * 2 + core
    mp_core = yl * 2 + (1 - core)
    mp_far = (1 - yl) * 2 + (1 - core)
    chip, other, far = (dp, mp_chip), (dp, mp_core), (dp, mp_far)

    def at_z(d):
        return ((x * NH + yh) * NZ + (z + d) % NZ, mp)

    def at_x(d):
        return ((((x + d) % NX) * NH + yh) * NZ + z, mp)

    def at_yh():
        return ((x * NH + (1 - yh)) * NZ + z, mp)

    def remote(src, dst, send_sem, recv_sem, device):
        return pltpu.make_async_remote_copy(
            src_ref=src,
            dst_ref=dst,
            send_sem=send_sem,
            recv_sem=recv_sem,
            device_id=device,
            device_id_type=MESH,
        )

    sent = []

    def send(src, dst, send_sem, recv_sem, device):
        copy = remote(src, dst, send_sem, recv_sem, device)
        copy.start()
        sent.append(copy)

    def arrived(dst, send_sem, recv_sem, device):
        remote(dst, dst, send_sem, recv_sem, device).wait_recv()

    sources = (w_in_hbm, w_out_hbm, w_text_hbm, images_hbm, texts_hbm, gain_hbm, bias_hbm, shift_hbm)
    targets = (w_in, w_out, w_text, images, texts, gain_row, bias_in, bias_text)
    loads = [
        pltpu.make_async_copy(source, target, s.load_sem.at[k])
        for k, (source, target) in enumerate(zip(sources, targets))
    ]
    for k in (3, 4, 5, 6, 0):
        loads[k].start()

    barrier = pltpu.get_barrier_semaphore()
    partners = [chip, other, far, at_yh()]
    partners += [at_z(d) for d in range(1, NZ)] + [at_x(d) for d in range(1, NX)]
    for partner in partners:
        pl.semaphore_signal(barrier, inc=1, device_id=partner, device_id_type=MESH)

    loads[3].wait()
    for i in range(2):
        for j in range(TILES):
            begin = j * TILE
            width = min(TILE, PATCH - begin)
            if width < TILE:
                full[i * TILES + j, mp] = jnp.zeros((OWN, TILE), b16)
            full[i * TILES + j, mp, :, 0:width] = images[i, :, begin : begin + width]
    loads[4].wait()
    s.texts.buf[x, z, yh] = texts[...].astype(f32)

    pl.semaphore_wait(barrier, len(partners))

    class Gather:
        def __init__(self, refs):
            self.buf, self.send_sem, self.recv_sem = refs.buf, refs.send, refs.recv

        def start(self, stage):
            for n, own, _, device in self.copies(stage):
                remote(own, own, self.send_sem.at[n], self.recv_sem.at[n], device).start()

        def wait(self, stage):
            for n, _, landed, device in self.copies(stage):
                arrived(landed, self.send_sem.at[n], self.recv_sem.at[n], device)

        def drain(self, stages):
            for stage in range(stages):
                for n, own, _, device in self.copies(stage):
                    remote(own, own, self.send_sem.at[n], self.recv_sem.at[n], device).wait_send()

    class TextGather(Gather):
        def copies(self, stage):
            at = self.buf.at
            if stage == 0:
                return [(0, at[x, z, yh], at[x, z, 1 - yh], at_yh())]
            if stage == 1:
                return [(d, at[x, z], at[x, (z + NZ - d) % NZ], at_z(d)) for d in range(1, NZ)]
            return [(7 + d, at[x], at[(x + NX - d) % NX], at_x(d)) for d in range(1, NX)]

    class PoolGather(Gather):
        def copies(self, stage):
            at = self.buf.at
            if stage == 0:
                return [
                    (d, at[x, yh, z], at[x, yh, (z + NZ - d) % NZ], at_z(d)) for d in range(1, NZ)
                ]
            if stage == 1:
                return [(0, at[x, yh], at[x, 1 - yh], at_yh())]
            before, after = (x + NX - 1) % NX, (x + 1) % NX
            if stage == 2:
                return [(8, at[x], at[before], at_x(1)), (9, at[x], at[after], at_x(NX - 1))]
            far = (x + 2) % NX
            return [
                (10, at[before, 0], at[far, 0], at_x(1)),
                (11, at[after, 1], at[far, 1], at_x(NX - 1)),
            ]

    def tile_copy(k, t):
        source = full.at[t, mp_chip if k == 2 else mp]
        return remote(source, source, s.img.send.at[k, t], s.img.recv.at[k, t], chip if k == 0 else other)

    for k in (2, 7, 1):
        loads[k].start()
    text_gather = TextGather(s.texts)
    tile_copy(0, 0).start()
    tile_copy(1, 0).start()
    text_gather.start(0)

    product[...] = jnp.zeros_like(product)
    act_lanes[...] = jnp.zeros_like(act_lanes)
    act_sum[...] = jnp.zeros_like(act_sum)
    image_sum[...] = jnp.zeros_like(image_sum)
    grad_act[...] = jnp.zeros_like(grad_act)
    loads[5].wait()
    loads[6].wait()
    tile_copy(0, 1).start()
    tile_copy(1, 1).start()
    diagonal = iota((128, 128), 0) == iota((128, 128), 1)
    row_pad = s.row_pad
    for row, column, width in ((gain_row, s.gain_col, D), (bias_in, s.bias_col, HID)):
        row_pad[...] = jnp.zeros_like(row_pad)
        row_pad[:, 0:width] = row[...].reshape(1, width)
        for k in range(D // 128):
            span = slice(128 * k, 128 * k + 128)
            picked = jnp.sum(jnp.where(diagonal, row_pad[:, span], 0.0), axis=1, keepdims=True)
            column[span, :] = jnp.broadcast_to(picked, (128, 128))
    whole = HID // TILE * TILE
    chunks = [(begin, TILE) for begin in range(0, whole, TILE)] + [(whole, PADDED - whole)]
    loads[0].wait()
    tail = (iota((PADDED - whole, HID - whole), 0) == iota((PADDED - whole, HID - whole), 1)).astype(
        b16
    )
    w_pad[0:whole, :] = w_in[0:whole, :]
    w_pad[whole:PADDED, :] = mm(tail, w_in[whole:HID, :]).astype(b16)

    def add_product(t):
        i = t // TILES
        for begin, width in chunks:
            span = slice(begin, begin + width)
            product[i, :, span] += mm_nt(normed[t], slopes[t, span, :])

    def pass_on(t):
        arrived(full.at[t, mp_chip], s.img.send.at[0, t], s.img.recv.at[0, t], chip)
        tile_copy(2, t).start()

    def work_on(t):
        i = t // TILES
        j = t % TILES
        for h in range(TILE // 128):
            lanes = slice(128 * h, 128 * h + 128)
            total = jnp.zeros((1, 128), f32)
            for m in range(NM):
                total += jnp.sum(full[t, m, :, lanes].astype(f32), axis=0, keepdims=True)
            mean = total * (1.0 / D)
            total = jnp.zeros((1, 128), f32)
            for m in range(NM):
                centered = full[t, m, :, lanes].astype(f32) - mean
                total += jnp.sum(centered * centered, axis=0, keepdims=True)
            factor = lax.rsqrt(total * (1.0 / D) + epsilon)
            for m in range(NM):
                rows = slice(OWN * m, OWN * m + OWN)
                centered = full[t, m, :, lanes].astype(f32) - mean
                normed[t, rows, lanes] = (centered * factor * s.gain_col[rows, :]).astype(b16)
        image_sum[i] += mm_nt(jnp.ones((8, TILE), b16), full[t].reshape(D, TILE))
        before[...] = mm(w_pad[...], normed[t])

        @pl.when(t < 2 * TILES - 1)
        def _():
            pass_on(t + 1)

        @pl.when(t < 2 * TILES - 3)
        def _():
            tile_copy(0, t + 3).start()
            tile_copy(1, t + 3).start()

        valid = (iota((1, 128), 1) + (j * TILE + 128) < PATCH).astype(f32)
        for begin, width in chunks:
            span = slice(begin, begin + width)
            bias = s.bias_col[span, :]
            act, slope = gelu_and_slope(before[span, :] + jnp.concatenate([bias, bias], axis=1))
            slopes[t, span, :] = slope.astype(b16)
            act_lanes[i, span, :] += act[:, 0:128] + act[:, 128:TILE] * valid

    def project_texts():
        loads[2].wait()
        loads[7].wait()
        for r in range(2):
            s.text_rows[HALF * r : HALF * r + HALF, :] = (
                s.texts.buf[:, :, :, r, :].reshape(HALF, D).astype(b16)
            )
        projected = mm(s.text_rows[...], w_text[...]) + bias_text[...].reshape(1, D)
        norm = jnp.sqrt(jnp.sum(projected * projected, axis=1, keepdims=True) + epsilon)
        unit = projected / norm
        s.text_norm[...] = jnp.broadcast_to(norm, (BATCH, 128))
        s.text_unit[...] = unit
        s.text_emb[...] = unit.astype(b16)

    def tile_step(t, carry):
        @pl.when(t > 0)
        def _():
            add_product(t - 1)

        @pl.when(t == 0)
        def _():
            text_gather.wait(0)
            text_gather.start(1)

        @pl.when(t == 2)
        def _():
            text_gather.wait(1)
            text_gather.start(2)

        @pl.when(t == 4)
        def _():
            text_gather.wait(2)
            project_texts()

        arrived(full.at[t, mp_core], s.img.send.at[1, t], s.img.recv.at[1, t], other)
        arrived(full.at[t, mp_far], s.img.send.at[2, t], s.img.recv.at[2, t], other)
        work_on(t)
        return carry

    pass_on(0)
    tile_copy(0, 2).start()
    tile_copy(1, 2).start()
    lax.fori_loop(0, 2 * TILES, tile_step, 0)

    loads[1].wait()
    ones = jnp.ones((8, 128), b16)
    for i in range(2):
        high, middle, low = three_parts(act_lanes[i])
        act_sum[i, :, 0:PADDED] = mm_nt(ones, high) + mm_nt(ones, middle) + mm_nt(ones, low)
    row = iota((8, HID), 0)
    split = three_parts(act_sum[0, :, 0:HID]) + three_parts(act_sum[1, :, 0:HID])
    stacked = jnp.zeros((8, HID), f32)
    for k in range(6):
        stacked = jnp.where(row == k, split[k].astype(f32), stacked)
    shares = mm(stacked.astype(b16), w_out[...])
    row = iota((8, D), 0)
    share_0 = jnp.sum(jnp.where(row < 3, shares, 0.0), axis=0, keepdims=True)
    share_1 = jnp.sum(jnp.where((row >= 3) & (row < 6), shares, 0.0), axis=0, keepdims=True)
    first = iota((2, D), 0) == 0
    parts[mp] = jnp.where(first, share_0, share_1)
    group = (chip, other, far)
    for k, partner in enumerate(group):
        own = parts.at[mp]
        send(own, own, s.part.send.at[k], s.part.recv.at[k], partner)
    add_product(2 * TILES - 1)
    for k, source in enumerate((mp_chip, mp_core, mp_far)):
        arrived(parts.at[source], s.part.send.at[k], s.part.recv.at[k], group[k])
    block = parts[0] + parts[1] + parts[2] + parts[3]
    pooled = (jnp.where(first, image_sum[0, 0:2, :], image_sum[1, 0:2, :]) + block) * (1.0 / PATCH)
    pool_gather = PoolGather(s.pool)
    mine = jnp.where(core == 0, pooled[0:1, :], pooled[1:2, :])
    pooled_high = mine.astype(b16)
    pooled_rest = (mine - pooled_high.astype(f32)).astype(b16)
    rows = (pooled_high.astype(f32), pooled_rest.astype(f32), act_sum[0, 0:1, :], act_sum[1, 0:1, :])
    order = iota((4, D), 0)
    packed = jnp.broadcast_to(rows[0], (4, D))
    for k in range(1, 4):
        packed = jnp.where(order == k, rows[k], packed)
    s.pool.buf[x, yh, z] = packed.astype(b16)
    pool_gather.start(0)

    scale = scale_ref[0]
    shift = shift_ref[0]

    def block_gradient(values):
        norm = jnp.sqrt(jnp.sum(values * values, axis=1, keepdims=True) + epsilon)
        unit = values / norm
        emb = unit.astype(b16)
        logits = scale * mm_nt(emb, s.text_emb[...]) + shift
        if values.shape[0] == 2:
            matches = iota((2, BATCH), 1) == iota((2, BATCH), 0) * HALF + slot
        else:
            at = iota((BATCH, BATCH), 0)
            matches = (at & 112) + ((at & 7) << 1) + ((at >> 3) & 1) == iota((BATCH, BATCH), 1)
        signs = jnp.where(matches, 1.0, -1.0)
        coef = -signs * jax.nn.sigmoid(-signs * logits)
        weights = (scale * coef).astype(b16)
        grad_emb = mm(weights, s.text_emb[...])
        along = jnp.sum(unit * grad_emb, axis=1, keepdims=True)
        grad_pooled = (grad_emb - unit * along) / norm
        return (grad_pooled * (1.0 / PATCH)).astype(b16), weights, emb

    own_block, _, _ = block_gradient(pooled)
    grad_act[:, 0:HID] = mm_nt(own_block, w_out[...])

    near_z = (at_z(1), at_z(NZ - 1))
    near_x = (at_x(1), at_x(NX - 1))

    def add_into(target, index, begin, count, received):
        for r in range(0, count, 48):
            there = slice(begin + r, begin + r + 48)
            target[index, there, :] = (
                target[index, there, :].astype(f32) + received[r : r + 48, :].astype(f32)
            ).astype(b16)

    class Ring:
        def __init__(self, refs, place, size, near, steps):
            self.buf = refs.buf
            self.recv = refs.right, refs.left
            self.sems = refs.send, refs.recv
            self.place, self.size, self.near, self.steps = place, size, near, steps

        def wait(self, way, k):
            n = way * self.steps[0] + k - 1
            there = self.recv[way].at[k - 1]
            arrived(there, self.sems[0].at[n], self.sems[1].at[n], self.near[way])
            return there

        def step(self, k):
            for way in range(2):
                if k > self.steps[way]:
                    continue
                away = self.steps[way] + 1 - k
                chunk = (self.place + (self.size - away if way else away)) % self.size
                if k > 1:
                    add_into(self.buf, chunk, 0, self.buf.shape[1], self.wait(way, k - 1))
                n = way * self.steps[0] + k - 1
                send(
                    self.buf.at[chunk],
                    self.recv[way].at[k - 1],
                    self.sems[0].at[n],
                    self.sems[1].at[n],
                    self.near[way],
                )

        def finish(self):
            for way in range(2):
                self.wait(way, self.steps[way])

        def total(self, rows):
            value = self.buf[self.place, rows, :].astype(f32)
            for way in range(2):
                value += self.recv[way][self.steps[way] - 1, rows, :].astype(f32)
            return value

    class Group:
        def __init__(self, refs, begin, width):
            self.refs, self.begin, self.width = refs, begin, width
            self.span = slice(begin, begin + width)

        def send_pair(self):
            value = self.last_total()
            for h in range(NH):
                self.refs.pair.buf[h] = value[24 * h : 24 * h + 24, :]
            sems = self.refs.pair.send.at[0], self.refs.pair.recv.at[0]
            send(self.refs.pair.buf.at[1 - yh], self.refs.pair.right, *sems, at_yh())

        def result(self):
            sems = self.refs.pair.send.at[0], self.refs.pair.recv.at[0]
            arrived(self.refs.pair.right, *sems, at_yh())
            width = min(self.width, HID - self.begin)
            value = self.refs.pair.buf[yh] + self.refs.pair.right[...]
            out_in[:, self.begin : self.begin + width] = value[0:ROWS, 0:width]

    class GroupA(Group):
        def __init__(self, refs, begin, width, steps):
            super().__init__(refs, begin, width)
            self.z = Ring(refs.ring, z, NZ, near_z, steps)
            self.q1, self.q2, self.q3 = (x + 1) % NX, (x + 2) % NX, (x + 3) % NX

        def combine(self, q):
            for r in range(OWN // 48):
                rows = pl.ds(pl.multiple_of(q * OWN + 48 * r, 16), 48)
                self.refs.stage.buf[q, 48 * r : 48 * r + 48, :] = (
                    product[0, rows, self.span] * grad_act[0:1, self.span]
                    + product[1, rows, self.span] * grad_act[1:2, self.span]
                ).astype(b16)

        def pieces(self, way, k):
            n = way * 3 + k
            return (
                (self.refs.stage.left if way else self.refs.stage.right).at[k],
                self.refs.stage.send.at[n],
                self.refs.stage.recv.at[n],
                near_x[way],
            )

        def send_half(self, q, half, way, k):
            send(self.refs.stage.buf.at[q, pl.ds(144 * half, 144)], *self.pieces(way, k))

        def wait_half(self, way, k):
            arrived(*self.pieces(way, k))

        def first(self):
            self.combine(self.q2)
            self.send_half(self.q2, 0, 0, 0)
            self.send_half(self.q2, 1, 1, 0)

        def second(self):
            self.combine(self.q1)
            self.send_half(self.q1, 1, 0, 1)
            self.combine(self.q3)
            self.send_half(self.q3, 0, 1, 1)

        def third(self):
            self.wait_half(0, 0)
            add_into(self.refs.stage.buf, self.q1, 0, 144, self.refs.stage.right.at[0])
            self.send_half(self.q1, 0, 0, 2)
            self.wait_half(1, 0)
            add_into(self.refs.stage.buf, self.q3, 144, 144, self.refs.stage.left.at[0])
            self.send_half(self.q3, 1, 1, 2)

        def finish_x(self):
            total = self.refs.sum
            for k in range(1, 3):
                self.wait_half(0, k)
                self.wait_half(1, k)
            for half in range(2):
                for r in range(0, 144, 48):
                    there = slice(144 * half + r, 144 * half + r + 48)
                    here = slice(r, r + 48)
                    total[there, :] = (
                        self.refs.stage.buf[x, there, :].astype(f32)
                        + self.refs.stage.right[2 - half, here, :].astype(f32)
                        + self.refs.stage.left[1 + half, here, :].astype(f32)
                    )
            total[OWN : OWN + 8, :] = jnp.zeros((8, self.width), f32)
            for k in range(NZ):
                both = [
                    total[h * (NZ * ROWS) + k * ROWS : h * (NZ * ROWS) + k * ROWS + 24, :]
                    for h in range(NH)
                ]
                self.refs.ring.buf[k] = jnp.concatenate(both, axis=0).astype(b16)

        def last_total(self):
            self.z.finish()
            return self.z.total(slice(0, PAIR))

    class GroupB(Group):
        def __init__(self, refs, begin, width, steps):
            super().__init__(refs, begin, width)
            self.z = Ring(refs.stage, z, NZ, near_z, steps)

        def pack(self):
            pack = self.refs.pack
            weight_0, weight_1 = grad_act[0:1, self.span], grad_act[1:2, self.span]
            for k in range(NZ):
                for g in range(NX * NH):
                    begin = g * (NZ * ROWS) + k * ROWS
                    source = slice(begin, begin + ROWS)
                    pack[g * ROWS : g * ROWS + ROWS, :] = (
                        product[0, source, self.span] * weight_0
                        + product[1, source, self.span] * weight_1
                    )
                self.refs.stage.buf[k] = pack[...].astype(b16)

        def finish_z(self):
            self.z.finish()
            total = self.refs.sum
            for r in range(0, 144, 48):
                total[r : r + 48, :] = self.z.total(slice(r, r + 48))
            total[144:152, :] = jnp.zeros((8, self.width), f32)
            for k in range(NX):
                both = [
                    total[(k * NH + h) * ROWS : (k * NH + h) * ROWS + 24, :] for h in range(NH)
                ]
                self.refs.ring.buf[k] = jnp.concatenate(both, axis=0).astype(b16)

        def send_x(self):
            refs = self.refs.ring
            for d in range(1, NX):
                source, sems = refs.buf.at[(x + d) % NX], (refs.send.at[d - 1], refs.recv.at[d - 1])
                send(source, refs.right.at[d - 1], *sems, at_x(d))

        def last_total(self):
            refs = self.refs.ring
            value = refs.buf[x].astype(f32)
            for d in range(1, NX):
                arrived(refs.right.at[d - 1], refs.send.at[d - 1], refs.recv.at[d - 1], at_x(d))
                value += refs.right[d - 1].astype(f32)
            return value

    a1 = GroupA(s.a[0], *GROUPS_A[0], (3, 4))
    a2 = GroupA(s.a[1], *GROUPS_A[1], (4, 3))
    b1 = GroupB(s.b[0], *GROUPS_B[0], (4, 3))
    b2 = GroupB(s.b[1], *GROUPS_B[1], (3, 4))

    pairs = Refs({})

    def pairs_1():
        halves = []
        for buf in (s.pool.buf, s.pool_other):
            both = [buf[:, :, :, r, :].reshape(HALF, D).astype(f32) for r in range(2)]
            halves.append(both[0] + both[1])
        lower = jnp.where(core == 0, halves[0], halves[1])
        upper = jnp.where(core == 0, halves[1], halves[0])
        all_pooled = jnp.concatenate([lower, upper], axis=0)
        block, weights, emb = block_gradient(all_pooled)
        pick = (iota((D, ROWS), 0) == iota((D, ROWS), 1) + dp * ROWS).astype(b16)
        pairs.columns = mm(block, pick).astype(b16)
        pairs.features = mm(s.text_rows[...], pick).astype(b16)
        pairs.weights, pairs.emb = weights, emb

    def pairs_2():
        grad_text = mm_tn(pairs.weights, pairs.emb)
        unit = s.text_unit[...]
        along = jnp.sum(unit * grad_text, axis=1, keepdims=True)
        pairs.proj = ((grad_text - unit * along) / s.text_norm[:, 0:1]).astype(b16)

    def pairs_3():
        for r in range(2):
            s.acts[HALF * r : HALF * r + HALF, :] = s.pool.buf[:, :, :, 2 + r, :].reshape(HALF, D)

    def pairs_4():
        out_out[...] = mm_tn(pairs.columns, s.acts[:, 0:HID])
        out_text[...] = mm_tn(pairs.features, pairs.proj)
        chosen = (iota((2, BATCH), 1) == iota((2, BATCH), 0) * HALF + slot).astype(b16)
        own_text = mm(chosen, pairs.proj).astype(b16)
        out_texts[...] = mm_nt(own_text, w_text[...]).astype(b16)

    a1.first()
    a2.first()
    b1.pack()
    b1.z.step(1)
    a1.second()
    b2.pack()
    b2.z.step(1)
    a2.second()
    pool_gather.wait(0)
    pool_gather.start(1)
    a1.third()
    b1.z.step(2)
    a2.third()
    b2.z.step(2)
    a1.combine(x)
    a2.combine(x)
    b1.z.step(3)
    pool_gather.wait(1)
    b2.z.step(3)
    a1.finish_x()
    a1.z.step(1)
    b1.z.step(4)
    a2.finish_x()
    a2.z.step(1)
    pool_gather.start(2)
    b2.z.step(4)
    a1.z.step(2)
    a2.z.step(2)
    b1.finish_z()
    b1.send_x()
    b2.finish_z()
    b2.send_x()
    a1.z.step(3)
    pool_gather.wait(2)
    pool_gather.start(3)
    a2.z.step(3)
    b1.send_pair()
    a1.z.step(4)
    b2.send_pair()
    a2.z.step(4)
    pool_gather.wait(3)
    core_sems = s.core.send.at[0], s.core.recv.at[0]
    send(s.pool.buf, s.pool_other, *core_sems, other)
    pairs_3()
    a1.send_pair()
    a2.send_pair()
    arrived(s.pool_other, *core_sems, other)
    pairs_1()
    pairs_2()
    pairs_4()
    for group in (b1, b2, a1, a2):
        group.result()
    for copy in sent:
        copy.wait_send()
    text_gather.drain(3)
    pool_gather.drain(4)

    def drain_tiles(t, carry):
        for k in range(3):
            tile_copy(k, t).wait_send()
        return carry

    lax.fori_loop(0, 2 * TILES, drain_tiles, 0)


def hand_on(*refs):
    for k in range(4):
        refs[4 + k][...] = refs[k][...]


def shards(images, ln_gain, w_in, b_in, w_out, texts, w_text, b_text, logit_scale, logit_bias):
    vmem = pl.BlockSpec(memory_space=pltpu.VMEM)
    smem = pl.BlockSpec(memory_space=pltpu.SMEM)
    hbm = pl.BlockSpec(memory_space=pl.ANY)
    dma = pltpu.SemaphoreType.DMA
    V = pltpu.VMEM
    def with_sems(count, **buffers):
        return dict(send=dma(count), recv=dma(count), **buffers)

    def ring(kind, shape, steps, width):
        return with_sems(
            (sum(steps),),
            buf=V(shape + (width,), kind),
            right=V((steps[0],) + shape[1:] + (width,), kind),
            left=V((steps[1],) + shape[1:] + (width,), kind),
        )

    def pair(width):
        return with_sems((1,), buf=V((NH, 24, width), f32), right=V((24, width), f32))

    refs = dict(
        w_in=V((HID, D), b16),
        w_pad=V((PADDED, D), b16),
        before=V((PADDED, TILE), f32),
        act_lanes=V((2, PADDED, 128), f32),
        w_out=V((HID, D), b16),
        w_text=V((D, D), b16),
        gain_col=V((D, 128), f32),
        bias_col=V((D, 128), f32),
        row_pad=V((1, D), f32),
        full=V((2 * TILES, NM, OWN, TILE), b16),
        normed=V((2 * TILES, D, TILE), b16),
        slopes=V((2 * TILES, PADDED, TILE), b16),
        act_sum=V((2, 8, D), f32),
        image_sum=V((2, 8, D), f32),
        product=V((2, D, D), f32),
        parts=V((NM, 2, D), f32),
        pool_other=V((NX, NH, NZ, 4, D), b16),
        acts=V((BATCH, D), b16),
        text_rows=V((BATCH, D), b16),
        text_emb=V((BATCH, D), b16),
        text_unit=V((BATCH, D), f32),
        text_norm=V((BATCH, 128), f32),
        grad_act=V((2, D), f32),
        load_sem=dma((8,)),
        images=V((2, OWN, PATCH), b16),
        own_texts=V((2, D), b16),
        gain_row=V((D,), f32),
        bias_in=V((HID,), f32),
        bias_text=V((D,), f32),
        img=with_sems((3, 2 * TILES)),
        part=with_sems((3,)),
        core=with_sems((1,)),
        texts=with_sems((11,), buf=V((NX, NZ, NH, 2, D), f32)),
        pool=with_sems((12,), buf=V((NX, NH, NZ, 4, D), b16)),
    )
    def group_a(width, steps):
        stage = with_sems(
            (6,),
            buf=V((NX, OWN, width), b16),
            right=V((3, 144, width), b16),
            left=V((3, 144, width), b16),
        )
        return dict(
            stage=stage,
            sum=V((OWN + 8, width), f32),
            ring=ring(b16, (NZ, PAIR), steps, width),
            pair=pair(width),
        )

    def group_b(width, steps):
        return dict(
            pack=V((144, width), f32),
            stage=ring(b16, (NZ, 144), steps, width),
            sum=V((152, width), f32),
            ring=with_sems(
                (NX - 1,), buf=V((NX, PAIR, width), b16), right=V((NX - 1, PAIR, width), b16)
            ),
            pair=pair(width),
        )

    refs.update(
        a=[group_a(GROUPS_A[0][1], (3, 4)), group_a(GROUPS_A[1][1], (4, 3))],
        b=[group_b(GROUPS_B[0][1], (4, 3)), group_b(GROUPS_B[1][1], (3, 4))],
    )
    out_shape = [
        jax.ShapeDtypeStruct((ROWS, HID), f32),
        jax.ShapeDtypeStruct((ROWS, HID), f32),
        jax.ShapeDtypeStruct((ROWS, D), f32),
        jax.ShapeDtypeStruct((2, D), b16),
    ]
    results = pl.pallas_call(
        kernel,
        out_shape=out_shape,
        in_specs=[hbm] * 5 + [smem] * 2 + [hbm] * 3,
        out_specs=[vmem] * 4,
        scratch_shapes=[refs],
        compiler_params=pltpu.CompilerParams(
            collective_id=0, has_side_effects=True, vmem_limit_bytes=58 << 20
        ),
    )(
        images.transpose(0, 2, 1),
        ln_gain,
        b_in,
        b_text,
        texts,
        logit_scale,
        logit_bias,
        w_in.T,
        w_out,
        w_text,
    )
    grad_in, grad_out, grad_text, grad_texts = pl.pallas_call(
        hand_on,
        out_shape=out_shape,
        in_specs=[vmem] * 4,
        out_specs=[vmem] * 4,
        compiler_params=pltpu.CompilerParams(vmem_limit_bytes=58 << 20),
    )(*results)
    return grad_in, grad_out.T, grad_text, grad_texts


def solution(mesh):
    placed = (
        P("dp", None, "mp"),
        P(),
        P(None, "mp"),
        P("mp"),
        P("mp", None),
        P("dp", None),
        P(),
        P(),
        P(),
        P(),
    )
    return jax.shard_map(
        shards,
        mesh=mesh,
        in_specs=placed,
        out_specs=(P("dp", "mp"), P("mp", "dp"), P("dp", None), P("dp", None)),
        check_vma=False,
    )
```

```python
import jax
import jax.numpy as jnp
from jax import lax
from jax.experimental import pallas as pl
from jax.experimental.pallas import tpu as pltpu
from jax.sharding import PartitionSpec as P

sqrt_two_pi = 0.7978845608028654
cubic_term = 0.044715
epsilon = 1e-06

NX, NH, NZ, NM = 4, 2, 8, 4
D = 1152
HID = 1076
PATCH = 729
OWN = D // 4
TILE = 256
TILES = 3
ROWS = 18
PAIR = 48
GROUPS_A = ((0, 384), (384, 256))
GROUPS_B = ((640, 256), (896, 256))
PADDED = 1088
BATCH = 128
HALF = 64

f32 = jnp.float32
b16 = jnp.bfloat16
MESH = pl.DeviceIdType.MESH


def mm(a, b):
    return lax.dot_general(a, b, (((1,), (0,)), ((), ())), preferred_element_type=f32)


def mm_nt(a, b):
    return lax.dot_general(a, b, (((1,), (1,)), ((), ())), preferred_element_type=f32)


def mm_tn(a, b):
    return lax.dot_general(a, b, (((0,), (0,)), ((), ())), preferred_element_type=f32)


class Refs:
    def __init__(self, values):
        for name, value in values.items():
            if isinstance(value, (tuple, list)):
                value = [Refs(part) for part in value]
            setattr(self, name, Refs(value) if isinstance(value, dict) else value)


def iota(shape, axis):
    return lax.broadcasted_iota(jnp.int32, shape, axis)


def three_parts(values):
    high = values.astype(b16)
    rest = values - high.astype(f32)
    middle = rest.astype(b16)
    low = (rest - middle.astype(f32)).astype(b16)
    return high, middle, low


def gelu_and_slope(values):
    squared = values * values
    tanh_part = jnp.tanh(values * (sqrt_two_pi + (sqrt_two_pi * cubic_term) * squared))
    half = 0.5 + 0.5 * tanh_part
    bend = (1.0 - tanh_part * tanh_part) * (
        0.5 * sqrt_two_pi + (1.5 * sqrt_two_pi * cubic_term) * squared
    )
    return values * half, half + values * bend


def kernel(
    images_hbm,
    gain_hbm,
    bias_hbm,
    shift_hbm,
    texts_hbm,
    scale_ref,
    shift_ref,
    w_in_hbm,
    w_out_hbm,
    w_text_hbm,
    out_in,
    out_out,
    out_text,
    out_texts,
    s,
):
    s = Refs(s)
    w_in, w_pad, w_out, w_text = s.w_in, s.w_pad, s.w_out, s.w_text
    images, texts = s.images, s.own_texts
    gain_row, bias_in, bias_text = s.gain_row, s.bias_in, s.bias_text
    full, normed, slopes, product = s.full, s.normed, s.slopes, s.product
    act_sum, image_sum, grad_act, parts = s.act_sum, s.image_sum, s.grad_act, s.parts
    act_lanes, before = s.act_lanes, s.before

    dp = lax.axis_index("dp")
    mp = lax.axis_index("mp")
    x = dp // (NH * NZ)
    yh = (dp // NZ) % NH
    z = dp % NZ
    slot = x * 32 + z * NH + yh
    yl = mp // 2
    core = mp % 2
    mp_chip = (1 - yl) * 2 + core
    mp_core = yl * 2 + (1 - core)
    mp_far = (1 - yl) * 2 + (1 - core)
    chip, other, far = (dp, mp_chip), (dp, mp_core), (dp, mp_far)

    def at_z(d):
        return ((x * NH + yh) * NZ + (z + d) % NZ, mp)

    def at_x(d):
        return ((((x + d) % NX) * NH + yh) * NZ + z, mp)

    def at_yh():
        return ((x * NH + (1 - yh)) * NZ + z, mp)

    def remote(src, dst, send_sem, recv_sem, device):
        return pltpu.make_async_remote_copy(
            src_ref=src,
            dst_ref=dst,
            send_sem=send_sem,
            recv_sem=recv_sem,
            device_id=device,
            device_id_type=MESH,
        )

    sent = []

    def send(src, dst, send_sem, recv_sem, device):
        copy = remote(src, dst, send_sem, recv_sem, device)
        copy.start()
        sent.append(copy)

    def arrived(dst, send_sem, recv_sem, device):
        remote(dst, dst, send_sem, recv_sem, device).wait_recv()

    sources = (w_in_hbm, w_out_hbm, w_text_hbm, images_hbm, texts_hbm, gain_hbm, bias_hbm, shift_hbm)
    targets = (w_in, w_out, w_text, images, texts, gain_row, bias_in, bias_text)
    loads = [
        pltpu.make_async_copy(source, target, s.load_sem.at[k])
        for k, (source, target) in enumerate(zip(sources, targets))
    ]
    for k in (3, 4, 5, 6, 0):
        loads[k].start()

    barrier = pltpu.get_barrier_semaphore()
    partners = [chip, other, far, at_yh()]
    partners += [at_z(d) for d in range(1, NZ)] + [at_x(d) for d in range(1, NX)]
    for partner in partners:
        pl.semaphore_signal(barrier, inc=1, device_id=partner, device_id_type=MESH)

    loads[3].wait()
    for i in range(2):
        for j in range(TILES):
            begin = j * TILE
            width = min(TILE, PATCH - begin)
            if width < TILE:
                full[i * TILES + j, mp] = jnp.zeros((OWN, TILE), b16)
            full[i * TILES + j, mp, :, 0:width] = images[i, :, begin : begin + width]
    loads[4].wait()
    s.texts.buf[z, yh] = texts[...].astype(f32)

    pl.semaphore_wait(barrier, len(partners))

    class Gather:
        def __init__(self, refs):
            self.buf, self.send_sem, self.recv_sem = refs.buf, refs.send, refs.recv

        def start(self, stage):
            for n, own, _, device in self.copies(stage):
                remote(own, own, self.send_sem.at[n], self.recv_sem.at[n], device).start()

        def wait(self, stage):
            for n, _, landed, device in self.copies(stage):
                arrived(landed, self.send_sem.at[n], self.recv_sem.at[n], device)

        def drain(self, stages):
            for stage in range(stages):
                for n, own, _, device in self.copies(stage):
                    remote(own, own, self.send_sem.at[n], self.recv_sem.at[n], device).wait_send()

    class TextGather(Gather):
        def copies(self, stage):
            at, dense = self.buf.at, s.text_dense.at
            if stage == 0:
                return [(0, at[z, yh], at[z, 1 - yh], at_yh())]
            if stage == 1:
                return [(d, at[z], at[(z + NZ - d) % NZ], at_z(d)) for d in range(1, NZ)]
            return [(7 + d, dense[x], dense[(x + NX - d) % NX], at_x(d)) for d in range(1, NX)]

        def make_dense(self):
            for r in range(2):
                s.text_dense[x, r] = self.buf[:, :, r, :].reshape(NZ * NH, D).astype(b16)

    class PoolGather(Gather):
        def copies(self, stage):
            at, pool, acts = self.buf.at, s.pool_dense.at, s.act_dense.at
            if stage == 0:
                return [(d, at[yh, z], at[yh, (z + NZ - d) % NZ], at_z(d)) for d in range(1, NZ)]
            if stage == 1:
                return [(0, at[yh], at[1 - yh], at_yh())]
            before, after, far = (x + NX - 1) % NX, (x + 1) % NX, (x + 2) % NX
            right, left = at_x(1), at_x(NX - 1)
            if stage == 2:
                return [
                    (8, pool[x], pool[before], right),
                    (9, pool[x], pool[after], left),
                    (10, acts[x], acts[before], right),
                    (11, acts[x], acts[after], left),
                ]
            lower, upper = pl.ds(0, 8), pl.ds(8, 8)
            return [
                (12, pool[before, lower], pool[far, lower], right),
                (13, pool[after, upper], pool[far, upper], left),
                (14, acts[before, 0], acts[far, 0], right),
                (15, acts[after, 1], acts[far, 1], left),
            ]

        def make_dense(self):
            rows = [self.buf[:, :, k, :].reshape(NH * NZ, D) for k in range(4)]
            s.pool_dense[x] = rows[0].astype(f32) + rows[1].astype(f32)
            s.act_dense[x, 0] = rows[2]
            s.act_dense[x, 1] = rows[3]

    def tile_copy(k, t):
        source = full.at[t, mp_chip if k == 2 else mp]
        return remote(source, source, s.img.send.at[k, t], s.img.recv.at[k, t], chip if k == 0 else other)

    for k in (2, 7, 1):
        loads[k].start()
    text_gather = TextGather(s.texts)
    tile_copy(0, 0).start()
    tile_copy(1, 0).start()
    text_gather.start(0)

    product[...] = jnp.zeros_like(product)
    act_lanes[...] = jnp.zeros_like(act_lanes)
    act_sum[...] = jnp.zeros_like(act_sum)
    image_sum[...] = jnp.zeros_like(image_sum)
    grad_act[...] = jnp.zeros_like(grad_act)
    loads[5].wait()
    loads[6].wait()
    tile_copy(0, 1).start()
    tile_copy(1, 1).start()
    diagonal = iota((128, 128), 0) == iota((128, 128), 1)
    row_pad = s.row_pad
    for row, column, width in ((gain_row, s.gain_col, D), (bias_in, s.bias_col, HID)):
        row_pad[...] = jnp.zeros_like(row_pad)
        row_pad[:, 0:width] = row[...].reshape(1, width)
        for k in range(D // 128):
            span = slice(128 * k, 128 * k + 128)
            picked = jnp.sum(jnp.where(diagonal, row_pad[:, span], 0.0), axis=1, keepdims=True)
            column[span, :] = jnp.broadcast_to(picked, (128, 128))
    whole = HID // TILE * TILE
    chunks = [(begin, TILE) for begin in range(0, whole, TILE)] + [(whole, PADDED - whole)]
    loads[0].wait()
    tail = (iota((PADDED - whole, HID - whole), 0) == iota((PADDED - whole, HID - whole), 1)).astype(
        b16
    )
    w_pad[0:whole, :] = w_in[0:whole, :]
    w_pad[whole:PADDED, :] = mm(tail, w_in[whole:HID, :]).astype(b16)

    def add_product(t):
        i = t // TILES
        for begin, width in chunks:
            span = slice(begin, begin + width)
            product[i, :, span] += mm_nt(normed[t], slopes[t, span, :])

    def pass_on(t):
        arrived(full.at[t, mp_chip], s.img.send.at[0, t], s.img.recv.at[0, t], chip)
        tile_copy(2, t).start()

    def work_on(t):
        i = t // TILES
        j = t % TILES
        for h in range(TILE // 128):
            lanes = slice(128 * h, 128 * h + 128)
            total = jnp.zeros((1, 128), f32)
            for m in range(NM):
                total += jnp.sum(full[t, m, :, lanes].astype(f32), axis=0, keepdims=True)
            mean = total * (1.0 / D)
            total = jnp.zeros((1, 128), f32)
            for m in range(NM):
                centered = full[t, m, :, lanes].astype(f32) - mean
                total += jnp.sum(centered * centered, axis=0, keepdims=True)
            factor = lax.rsqrt(total * (1.0 / D) + epsilon)
            for m in range(NM):
                rows = slice(OWN * m, OWN * m + OWN)
                centered = full[t, m, :, lanes].astype(f32) - mean
                normed[t, rows, lanes] = (centered * factor * s.gain_col[rows, :]).astype(b16)
        image_sum[i] += mm_nt(jnp.ones((8, TILE), b16), full[t].reshape(D, TILE))
        before[...] = mm(w_pad[...], normed[t])

        @pl.when(t < 2 * TILES - 1)
        def _():
            pass_on(t + 1)

        @pl.when(t < 2 * TILES - 3)
        def _():
            tile_copy(0, t + 3).start()
            tile_copy(1, t + 3).start()

        valid = (iota((1, 128), 1) + (j * TILE + 128) < PATCH).astype(f32)
        for begin, width in chunks:
            span = slice(begin, begin + width)
            bias = s.bias_col[span, :]
            act, slope = gelu_and_slope(before[span, :] + jnp.concatenate([bias, bias], axis=1))
            slopes[t, span, :] = slope.astype(b16)
            act_lanes[i, span, :] += act[:, 0:128] + act[:, 128:TILE] * valid

    def project_texts():
        loads[2].wait()
        loads[7].wait()
        projected = mm(s.text_dense[...].reshape(BATCH, D), w_text[...]) + bias_text[...].reshape(1, D)
        norm = jnp.sqrt(jnp.sum(projected * projected, axis=1, keepdims=True) + epsilon)
        unit = projected / norm
        s.text_norm[...] = jnp.broadcast_to(norm, (BATCH, 128))
        s.text_unit[...] = unit
        s.text_emb[...] = unit.astype(b16)

    def tile_step(t, carry):
        @pl.when(t > 0)
        def _():
            add_product(t - 1)

        @pl.when(t == 0)
        def _():
            text_gather.wait(0)
            text_gather.start(1)

        @pl.when(t == 2)
        def _():
            text_gather.wait(1)
            text_gather.make_dense()
            text_gather.start(2)

        @pl.when(t == 4)
        def _():
            text_gather.wait(2)
            project_texts()

        arrived(full.at[t, mp_core], s.img.send.at[1, t], s.img.recv.at[1, t], other)
        arrived(full.at[t, mp_far], s.img.send.at[2, t], s.img.recv.at[2, t], other)
        work_on(t)
        return carry

    pass_on(0)
    tile_copy(0, 2).start()
    tile_copy(1, 2).start()
    lax.fori_loop(0, 2 * TILES, tile_step, 0)

    loads[1].wait()
    ones = jnp.ones((8, 128), b16)
    for i in range(2):
        high, middle, low = three_parts(act_lanes[i])
        act_sum[i, :, 0:PADDED] = mm_nt(ones, high) + mm_nt(ones, middle) + mm_nt(ones, low)
    row = iota((8, HID), 0)
    split = three_parts(act_sum[0, :, 0:HID]) + three_parts(act_sum[1, :, 0:HID])
    stacked = jnp.zeros((8, HID), f32)
    for k in range(6):
        stacked = jnp.where(row == k, split[k].astype(f32), stacked)
    shares = mm(stacked.astype(b16), w_out[...])
    row = iota((8, D), 0)
    share_0 = jnp.sum(jnp.where(row < 3, shares, 0.0), axis=0, keepdims=True)
    share_1 = jnp.sum(jnp.where((row >= 3) & (row < 6), shares, 0.0), axis=0, keepdims=True)
    first = iota((2, D), 0) == 0
    parts[mp] = jnp.where(first, share_0, share_1)
    group = (chip, other, far)
    for k, partner in enumerate(group):
        own = parts.at[mp]
        send(own, own, s.part.send.at[k], s.part.recv.at[k], partner)
    add_product(2 * TILES - 1)
    for k, source in enumerate((mp_chip, mp_core, mp_far)):
        arrived(parts.at[source], s.part.send.at[k], s.part.recv.at[k], group[k])
    block = parts[0] + parts[1] + parts[2] + parts[3]
    pooled = (jnp.where(first, image_sum[0, 0:2, :], image_sum[1, 0:2, :]) + block) * (1.0 / PATCH)
    pool_gather = PoolGather(s.pool)
    mine = jnp.where(core == 0, pooled[0:1, :], pooled[1:2, :])
    pooled_high = mine.astype(b16)
    pooled_rest = (mine - pooled_high.astype(f32)).astype(b16)
    rows = (pooled_high.astype(f32), pooled_rest.astype(f32), act_sum[0, 0:1, :], act_sum[1, 0:1, :])
    order = iota((4, D), 0)
    packed = jnp.broadcast_to(rows[0], (4, D))
    for k in range(1, 4):
        packed = jnp.where(order == k, rows[k], packed)
    s.pool.buf[yh, z] = packed.astype(b16)
    pool_gather.start(0)

    scale = scale_ref[0]
    shift = shift_ref[0]

    def block_gradient(values):
        norm = jnp.sqrt(jnp.sum(values * values, axis=1, keepdims=True) + epsilon)
        unit = values / norm
        emb = unit.astype(b16)
        logits = scale * mm_nt(emb, s.text_emb[...]) + shift
        if values.shape[0] == 2:
            matches = iota((2, BATCH), 1) == iota((2, BATCH), 0) * 16 + slot
        else:
            at = iota((BATCH, BATCH), 0)
            text = (((at >> 4) & 3) << 5) + ((at >> 6) << 4) + ((at & 7) << 1) + ((at >> 3) & 1)
            matches = text == iota((BATCH, BATCH), 1)
        signs = jnp.where(matches, 1.0, -1.0)
        coef = -signs * jax.nn.sigmoid(-signs * logits)
        weights = (scale * coef).astype(b16)
        grad_emb = mm(weights, s.text_emb[...])
        along = jnp.sum(unit * grad_emb, axis=1, keepdims=True)
        grad_pooled = (grad_emb - unit * along) / norm
        return (grad_pooled * (1.0 / PATCH)).astype(b16), weights, emb

    own_block, _, _ = block_gradient(pooled)
    grad_act[:, 0:HID] = mm_nt(own_block, w_out[...])

    near_z = (at_z(1), at_z(NZ - 1))
    near_x = (at_x(1), at_x(NX - 1))

    def add_into(target, index, begin, count, received):
        for r in range(0, count, 48):
            there = slice(begin + r, begin + r + 48)
            target[index, there, :] = (
                target[index, there, :].astype(f32) + received[r : r + 48, :].astype(f32)
            ).astype(b16)

    class Ring:
        def __init__(self, refs, place, size, near, steps):
            self.buf = refs.buf
            self.recv = refs.right, refs.left
            self.sems = refs.send, refs.recv
            self.place, self.size, self.near, self.steps = place, size, near, steps

        def wait(self, way, k):
            n = way * self.steps[0] + k - 1
            there = self.recv[way].at[k - 1]
            arrived(there, self.sems[0].at[n], self.sems[1].at[n], self.near[way])
            return there

        def step(self, k):
            for way in range(2):
                if k > self.steps[way]:
                    continue
                away = self.steps[way] + 1 - k
                chunk = (self.place + (self.size - away if way else away)) % self.size
                if k > 1:
                    add_into(self.buf, chunk, 0, self.buf.shape[1], self.wait(way, k - 1))
                n = way * self.steps[0] + k - 1
                send(
                    self.buf.at[chunk],
                    self.recv[way].at[k - 1],
                    self.sems[0].at[n],
                    self.sems[1].at[n],
                    self.near[way],
                )

        def finish(self):
            for way in range(2):
                self.wait(way, self.steps[way])

        def total(self, rows):
            value = self.buf[self.place, rows, :].astype(f32)
            for way in range(2):
                value += self.recv[way][self.steps[way] - 1, rows, :].astype(f32)
            return value

    class Group:
        def __init__(self, refs, begin, width):
            self.refs, self.begin, self.width = refs, begin, width
            self.span = slice(begin, begin + width)

        def send_pair(self):
            value = self.last_total()
            for h in range(NH):
                self.refs.pair.buf[h] = value[24 * h : 24 * h + 24, :]
            sems = self.refs.pair.send.at[0], self.refs.pair.recv.at[0]
            send(self.refs.pair.buf.at[1 - yh], self.refs.pair.right, *sems, at_yh())

        def result(self):
            sems = self.refs.pair.send.at[0], self.refs.pair.recv.at[0]
            arrived(self.refs.pair.right, *sems, at_yh())
            width = min(self.width, HID - self.begin)
            value = self.refs.pair.buf[yh] + self.refs.pair.right[...]
            out_in[:, self.begin : self.begin + width] = value[0:ROWS, 0:width]

    class GroupA(Group):
        def __init__(self, refs, begin, width, steps):
            super().__init__(refs, begin, width)
            self.z = Ring(refs.ring, z, NZ, near_z, steps)
            self.q1, self.q2, self.q3 = (x + 1) % NX, (x + 2) % NX, (x + 3) % NX

        def combine(self, q):
            for r in range(OWN // 48):
                rows = pl.ds(pl.multiple_of(q * OWN + 48 * r, 16), 48)
                self.refs.stage.buf[q, 48 * r : 48 * r + 48, :] = (
                    product[0, rows, self.span] * grad_act[0:1, self.span]
                    + product[1, rows, self.span] * grad_act[1:2, self.span]
                ).astype(b16)

        def pieces(self, way, k):
            n = way * 3 + k
            return (
                (self.refs.stage.left if way else self.refs.stage.right).at[k],
                self.refs.stage.send.at[n],
                self.refs.stage.recv.at[n],
                near_x[way],
            )

        def send_half(self, q, half, way, k):
            send(self.refs.stage.buf.at[q, pl.ds(144 * half, 144)], *self.pieces(way, k))

        def wait_half(self, way, k):
            arrived(*self.pieces(way, k))

        def first(self):
            self.combine(self.q2)
            self.send_half(self.q2, 0, 0, 0)
            self.send_half(self.q2, 1, 1, 0)

        def second(self):
            self.combine(self.q1)
            self.send_half(self.q1, 1, 0, 1)
            self.combine(self.q3)
            self.send_half(self.q3, 0, 1, 1)

        def third(self):
            self.wait_half(0, 0)
            add_into(self.refs.stage.buf, self.q1, 0, 144, self.refs.stage.right.at[0])
            self.send_half(self.q1, 0, 0, 2)
            self.wait_half(1, 0)
            add_into(self.refs.stage.buf, self.q3, 144, 144, self.refs.stage.left.at[0])
            self.send_half(self.q3, 1, 1, 2)

        def finish_x(self):
            total = self.refs.sum
            for k in range(1, 3):
                self.wait_half(0, k)
                self.wait_half(1, k)
            for half in range(2):
                for r in range(0, 144, 48):
                    there = slice(144 * half + r, 144 * half + r + 48)
                    here = slice(r, r + 48)
                    total[there, :] = (
                        self.refs.stage.buf[x, there, :].astype(f32)
                        + self.refs.stage.right[2 - half, here, :].astype(f32)
                        + self.refs.stage.left[1 + half, here, :].astype(f32)
                    )
            total[OWN : OWN + 8, :] = jnp.zeros((8, self.width), f32)
            for k in range(NZ):
                both = [
                    total[h * (NZ * ROWS) + k * ROWS : h * (NZ * ROWS) + k * ROWS + 24, :]
                    for h in range(NH)
                ]
                self.refs.ring.buf[k] = jnp.concatenate(both, axis=0).astype(b16)

        def last_total(self):
            self.z.finish()
            return self.z.total(slice(0, PAIR))

    class GroupB(Group):
        def __init__(self, refs, begin, width, steps):
            super().__init__(refs, begin, width)
            self.z = Ring(refs.stage, z, NZ, near_z, steps)

        def pack(self):
            pack = self.refs.pack
            weight_0, weight_1 = grad_act[0:1, self.span], grad_act[1:2, self.span]
            for k in range(NZ):
                for g in range(NX * NH):
                    begin = g * (NZ * ROWS) + k * ROWS
                    source = slice(begin, begin + ROWS)
                    pack[g * ROWS : g * ROWS + ROWS, :] = (
                        product[0, source, self.span] * weight_0
                        + product[1, source, self.span] * weight_1
                    )
                self.refs.stage.buf[k] = pack[...].astype(b16)

        def finish_z(self):
            self.z.finish()
            total = self.refs.sum
            for r in range(0, 144, 48):
                total[r : r + 48, :] = self.z.total(slice(r, r + 48))
            total[144:152, :] = jnp.zeros((8, self.width), f32)
            for k in range(NX):
                both = [
                    total[(k * NH + h) * ROWS : (k * NH + h) * ROWS + 24, :] for h in range(NH)
                ]
                self.refs.ring.buf[k] = jnp.concatenate(both, axis=0).astype(b16)

        def send_x(self):
            refs = self.refs.ring
            for d in range(1, NX):
                source, sems = refs.buf.at[(x + d) % NX], (refs.send.at[d - 1], refs.recv.at[d - 1])
                send(source, refs.right.at[d - 1], *sems, at_x(d))

        def last_total(self):
            refs = self.refs.ring
            value = refs.buf[x].astype(f32)
            for d in range(1, NX):
                arrived(refs.right.at[d - 1], refs.send.at[d - 1], refs.recv.at[d - 1], at_x(d))
                value += refs.right[d - 1].astype(f32)
            return value

    a1 = GroupA(s.a[0], *GROUPS_A[0], (3, 4))
    a2 = GroupA(s.a[1], *GROUPS_A[1], (4, 3))
    b1 = GroupB(s.b[0], *GROUPS_B[0], (4, 3))
    b2 = GroupB(s.b[1], *GROUPS_B[1], (3, 4))

    pairs = Refs({})

    def pairs_1():
        halves = [buf[...].reshape(HALF, D) for buf in (s.pool_dense, s.pool_other)]
        lower = jnp.where(core == 0, halves[0], halves[1])
        upper = jnp.where(core == 0, halves[1], halves[0])
        all_pooled = jnp.concatenate([lower, upper], axis=0)
        block, weights, emb = block_gradient(all_pooled)
        pick = (iota((D, ROWS), 0) == iota((D, ROWS), 1) + dp * ROWS).astype(b16)
        pairs.columns = mm(block, pick).astype(b16)
        pairs.features = mm(s.text_dense[...].reshape(BATCH, D), pick).astype(b16)
        pairs.weights, pairs.emb = weights, emb

    def pairs_2():
        grad_text = mm_tn(pairs.weights, pairs.emb)
        unit = s.text_unit[...]
        along = jnp.sum(unit * grad_text, axis=1, keepdims=True)
        pairs.proj = ((grad_text - unit * along) / s.text_norm[:, 0:1]).astype(b16)

    def pairs_4():
        acts = [s.act_dense[:, r, :, 0:HID].reshape(HALF, HID) for r in range(2)]
        out_out[...] = mm_tn(pairs.columns, jnp.concatenate(acts, axis=0))
        out_text[...] = mm_tn(pairs.features, pairs.proj)
        chosen = (iota((2, BATCH), 1) == iota((2, BATCH), 0) * 16 + slot).astype(b16)
        own_text = mm(chosen, pairs.proj).astype(b16)
        out_texts[...] = mm_nt(own_text, w_text[...]).astype(b16)

    a1.first()
    a2.first()
    b1.pack()
    b1.z.step(1)
    a1.second()
    b2.pack()
    b2.z.step(1)
    a2.second()
    pool_gather.wait(0)
    pool_gather.start(1)
    a1.third()
    b1.z.step(2)
    a2.third()
    b2.z.step(2)
    a1.combine(x)
    a2.combine(x)
    b1.z.step(3)
    pool_gather.wait(1)
    pool_gather.make_dense()
    b2.z.step(3)
    a1.finish_x()
    a1.z.step(1)
    b1.z.step(4)
    a2.finish_x()
    a2.z.step(1)
    pool_gather.start(2)
    b2.z.step(4)
    a1.z.step(2)
    a2.z.step(2)
    b1.finish_z()
    b1.send_x()
    b2.finish_z()
    b2.send_x()
    a1.z.step(3)
    pool_gather.wait(2)
    pool_gather.start(3)
    a2.z.step(3)
    b1.send_pair()
    a1.z.step(4)
    b2.send_pair()
    a2.z.step(4)
    pool_gather.wait(3)
    core_sems = s.core.send.at[0], s.core.recv.at[0]
    send(s.pool_dense, s.pool_other, *core_sems, other)
    a1.send_pair()
    a2.send_pair()
    arrived(s.pool_other, *core_sems, other)
    pairs_1()
    pairs_2()
    pairs_4()
    for group in (b1, b2, a1, a2):
        group.result()
    for copy in sent:
        copy.wait_send()
    text_gather.drain(3)
    pool_gather.drain(4)

    def drain_tiles(t, carry):
        for k in range(3):
            tile_copy(k, t).wait_send()
        return carry

    lax.fori_loop(0, 2 * TILES, drain_tiles, 0)


def hand_on(*refs):
    for k in range(4):
        refs[4 + k][...] = refs[k][...]


def shards(images, ln_gain, w_in, b_in, w_out, texts, w_text, b_text, logit_scale, logit_bias):
    vmem = pl.BlockSpec(memory_space=pltpu.VMEM)
    smem = pl.BlockSpec(memory_space=pltpu.SMEM)
    hbm = pl.BlockSpec(memory_space=pl.ANY)
    dma = pltpu.SemaphoreType.DMA
    V = pltpu.VMEM
    def with_sems(count, **buffers):
        return dict(send=dma(count), recv=dma(count), **buffers)

    def ring(kind, shape, steps, width):
        return with_sems(
            (sum(steps),),
            buf=V(shape + (width,), kind),
            right=V((steps[0],) + shape[1:] + (width,), kind),
            left=V((steps[1],) + shape[1:] + (width,), kind),
        )

    def pair(width):
        return with_sems((1,), buf=V((NH, 24, width), f32), right=V((24, width), f32))

    refs = dict(
        w_in=V((HID, D), b16),
        w_pad=V((PADDED, D), b16),
        before=V((PADDED, TILE), f32),
        act_lanes=V((2, PADDED, 128), f32),
        w_out=V((HID, D), b16),
        w_text=V((D, D), b16),
        gain_col=V((D, 128), f32),
        bias_col=V((D, 128), f32),
        row_pad=V((1, D), f32),
        full=V((2 * TILES, NM, OWN, TILE), b16),
        normed=V((2 * TILES, D, TILE), b16),
        slopes=V((2 * TILES, PADDED, TILE), b16),
        act_sum=V((2, 8, D), f32),
        image_sum=V((2, 8, D), f32),
        product=V((2, D, D), f32),
        parts=V((NM, 2, D), f32),
        pool_other=V((NX, 16, D), f32),
        text_dense=V((NX, 2, 16, D), b16),
        pool_dense=V((NX, 16, D), f32),
        act_dense=V((NX, 2, 16, D), b16),
        text_emb=V((BATCH, D), b16),
        text_unit=V((BATCH, D), f32),
        text_norm=V((BATCH, 128), f32),
        grad_act=V((2, D), f32),
        load_sem=dma((8,)),
        images=V((2, OWN, PATCH), b16),
        own_texts=V((2, D), b16),
        gain_row=V((D,), f32),
        bias_in=V((HID,), f32),
        bias_text=V((D,), f32),
        img=with_sems((3, 2 * TILES)),
        part=with_sems((3,)),
        core=with_sems((1,)),
        texts=with_sems((11,), buf=V((NZ, NH, 2, D), f32)),
        pool=with_sems((16,), buf=V((NH, NZ, 4, D), b16)),
    )
    def group_a(width, steps):
        stage = with_sems(
            (6,),
            buf=V((NX, OWN, width), b16),
            right=V((3, 144, width), b16),
            left=V((3, 144, width), b16),
        )
        return dict(
            stage=stage,
            sum=V((OWN + 8, width), f32),
            ring=ring(b16, (NZ, PAIR), steps, width),
            pair=pair(width),
        )

    def group_b(width, steps):
        return dict(
            pack=V((144, width), f32),
            stage=ring(b16, (NZ, 144), steps, width),
            sum=V((152, width), f32),
            ring=with_sems(
                (NX - 1,), buf=V((NX, PAIR, width), b16), right=V((NX - 1, PAIR, width), b16)
            ),
            pair=pair(width),
        )

    refs.update(
        a=[group_a(GROUPS_A[0][1], (3, 4)), group_a(GROUPS_A[1][1], (4, 3))],
        b=[group_b(GROUPS_B[0][1], (4, 3)), group_b(GROUPS_B[1][1], (3, 4))],
    )
    out_shape = [
        jax.ShapeDtypeStruct((ROWS, HID), f32),
        jax.ShapeDtypeStruct((ROWS, HID), f32),
        jax.ShapeDtypeStruct((ROWS, D), f32),
        jax.ShapeDtypeStruct((2, D), b16),
    ]
    results = pl.pallas_call(
        kernel,
        out_shape=out_shape,
        in_specs=[hbm] * 5 + [smem] * 2 + [hbm] * 3,
        out_specs=[vmem] * 4,
        scratch_shapes=[refs],
        compiler_params=pltpu.CompilerParams(
            collective_id=0, has_side_effects=True, vmem_limit_bytes=58 << 20
        ),
    )(
        images.transpose(0, 2, 1),
        ln_gain,
        b_in,
        b_text,
        texts,
        logit_scale,
        logit_bias,
        w_in.T,
        w_out,
        w_text,
    )
    grad_in, grad_out, grad_text, grad_texts = pl.pallas_call(
        hand_on,
        out_shape=out_shape,
        in_specs=[vmem] * 4,
        out_specs=[vmem] * 4,
        compiler_params=pltpu.CompilerParams(vmem_limit_bytes=58 << 20),
    )(*results)
    return grad_in, grad_out.T, grad_text, grad_texts


def solution(mesh):
    placed = (
        P("dp", None, "mp"),
        P(),
        P(None, "mp"),
        P("mp"),
        P("mp", None),
        P("dp", None),
        P(),
        P(),
        P(),
        P(),
    )
    return jax.shard_map(
        shards,
        mesh=mesh,
        in_specs=placed,
        out_specs=(P("dp", "mp"), P("mp", "dp"), P("dp", None), P("dp", None)),
        check_vma=False,
    )
```

```python
import jax
import jax.numpy as jnp
from jax import lax
from jax.experimental import pallas as pl
from jax.experimental.pallas import tpu as pltpu
from jax.sharding import PartitionSpec as P

sqrt_two_pi = 0.7978845608028654
cubic_term = 0.044715
epsilon = 1e-06

NX, NH, NZ, NM = 4, 2, 8, 4
D = 1152
HID = 1076
PATCH = 729
OWN = D // 4
TILE = 256
TILES = 3
ROWS = 18
PAIR = 48
GROUPS_A = ((0, 384), (384, 256))
GROUPS_B = ((640, 256), (896, 256))
PADDED = 1088
BATCH = 128
HALF = 64

f32 = jnp.float32
b16 = jnp.bfloat16
MESH = pl.DeviceIdType.MESH


def mm(a, b):
    return lax.dot_general(a, b, (((1,), (0,)), ((), ())), preferred_element_type=f32)


def mm_nt(a, b):
    return lax.dot_general(a, b, (((1,), (1,)), ((), ())), preferred_element_type=f32)


def mm_tn(a, b):
    return lax.dot_general(a, b, (((0,), (0,)), ((), ())), preferred_element_type=f32)


class Refs:
    def __init__(self, values):
        for name, value in values.items():
            if isinstance(value, (tuple, list)):
                value = [Refs(part) for part in value]
            setattr(self, name, Refs(value) if isinstance(value, dict) else value)


def iota(shape, axis):
    return lax.broadcasted_iota(jnp.int32, shape, axis)


def three_parts(values):
    high = values.astype(b16)
    rest = values - high.astype(f32)
    middle = rest.astype(b16)
    low = (rest - middle.astype(f32)).astype(b16)
    return high, middle, low


def gelu_and_slope(values):
    squared = values * values
    tanh_part = jnp.tanh(values * (sqrt_two_pi + (sqrt_two_pi * cubic_term) * squared))
    half = 0.5 + 0.5 * tanh_part
    bend = (1.0 - tanh_part * tanh_part) * (
        0.5 * sqrt_two_pi + (1.5 * sqrt_two_pi * cubic_term) * squared
    )
    return values * half, half + values * bend


def kernel(
    images_hbm,
    gain_hbm,
    bias_hbm,
    shift_hbm,
    texts_hbm,
    scale_ref,
    shift_ref,
    w_in_hbm,
    w_out_hbm,
    w_text_hbm,
    out_in,
    out_out,
    out_text,
    out_texts,
    s,
):
    s = Refs(s)
    w_in, w_pad, w_out, w_text = s.w_in, s.w_pad, s.w_out, s.w_text
    images, texts = s.images, s.own_texts
    gain_row, bias_in, bias_text = s.gain_row, s.bias_in, s.bias_text
    full, normed, slopes, product = s.full, s.normed, s.slopes, s.product
    act_sum, image_sum, grad_act, parts = s.act_sum, s.image_sum, s.grad_act, s.parts
    act_lanes, before = s.act_lanes, s.before

    dp = lax.axis_index("dp")
    mp = lax.axis_index("mp")
    x = dp // (NH * NZ)
    yh = (dp // NZ) % NH
    z = dp % NZ
    slot = x * 32 + z * NH + yh
    yl = mp // 2
    core = mp % 2
    mp_chip = (1 - yl) * 2 + core
    mp_core = yl * 2 + (1 - core)
    mp_far = (1 - yl) * 2 + (1 - core)
    chip, other, far = (dp, mp_chip), (dp, mp_core), (dp, mp_far)

    def at_z(d):
        return ((x * NH + yh) * NZ + (z + d) % NZ, mp)

    def at_x(d):
        return ((((x + d) % NX) * NH + yh) * NZ + z, mp)

    def at_yh():
        return ((x * NH + (1 - yh)) * NZ + z, mp)

    def remote(src, dst, send_sem, recv_sem, device):
        return pltpu.make_async_remote_copy(
            src_ref=src,
            dst_ref=dst,
            send_sem=send_sem,
            recv_sem=recv_sem,
            device_id=device,
            device_id_type=MESH,
        )

    sent = []

    def send(src, dst, send_sem, recv_sem, device):
        copy = remote(src, dst, send_sem, recv_sem, device)
        copy.start()
        sent.append(copy)

    def arrived(dst, send_sem, recv_sem, device):
        remote(dst, dst, send_sem, recv_sem, device).wait_recv()

    sources = (w_in_hbm, w_out_hbm, w_text_hbm, images_hbm, texts_hbm, gain_hbm, bias_hbm, shift_hbm)
    targets = (w_in, w_out, w_text, images, texts, gain_row, bias_in, bias_text)
    loads = [
        pltpu.make_async_copy(source, target, s.load_sem.at[k])
        for k, (source, target) in enumerate(zip(sources, targets))
    ]
    for k in (3, 4, 5, 6, 0):
        loads[k].start()

    barrier = pltpu.get_barrier_semaphore()
    partners = [chip, other, far, at_yh()]
    partners += [at_z(d) for d in range(1, NZ)] + [at_x(d) for d in range(1, NX)]
    for partner in partners:
        pl.semaphore_signal(barrier, inc=1, device_id=partner, device_id_type=MESH)

    loads[3].wait()
    for i in range(2):
        for j in range(TILES):
            begin = j * TILE
            width = min(TILE, PATCH - begin)
            if width < TILE:
                full[i * TILES + j, mp] = jnp.zeros((OWN, TILE), b16)
            full[i * TILES + j, mp, :, 0:width] = images[i, :, begin : begin + width]
    loads[4].wait()
    s.texts.buf[z, yh] = texts[...].astype(f32)

    pl.semaphore_wait(barrier, len(partners))

    class Gather:
        def __init__(self, refs):
            self.buf, self.send_sem, self.recv_sem = refs.buf, refs.send, refs.recv

        def start(self, stage):
            for n, own, _, device in self.copies(stage):
                remote(own, own, self.send_sem.at[n], self.recv_sem.at[n], device).start()

        def wait(self, stage):
            for n, _, landed, device in self.copies(stage):
                arrived(landed, self.send_sem.at[n], self.recv_sem.at[n], device)

        def drain(self, stages):
            for stage in range(stages):
                for n, own, _, device in self.copies(stage):
                    remote(own, own, self.send_sem.at[n], self.recv_sem.at[n], device).wait_send()

    class TextGather(Gather):
        def copies(self, stage):
            at, dense = self.buf.at, s.text_dense.at
            if stage == 0:
                return [(0, at[z, yh], at[z, 1 - yh], at_yh())]
            if stage == 1:
                return [(d, at[z], at[(z + NZ - d) % NZ], at_z(d)) for d in range(1, NZ)]
            return [(7 + d, dense[x], dense[(x + NX - d) % NX], at_x(d)) for d in range(1, NX)]

        def make_dense(self):
            for r in range(2):
                s.text_dense[x, r] = self.buf[:, :, r, :].reshape(NZ * NH, D).astype(b16)

    class PoolGather(Gather):
        def copies(self, stage):
            at, pool, acts = self.buf.at, s.pool_dense.at, s.act_dense.at
            if stage == 0:
                return [(d, at[yh, z], at[yh, (z + NZ - d) % NZ], at_z(d)) for d in range(1, NZ)]
            if stage == 1:
                return [(0, at[yh], at[1 - yh], at_yh())]
            before, after, far = (x + NX - 1) % NX, (x + 1) % NX, (x + 2) % NX
            right, left = at_x(1), at_x(NX - 1)
            if stage == 2:
                return [
                    (8, pool[x], pool[before], right),
                    (9, pool[x], pool[after], left),
                    (10, acts[x], acts[before], right),
                    (11, acts[x], acts[after], left),
                ]
            lower, upper = pl.ds(0, 8), pl.ds(8, 8)
            return [
                (12, pool[before, lower], pool[far, lower], right),
                (13, pool[after, upper], pool[far, upper], left),
                (14, acts[before, 0], acts[far, 0], right),
                (15, acts[after, 1], acts[far, 1], left),
            ]

        def make_dense(self):
            rows = [self.buf[:, :, k, :].reshape(NH * NZ, D) for k in range(4)]
            s.pool_dense[x] = rows[0].astype(f32) + rows[1].astype(f32)
            s.act_dense[x, 0] = rows[2]
            s.act_dense[x, 1] = rows[3]

    def tile_copy(k, t):
        source = full.at[t, mp_chip if k == 2 else mp]
        return remote(source, source, s.img.send.at[k, t], s.img.recv.at[k, t], chip if k == 0 else other)

    for k in (2, 7, 1):
        loads[k].start()
    text_gather = TextGather(s.texts)
    tile_copy(0, 0).start()
    tile_copy(1, 0).start()
    text_gather.start(0)

    product[:, :, PADDED:D] = jnp.zeros((2, D, D - PADDED), f32)
    act_lanes[...] = jnp.zeros_like(act_lanes)
    act_sum[...] = jnp.zeros_like(act_sum)
    image_sum[...] = jnp.zeros_like(image_sum)
    grad_act[...] = jnp.zeros_like(grad_act)
    loads[5].wait()
    loads[6].wait()
    tile_copy(0, 1).start()
    tile_copy(1, 1).start()
    diagonal = iota((128, 128), 0) == iota((128, 128), 1)
    row_pad = s.row_pad
    for row, column, width in ((gain_row, s.gain_col, D), (bias_in, s.bias_col, HID)):
        row_pad[...] = jnp.zeros_like(row_pad)
        row_pad[:, 0:width] = row[...].reshape(1, width)
        for k in range(D // 128):
            span = slice(128 * k, 128 * k + 128)
            picked = jnp.sum(jnp.where(diagonal, row_pad[:, span], 0.0), axis=1, keepdims=True)
            column[span, :] = jnp.broadcast_to(picked, (128, 128))
    whole = HID // TILE * TILE
    chunks = [(begin, TILE) for begin in range(0, whole, TILE)] + [(whole, PADDED - whole)]
    loads[0].wait()
    tail = (iota((PADDED - whole, HID - whole), 0) == iota((PADDED - whole, HID - whole), 1)).astype(
        b16
    )
    w_pad[0:whole, :] = w_in[0:whole, :]
    w_pad[whole:PADDED, :] = mm(tail, w_in[whole:HID, :]).astype(b16)

    def add_product(t, first):
        i = t // TILES
        for begin, width in chunks:
            span = slice(begin, begin + width)
            term = mm_nt(normed[t], slopes[t, span, :])
            product[i, :, span] = term if first else product[i, :, span] + term

    def pass_on(t):
        arrived(full.at[t, mp_chip], s.img.send.at[0, t], s.img.recv.at[0, t], chip)
        tile_copy(2, t).start()

    def work_on(t):
        i = t // TILES
        j = t % TILES
        for h in range(TILE // 128):
            lanes = slice(128 * h, 128 * h + 128)
            total = jnp.zeros((1, 128), f32)
            for m in range(NM):
                total += jnp.sum(full[t, m, :, lanes].astype(f32), axis=0, keepdims=True)
            mean = total * (1.0 / D)
            total = jnp.zeros((1, 128), f32)
            for m in range(NM):
                centered = full[t, m, :, lanes].astype(f32) - mean
                total += jnp.sum(centered * centered, axis=0, keepdims=True)
            factor = lax.rsqrt(total * (1.0 / D) + epsilon)
            for m in range(NM):
                rows = slice(OWN * m, OWN * m + OWN)
                centered = full[t, m, :, lanes].astype(f32) - mean
                normed[t, rows, lanes] = (centered * factor * s.gain_col[rows, :]).astype(b16)
        image_sum[i] += mm_nt(jnp.ones((8, TILE), b16), full[t].reshape(D, TILE))
        before[...] = mm(w_pad[...], normed[t])

        @pl.when(t < 2 * TILES - 1)
        def _():
            pass_on(t + 1)

        @pl.when(t < 2 * TILES - 3)
        def _():
            tile_copy(0, t + 3).start()
            tile_copy(1, t + 3).start()

        valid = (iota((1, 128), 1) + (j * TILE + 128) < PATCH).astype(f32)
        for begin, width in chunks:
            span = slice(begin, begin + width)
            bias = s.bias_col[span, :]
            act, slope = gelu_and_slope(before[span, :] + jnp.concatenate([bias, bias], axis=1))
            slopes[t, span, :] = slope.astype(b16)
            act_lanes[i, span, :] += act[:, 0:128] + act[:, 128:TILE] * valid

    def project_texts():
        loads[2].wait()
        loads[7].wait()
        projected = mm(s.text_dense[...].reshape(BATCH, D), w_text[...]) + bias_text[...].reshape(1, D)
        norm = jnp.sqrt(jnp.sum(projected * projected, axis=1, keepdims=True) + epsilon)
        unit = projected / norm
        s.text_norm[...] = jnp.broadcast_to(norm, (BATCH, 128))
        s.text_unit[...] = unit
        s.text_emb[...] = unit.astype(b16)

    def tile_step(t, carry):
        @pl.when((t > 0) & (t % TILES == 1))
        def _():
            add_product(t - 1, True)

        @pl.when((t > 0) & (t % TILES != 1))
        def _():
            add_product(t - 1, False)

        @pl.when(t == 0)
        def _():
            text_gather.wait(0)
            text_gather.start(1)

        @pl.when(t == 2)
        def _():
            text_gather.wait(1)
            text_gather.make_dense()
            text_gather.start(2)

        @pl.when(t == 4)
        def _():
            text_gather.wait(2)
            project_texts()

        arrived(full.at[t, mp_core], s.img.send.at[1, t], s.img.recv.at[1, t], other)
        arrived(full.at[t, mp_far], s.img.send.at[2, t], s.img.recv.at[2, t], other)
        work_on(t)
        return carry

    pass_on(0)
    tile_copy(0, 2).start()
    tile_copy(1, 2).start()
    lax.fori_loop(0, 2 * TILES, tile_step, 0)

    loads[1].wait()
    ones = jnp.ones((8, 128), b16)
    for i in range(2):
        high, middle, _ = three_parts(act_lanes[i])
        act_sum[i, :, 0:PADDED] = mm_nt(ones, high) + mm_nt(ones, middle)
    row = iota((8, HID), 0)
    split = three_parts(act_sum[0, :, 0:HID]) + three_parts(act_sum[1, :, 0:HID])
    stacked = jnp.zeros((8, HID), f32)
    for k in range(6):
        stacked = jnp.where(row == k, split[k].astype(f32), stacked)
    shares = mm(stacked.astype(b16), w_out[...])
    row = iota((8, D), 0)
    share_0 = jnp.sum(jnp.where(row < 3, shares, 0.0), axis=0, keepdims=True)
    share_1 = jnp.sum(jnp.where((row >= 3) & (row < 6), shares, 0.0), axis=0, keepdims=True)
    first = iota((2, D), 0) == 0
    parts[mp] = jnp.where(first, share_0, share_1)
    group = (chip, other, far)
    for k, partner in enumerate(group):
        own = parts.at[mp]
        send(own, own, s.part.send.at[k], s.part.recv.at[k], partner)
    add_product(2 * TILES - 1, False)
    for k, source in enumerate((mp_chip, mp_core, mp_far)):
        arrived(parts.at[source], s.part.send.at[k], s.part.recv.at[k], group[k])
    block = parts[0] + parts[1] + parts[2] + parts[3]
    pooled = (jnp.where(first, image_sum[0, 0:2, :], image_sum[1, 0:2, :]) + block) * (1.0 / PATCH)
    pool_gather = PoolGather(s.pool)
    mine = jnp.where(core == 0, pooled[0:1, :], pooled[1:2, :])
    pooled_high = mine.astype(b16)
    pooled_rest = (mine - pooled_high.astype(f32)).astype(b16)
    rows = (pooled_high.astype(f32), pooled_rest.astype(f32), act_sum[0, 0:1, :], act_sum[1, 0:1, :])
    order = iota((4, D), 0)
    packed = jnp.broadcast_to(rows[0], (4, D))
    for k in range(1, 4):
        packed = jnp.where(order == k, rows[k], packed)
    s.pool.buf[yh, z] = packed.astype(b16)
    pool_gather.start(0)

    scale = scale_ref[0]
    shift = shift_ref[0]

    def block_gradient(values):
        norm = jnp.sqrt(jnp.sum(values * values, axis=1, keepdims=True) + epsilon)
        unit = values / norm
        emb = unit.astype(b16)
        logits = scale * mm_nt(emb, s.text_emb[...]) + shift
        if values.shape[0] == 2:
            matches = iota((2, BATCH), 1) == iota((2, BATCH), 0) * 16 + slot
        else:
            at = iota((BATCH, BATCH), 0)
            text = (((at >> 4) & 3) << 5) + ((at >> 6) << 4) + ((at & 7) << 1) + ((at >> 3) & 1)
            matches = text == iota((BATCH, BATCH), 1)
        signs = jnp.where(matches, 1.0, -1.0)
        coef = -signs * jax.nn.sigmoid(-signs * logits)
        weights = (scale * coef).astype(b16)
        grad_emb = mm(weights, s.text_emb[...])
        along = jnp.sum(unit * grad_emb, axis=1, keepdims=True)
        grad_pooled = (grad_emb - unit * along) / norm
        return (grad_pooled * (1.0 / PATCH)).astype(b16), weights, emb

    own_block, _, _ = block_gradient(pooled)
    grad_act[:, 0:HID] = mm_nt(own_block, w_out[...])

    near_z = (at_z(1), at_z(NZ - 1))
    near_x = (at_x(1), at_x(NX - 1))

    def add_into(target, index, begin, count, received):
        for r in range(0, count, 48):
            there = slice(begin + r, begin + r + 48)
            target[index, there, :] = (
                target[index, there, :].astype(f32) + received[r : r + 48, :].astype(f32)
            ).astype(b16)

    class Ring:
        def __init__(self, refs, place, size, near, steps):
            self.buf = refs.buf
            self.recv = refs.right, refs.left
            self.sems = refs.send, refs.recv
            self.place, self.size, self.near, self.steps = place, size, near, steps

        def wait(self, way, k):
            n = way * self.steps[0] + k - 1
            there = self.recv[way].at[k - 1]
            arrived(there, self.sems[0].at[n], self.sems[1].at[n], self.near[way])
            return there

        def step(self, k):
            for way in range(2):
                if k > self.steps[way]:
                    continue
                away = self.steps[way] + 1 - k
                chunk = (self.place + (self.size - away if way else away)) % self.size
                if k > 1:
                    add_into(self.buf, chunk, 0, self.buf.shape[1], self.wait(way, k - 1))
                n = way * self.steps[0] + k - 1
                send(
                    self.buf.at[chunk],
                    self.recv[way].at[k - 1],
                    self.sems[0].at[n],
                    self.sems[1].at[n],
                    self.near[way],
                )

        def finish(self):
            for way in range(2):
                self.wait(way, self.steps[way])

        def total(self, rows):
            value = self.buf[self.place, rows, :].astype(f32)
            for way in range(2):
                value += self.recv[way][self.steps[way] - 1, rows, :].astype(f32)
            return value

    class Group:
        def __init__(self, refs, begin, width):
            self.refs, self.begin, self.width = refs, begin, width
            self.span = slice(begin, begin + width)

        def send_pair(self):
            value = self.last_total()
            for h in range(NH):
                self.refs.pair.buf[h] = value[24 * h : 24 * h + 24, :]
            sems = self.refs.pair.send.at[0], self.refs.pair.recv.at[0]
            send(self.refs.pair.buf.at[1 - yh], self.refs.pair.right, *sems, at_yh())

        def result(self):
            sems = self.refs.pair.send.at[0], self.refs.pair.recv.at[0]
            arrived(self.refs.pair.right, *sems, at_yh())
            width = min(self.width, HID - self.begin)
            value = self.refs.pair.buf[yh] + self.refs.pair.right[...]
            out_in[:, self.begin : self.begin + width] = value[0:ROWS, 0:width]

    class GroupA(Group):
        def __init__(self, refs, begin, width, steps):
            super().__init__(refs, begin, width)
            self.z = Ring(refs.ring, z, NZ, near_z, steps)
            self.q1, self.q2, self.q3 = (x + 1) % NX, (x + 2) % NX, (x + 3) % NX

        def combine(self, q):
            for r in range(OWN // 48):
                rows = pl.ds(pl.multiple_of(q * OWN + 48 * r, 16), 48)
                self.refs.stage.buf[q, 48 * r : 48 * r + 48, :] = (
                    product[0, rows, self.span] * grad_act[0:1, self.span]
                    + product[1, rows, self.span] * grad_act[1:2, self.span]
                ).astype(b16)

        def pieces(self, way, k):
            n = way * 3 + k
            return (
                (self.refs.stage.left if way else self.refs.stage.right).at[k],
                self.refs.stage.send.at[n],
                self.refs.stage.recv.at[n],
                near_x[way],
            )

        def send_half(self, q, half, way, k):
            send(self.refs.stage.buf.at[q, pl.ds(144 * half, 144)], *self.pieces(way, k))

        def wait_half(self, way, k):
            arrived(*self.pieces(way, k))

        def first(self):
            self.combine(self.q2)
            self.send_half(self.q2, 0, 0, 0)
            self.send_half(self.q2, 1, 1, 0)

        def second(self):
            self.combine(self.q1)
            self.send_half(self.q1, 1, 0, 1)
            self.combine(self.q3)
            self.send_half(self.q3, 0, 1, 1)

        def third(self):
            self.wait_half(0, 0)
            add_into(self.refs.stage.buf, self.q1, 0, 144, self.refs.stage.right.at[0])
            self.send_half(self.q1, 0, 0, 2)
            self.wait_half(1, 0)
            add_into(self.refs.stage.buf, self.q3, 144, 144, self.refs.stage.left.at[0])
            self.send_half(self.q3, 1, 1, 2)

        def finish_x(self):
            total = self.refs.sum
            for k in range(1, 3):
                self.wait_half(0, k)
                self.wait_half(1, k)
            for half in range(2):
                for r in range(0, 144, 48):
                    there = slice(144 * half + r, 144 * half + r + 48)
                    here = slice(r, r + 48)
                    total[there, :] = (
                        self.refs.stage.buf[x, there, :].astype(f32)
                        + self.refs.stage.right[2 - half, here, :].astype(f32)
                        + self.refs.stage.left[1 + half, here, :].astype(f32)
                    )
            total[OWN : OWN + 8, :] = jnp.zeros((8, self.width), f32)
            for k in range(NZ):
                both = [
                    total[h * (NZ * ROWS) + k * ROWS : h * (NZ * ROWS) + k * ROWS + 24, :]
                    for h in range(NH)
                ]
                self.refs.ring.buf[k] = jnp.concatenate(both, axis=0).astype(b16)

        def last_total(self):
            self.z.finish()
            return self.z.total(slice(0, PAIR))

    class GroupB(Group):
        def __init__(self, refs, begin, width, steps):
            super().__init__(refs, begin, width)
            self.z = Ring(refs.stage, z, NZ, near_z, steps)

        def pack(self):
            pack = self.refs.pack
            weight_0, weight_1 = grad_act[0:1, self.span], grad_act[1:2, self.span]
            for k in range(NZ):
                for g in range(NX * NH):
                    begin = g * (NZ * ROWS) + k * ROWS
                    source = slice(begin, begin + ROWS)
                    pack[g * ROWS : g * ROWS + ROWS, :] = (
                        product[0, source, self.span] * weight_0
                        + product[1, source, self.span] * weight_1
                    )
                self.refs.stage.buf[k] = pack[...].astype(b16)

        def finish_z(self):
            self.z.finish()
            total = self.refs.sum
            for r in range(0, 144, 48):
                total[r : r + 48, :] = self.z.total(slice(r, r + 48))
            total[144:152, :] = jnp.zeros((8, self.width), f32)
            for k in range(NX):
                both = [
                    total[(k * NH + h) * ROWS : (k * NH + h) * ROWS + 24, :] for h in range(NH)
                ]
                self.refs.ring.buf[k] = jnp.concatenate(both, axis=0).astype(b16)

        def send_x(self):
            refs = self.refs.ring
            for d in range(1, NX):
                source, sems = refs.buf.at[(x + d) % NX], (refs.send.at[d - 1], refs.recv.at[d - 1])
                send(source, refs.right.at[d - 1], *sems, at_x(d))

        def last_total(self):
            refs = self.refs.ring
            value = refs.buf[x].astype(f32)
            for d in range(1, NX):
                arrived(refs.right.at[d - 1], refs.send.at[d - 1], refs.recv.at[d - 1], at_x(d))
                value += refs.right[d - 1].astype(f32)
            return value

    a1 = GroupA(s.a[0], *GROUPS_A[0], (3, 4))
    a2 = GroupA(s.a[1], *GROUPS_A[1], (4, 3))
    b1 = GroupB(s.b[0], *GROUPS_B[0], (4, 3))
    b2 = GroupB(s.b[1], *GROUPS_B[1], (3, 4))

    pairs = Refs({})

    def pairs_1():
        halves = [buf[...].reshape(HALF, D) for buf in (s.pool_dense, s.pool_other)]
        lower = jnp.where(core == 0, halves[0], halves[1])
        upper = jnp.where(core == 0, halves[1], halves[0])
        all_pooled = jnp.concatenate([lower, upper], axis=0)
        block, weights, emb = block_gradient(all_pooled)
        pick = (iota((D, ROWS), 0) == iota((D, ROWS), 1) + dp * ROWS).astype(b16)
        pairs.columns = mm(block, pick).astype(b16)
        pairs.features = mm(s.text_dense[...].reshape(BATCH, D), pick).astype(b16)
        pairs.weights, pairs.emb = weights, emb

    def pairs_2():
        grad_text = mm_tn(pairs.weights, pairs.emb)
        unit = s.text_unit[...]
        along = jnp.sum(unit * grad_text, axis=1, keepdims=True)
        pairs.proj = ((grad_text - unit * along) / s.text_norm[:, 0:1]).astype(b16)

    def pairs_4():
        acts = [s.act_dense[:, r, :, 0:HID].reshape(HALF, HID) for r in range(2)]
        out_out[...] = mm_tn(pairs.columns, jnp.concatenate(acts, axis=0))
        out_text[...] = mm_tn(pairs.features, pairs.proj)
        chosen = (iota((2, BATCH), 1) == iota((2, BATCH), 0) * 16 + slot).astype(b16)
        own_text = mm(chosen, pairs.proj).astype(b16)
        out_texts[...] = mm_nt(own_text, w_text[...]).astype(b16)

    a1.first()
    a2.first()
    b1.pack()
    b1.z.step(1)
    a1.second()
    b2.pack()
    b2.z.step(1)
    a2.second()
    pool_gather.wait(0)
    pool_gather.start(1)
    a1.third()
    b1.z.step(2)
    a2.third()
    b2.z.step(2)
    a1.combine(x)
    a2.combine(x)
    b1.z.step(3)
    pool_gather.wait(1)
    pool_gather.make_dense()
    b2.z.step(3)
    a1.finish_x()
    a1.z.step(1)
    b1.z.step(4)
    a2.finish_x()
    a2.z.step(1)
    pool_gather.start(2)
    b2.z.step(4)
    a1.z.step(2)
    a2.z.step(2)
    b1.finish_z()
    b1.send_x()
    b2.finish_z()
    b2.send_x()
    a1.z.step(3)
    pool_gather.wait(2)
    pool_gather.start(3)
    a2.z.step(3)
    b1.send_pair()
    a1.z.step(4)
    b2.send_pair()
    a2.z.step(4)
    pool_gather.wait(3)
    core_sems = s.core.send.at[0], s.core.recv.at[0]
    send(s.pool_dense, s.pool_other, *core_sems, other)
    a1.send_pair()
    a2.send_pair()
    arrived(s.pool_other, *core_sems, other)
    pairs_1()
    pairs_2()
    pairs_4()
    for group in (b1, b2, a1, a2):
        group.result()
    for copy in sent:
        copy.wait_send()
    text_gather.drain(3)
    pool_gather.drain(4)

    def drain_tiles(t, carry):
        for k in range(3):
            tile_copy(k, t).wait_send()
        return carry

    lax.fori_loop(0, 2 * TILES, drain_tiles, 0)


def hand_on(*refs):
    for k in range(4):
        refs[4 + k][...] = refs[k][...]


def shards(images, ln_gain, w_in, b_in, w_out, texts, w_text, b_text, logit_scale, logit_bias):
    vmem = pl.BlockSpec(memory_space=pltpu.VMEM)
    smem = pl.BlockSpec(memory_space=pltpu.SMEM)
    hbm = pl.BlockSpec(memory_space=pl.ANY)
    dma = pltpu.SemaphoreType.DMA
    V = pltpu.VMEM
    def with_sems(count, **buffers):
        return dict(send=dma(count), recv=dma(count), **buffers)

    def ring(kind, shape, steps, width):
        return with_sems(
            (sum(steps),),
            buf=V(shape + (width,), kind),
            right=V((steps[0],) + shape[1:] + (width,), kind),
            left=V((steps[1],) + shape[1:] + (width,), kind),
        )

    def pair(width):
        return with_sems((1,), buf=V((NH, 24, width), f32), right=V((24, width), f32))

    refs = dict(
        w_in=V((HID, D), b16),
        w_pad=V((PADDED, D), b16),
        before=V((PADDED, TILE), f32),
        act_lanes=V((2, PADDED, 128), f32),
        w_out=V((HID, D), b16),
        w_text=V((D, D), b16),
        gain_col=V((D, 128), f32),
        bias_col=V((D, 128), f32),
        row_pad=V((1, D), f32),
        full=V((2 * TILES, NM, OWN, TILE), b16),
        normed=V((2 * TILES, D, TILE), b16),
        slopes=V((2 * TILES, PADDED, TILE), b16),
        act_sum=V((2, 8, D), f32),
        image_sum=V((2, 8, D), f32),
        product=V((2, D, D), f32),
        parts=V((NM, 2, D), f32),
        pool_other=V((NX, 16, D), f32),
        text_dense=V((NX, 2, 16, D), b16),
        pool_dense=V((NX, 16, D), f32),
        act_dense=V((NX, 2, 16, D), b16),
        text_emb=V((BATCH, D), b16),
        text_unit=V((BATCH, D), f32),
        text_norm=V((BATCH, 128), f32),
        grad_act=V((2, D), f32),
        load_sem=dma((8,)),
        images=V((2, OWN, PATCH), b16),
        own_texts=V((2, D), b16),
        gain_row=V((D,), f32),
        bias_in=V((HID,), f32),
        bias_text=V((D,), f32),
        img=with_sems((3, 2 * TILES)),
        part=with_sems((3,)),
        core=with_sems((1,)),
        texts=with_sems((11,), buf=V((NZ, NH, 2, D), f32)),
        pool=with_sems((16,), buf=V((NH, NZ, 4, D), b16)),
    )
    def group_a(width, steps):
        stage = with_sems(
            (6,),
            buf=V((NX, OWN, width), b16),
            right=V((3, 144, width), b16),
            left=V((3, 144, width), b16),
        )
        return dict(
            stage=stage,
            sum=V((OWN + 8, width), f32),
            ring=ring(b16, (NZ, PAIR), steps, width),
            pair=pair(width),
        )

    def group_b(width, steps):
        return dict(
            pack=V((144, width), f32),
            stage=ring(b16, (NZ, 144), steps, width),
            sum=V((152, width), f32),
            ring=with_sems(
                (NX - 1,), buf=V((NX, PAIR, width), b16), right=V((NX - 1, PAIR, width), b16)
            ),
            pair=pair(width),
        )

    refs.update(
        a=[group_a(GROUPS_A[0][1], (3, 4)), group_a(GROUPS_A[1][1], (4, 3))],
        b=[group_b(GROUPS_B[0][1], (4, 3)), group_b(GROUPS_B[1][1], (3, 4))],
    )
    out_shape = [
        jax.ShapeDtypeStruct((ROWS, HID), f32),
        jax.ShapeDtypeStruct((ROWS, HID), f32),
        jax.ShapeDtypeStruct((ROWS, D), f32),
        jax.ShapeDtypeStruct((2, D), b16),
    ]
    results = pl.pallas_call(
        kernel,
        out_shape=[V(shape.shape, shape.dtype) for shape in out_shape],
        in_specs=[hbm] * 5 + [smem] * 2 + [hbm] * 3,
        out_specs=[vmem] * 4,
        scratch_shapes=[refs],
        compiler_params=pltpu.CompilerParams(
            collective_id=0, has_side_effects=True, vmem_limit_bytes=58 << 20
        ),
    )(
        images.transpose(0, 2, 1),
        ln_gain,
        b_in,
        b_text,
        texts,
        logit_scale,
        logit_bias,
        w_in.T,
        w_out,
        w_text,
    )
    grad_in, grad_out, grad_text, grad_texts = pl.pallas_call(
        hand_on,
        out_shape=out_shape,
        in_specs=[vmem] * 4,
        out_specs=[vmem] * 4,
        compiler_params=pltpu.CompilerParams(vmem_limit_bytes=4 << 20),
    )(*results)
    return grad_in, grad_out.T, grad_text, grad_texts


def solution(mesh):
    placed = (
        P("dp", None, "mp"),
        P(),
        P(None, "mp"),
        P("mp"),
        P("mp", None),
        P("dp", None),
        P(),
        P(),
        P(),
        P(),
    )
    return jax.shard_map(
        shards,
        mesh=mesh,
        in_specs=placed,
        out_specs=(P("dp", "mp"), P("mp", "dp"), P("dp", None), P("dp", None)),
        check_vma=False,
    )
```

```python
import jax
import jax.numpy as jnp
from jax import lax
from jax.experimental import pallas as pl
from jax.experimental.pallas import tpu as pltpu
from jax.sharding import PartitionSpec as P

sqrt_two_pi = 0.7978845608028654
cubic_term = 0.044715
epsilon = 1e-06

NX, NH, NZ, NM = 4, 2, 8, 4
D = 1152
HID = 1076
PATCH = 729
OWN = D // 4
TILE = 256
TILES = 3
ROWS = 18
PAIR = 48
GROUPS_A = ((0, 256), (256, 256))
GROUPS_B = ((512, 384), (896, 256))
PADDED = 1088
BATCH = 128
HALF = 64

f32 = jnp.float32
b16 = jnp.bfloat16
MESH = pl.DeviceIdType.MESH


def mm(a, b):
    return lax.dot_general(a, b, (((1,), (0,)), ((), ())), preferred_element_type=f32)


def mm_nt(a, b):
    return lax.dot_general(a, b, (((1,), (1,)), ((), ())), preferred_element_type=f32)


def mm_tn(a, b):
    return lax.dot_general(a, b, (((0,), (0,)), ((), ())), preferred_element_type=f32)


class Refs:
    def __init__(self, values):
        for name, value in values.items():
            if isinstance(value, (tuple, list)):
                value = [Refs(part) for part in value]
            setattr(self, name, Refs(value) if isinstance(value, dict) else value)


def iota(shape, axis):
    return lax.broadcasted_iota(jnp.int32, shape, axis)


def three_parts(values):
    high = values.astype(b16)
    rest = values - high.astype(f32)
    middle = rest.astype(b16)
    low = (rest - middle.astype(f32)).astype(b16)
    return high, middle, low


def gelu_and_slope(values):
    squared = values * values
    tanh_part = jnp.tanh(values * (sqrt_two_pi + (sqrt_two_pi * cubic_term) * squared))
    half = 0.5 + 0.5 * tanh_part
    bend = (1.0 - tanh_part * tanh_part) * (
        0.5 * sqrt_two_pi + (1.5 * sqrt_two_pi * cubic_term) * squared
    )
    return values * half, half + values * bend


def kernel(
    images_hbm,
    gain_hbm,
    bias_hbm,
    shift_hbm,
    texts_hbm,
    scale_ref,
    shift_ref,
    w_in_hbm,
    w_out_hbm,
    w_text_hbm,
    out_in,
    out_out,
    out_text,
    out_texts,
    s,
):
    s = Refs(s)
    w_in, w_pad, w_out, w_text = s.w_in, s.w_pad, s.w_out, s.w_text
    images, texts = s.images, s.own_texts
    gain_row, bias_in, bias_text = s.gain_row, s.bias_in, s.bias_text
    full, normed, slopes, product = s.full, s.normed, s.slopes, s.product
    act_sum, image_sum, grad_act, parts = s.act_sum, s.image_sum, s.grad_act, s.parts
    act_lanes, before = s.act_lanes, s.before

    dp = lax.axis_index("dp")
    mp = lax.axis_index("mp")
    x = dp // (NH * NZ)
    yh = (dp // NZ) % NH
    z = dp % NZ
    slot = x * 32 + z * NH + yh
    yl = mp // 2
    core = mp % 2
    mp_chip = (1 - yl) * 2 + core
    mp_core = yl * 2 + (1 - core)
    mp_far = (1 - yl) * 2 + (1 - core)
    chip, other, far = (dp, mp_chip), (dp, mp_core), (dp, mp_far)

    def at_z(d):
        return ((x * NH + yh) * NZ + (z + d) % NZ, mp)

    def at_x(d):
        return ((((x + d) % NX) * NH + yh) * NZ + z, mp)

    def at_yh():
        return ((x * NH + (1 - yh)) * NZ + z, mp)

    def remote(src, dst, send_sem, recv_sem, device):
        return pltpu.make_async_remote_copy(
            src_ref=src,
            dst_ref=dst,
            send_sem=send_sem,
            recv_sem=recv_sem,
            device_id=device,
            device_id_type=MESH,
        )

    sent = []

    def send(src, dst, send_sem, recv_sem, device):
        copy = remote(src, dst, send_sem, recv_sem, device)
        copy.start()
        sent.append(copy)

    def arrived(dst, send_sem, recv_sem, device):
        remote(dst, dst, send_sem, recv_sem, device).wait_recv()

    sources = (w_in_hbm, w_out_hbm, w_text_hbm, images_hbm, texts_hbm, gain_hbm, bias_hbm, shift_hbm)
    targets = (w_in, w_out, w_text, images, texts, gain_row, bias_in, bias_text)
    loads = [
        pltpu.make_async_copy(source, target, s.load_sem.at[k])
        for k, (source, target) in enumerate(zip(sources, targets))
    ]
    for k in (3, 4, 5, 6, 0):
        loads[k].start()

    barrier = pltpu.get_barrier_semaphore()
    partners = [chip, other, far, at_yh()]
    partners += [at_z(d) for d in range(1, NZ)] + [at_x(d) for d in range(1, NX)]
    for partner in partners:
        pl.semaphore_signal(barrier, inc=1, device_id=partner, device_id_type=MESH)

    loads[3].wait()
    for i in range(2):
        for j in range(TILES):
            begin = j * TILE
            width = min(TILE, PATCH - begin)
            if width < TILE:
                full[i * TILES + j, mp] = jnp.zeros((OWN, TILE), b16)
            full[i * TILES + j, mp, :, 0:width] = images[i, :, begin : begin + width]
    loads[4].wait()
    s.texts.buf[z, yh] = texts[...].astype(f32)

    pl.semaphore_wait(barrier, len(partners))

    class Gather:
        def __init__(self, refs):
            self.buf, self.send_sem, self.recv_sem = refs.buf, refs.send, refs.recv

        def start(self, stage):
            for n, own, _, device in self.copies(stage):
                remote(own, own, self.send_sem.at[n], self.recv_sem.at[n], device).start()

        def wait(self, stage):
            for n, _, landed, device in self.copies(stage):
                arrived(landed, self.send_sem.at[n], self.recv_sem.at[n], device)

        def drain(self, stages):
            for stage in range(stages):
                for n, own, _, device in self.copies(stage):
                    remote(own, own, self.send_sem.at[n], self.recv_sem.at[n], device).wait_send()

    class TextGather(Gather):
        def copies(self, stage):
            at, dense = self.buf.at, s.text_dense.at
            if stage == 0:
                return [(0, at[z, yh], at[z, 1 - yh], at_yh())]
            if stage == 1:
                return [(d, at[z], at[(z + NZ - d) % NZ], at_z(d)) for d in range(1, NZ)]
            return [(7 + d, dense[x], dense[(x + NX - d) % NX], at_x(d)) for d in range(1, NX)]

        def make_dense(self):
            for r in range(2):
                s.text_dense[x, r] = self.buf[:, :, r, :].reshape(NZ * NH, D).astype(b16)

    class PoolGather(Gather):
        def copies(self, stage):
            at, pool, acts = self.buf.at, s.pool_dense.at, s.act_dense.at
            if stage == 0:
                return [(d, at[yh, z], at[yh, (z + NZ - d) % NZ], at_z(d)) for d in range(1, NZ)]
            if stage == 1:
                return [(0, at[yh], at[1 - yh], at_yh())]
            before, after, far = (x + NX - 1) % NX, (x + 1) % NX, (x + 2) % NX
            right, left = at_x(1), at_x(NX - 1)
            if stage == 2:
                return [
                    (8, pool[x], pool[before], right),
                    (9, pool[x], pool[after], left),
                    (10, acts[x], acts[before], right),
                    (11, acts[x], acts[after], left),
                ]
            lower, upper = pl.ds(0, 8), pl.ds(8, 8)
            return [
                (12, pool[before, lower], pool[far, lower], right),
                (13, pool[after, upper], pool[far, upper], left),
                (14, acts[before, 0], acts[far, 0], right),
                (15, acts[after, 1], acts[far, 1], left),
            ]

        def make_dense(self):
            rows = [self.buf[:, :, k, :].reshape(NH * NZ, D) for k in range(4)]
            s.pool_dense[x] = rows[0].astype(f32) + rows[1].astype(f32)
            s.act_dense[x, 0] = rows[2]
            s.act_dense[x, 1] = rows[3]

    def tile_copy(k, t):
        source = full.at[t, mp_chip if k == 2 else mp]
        return remote(source, source, s.img.send.at[k, t], s.img.recv.at[k, t], chip if k == 0 else other)

    for k in (2, 7, 1):
        loads[k].start()
    text_gather = TextGather(s.texts)
    tile_copy(0, 0).start()
    tile_copy(1, 0).start()
    text_gather.start(0)

    product[:, :, PADDED:D] = jnp.zeros((2, D, D - PADDED), f32)
    act_lanes[...] = jnp.zeros_like(act_lanes)
    act_sum[...] = jnp.zeros_like(act_sum)
    image_sum[...] = jnp.zeros_like(image_sum)
    grad_act[...] = jnp.zeros_like(grad_act)
    loads[5].wait()
    loads[6].wait()
    tile_copy(0, 1).start()
    tile_copy(1, 1).start()
    diagonal = iota((128, 128), 0) == iota((128, 128), 1)
    row_pad = s.row_pad
    for row, column, width in ((gain_row, s.gain_col, D), (bias_in, s.bias_col, HID)):
        row_pad[...] = jnp.zeros_like(row_pad)
        row_pad[:, 0:width] = row[...].reshape(1, width)
        for k in range(D // 128):
            span = slice(128 * k, 128 * k + 128)
            picked = jnp.sum(jnp.where(diagonal, row_pad[:, span], 0.0), axis=1, keepdims=True)
            column[span, :] = jnp.broadcast_to(picked, (128, 128))
    whole = HID // TILE * TILE
    chunks = [(begin, TILE) for begin in range(0, whole, TILE)] + [(whole, PADDED - whole)]
    loads[0].wait()
    tail = (iota((PADDED - whole, HID - whole), 0) == iota((PADDED - whole, HID - whole), 1)).astype(
        b16
    )
    w_pad[0:whole, :] = w_in[0:whole, :]
    w_pad[whole:PADDED, :] = mm(tail, w_in[whole:HID, :]).astype(b16)

    def add_product(t, first):
        i = t // TILES
        for begin, width in chunks:
            span = slice(begin, begin + width)
            term = mm_nt(normed[t], slopes[t, span, :])
            product[i, :, span] = term if first else product[i, :, span] + term

    def pass_on(t):
        arrived(full.at[t, mp_chip], s.img.send.at[0, t], s.img.recv.at[0, t], chip)
        tile_copy(2, t).start()

    def work_on(t):
        i = t // TILES
        j = t % TILES
        for h in range(TILE // 128):
            lanes = slice(128 * h, 128 * h + 128)
            total = jnp.zeros((1, 128), f32)
            for m in range(NM):
                total += jnp.sum(full[t, m, :, lanes].astype(f32), axis=0, keepdims=True)
            mean = total * (1.0 / D)
            total = jnp.zeros((1, 128), f32)
            for m in range(NM):
                centered = full[t, m, :, lanes].astype(f32) - mean
                total += jnp.sum(centered * centered, axis=0, keepdims=True)
            factor = lax.rsqrt(total * (1.0 / D) + epsilon)
            for m in range(NM):
                rows = slice(OWN * m, OWN * m + OWN)
                centered = full[t, m, :, lanes].astype(f32) - mean
                normed[t, rows, lanes] = (centered * factor * s.gain_col[rows, :]).astype(b16)
        image_sum[i] += mm_nt(jnp.ones((8, TILE), b16), full[t].reshape(D, TILE))
        before[...] = mm(w_pad[...], normed[t])

        @pl.when(t < 2 * TILES - 1)
        def _():
            pass_on(t + 1)

        @pl.when(t < 2 * TILES - 3)
        def _():
            tile_copy(0, t + 3).start()
            tile_copy(1, t + 3).start()

        valid = (iota((1, 128), 1) + (j * TILE + 128) < PATCH).astype(f32)
        for begin, width in chunks:
            span = slice(begin, begin + width)
            bias = s.bias_col[span, :]
            act, slope = gelu_and_slope(before[span, :] + jnp.concatenate([bias, bias], axis=1))
            slopes[t, span, :] = slope.astype(b16)
            act_lanes[i, span, :] += act[:, 0:128] + act[:, 128:TILE] * valid

    def project_texts():
        loads[2].wait()
        loads[7].wait()
        projected = mm(s.text_dense[...].reshape(BATCH, D), w_text[...]) + bias_text[...].reshape(1, D)
        norm = jnp.sqrt(jnp.sum(projected * projected, axis=1, keepdims=True) + epsilon)
        unit = projected / norm
        s.text_norm[...] = jnp.broadcast_to(norm, (BATCH, 128))
        s.text_unit[...] = unit
        s.text_emb[...] = unit.astype(b16)

    def tile_step(t, carry):
        @pl.when((t > 0) & (t % TILES == 1))
        def _():
            add_product(t - 1, True)

        @pl.when((t > 0) & (t % TILES != 1))
        def _():
            add_product(t - 1, False)

        @pl.when(t == 0)
        def _():
            text_gather.wait(0)
            text_gather.start(1)

        @pl.when(t == 2)
        def _():
            text_gather.wait(1)
            text_gather.make_dense()
            text_gather.start(2)

        @pl.when(t == 4)
        def _():
            text_gather.wait(2)
            project_texts()

        arrived(full.at[t, mp_core], s.img.send.at[1, t], s.img.recv.at[1, t], other)
        arrived(full.at[t, mp_far], s.img.send.at[2, t], s.img.recv.at[2, t], other)
        work_on(t)
        return carry

    pass_on(0)
    tile_copy(0, 2).start()
    tile_copy(1, 2).start()
    lax.fori_loop(0, 2 * TILES, tile_step, 0)

    loads[1].wait()
    ones = jnp.ones((8, 128), b16)
    for i in range(2):
        high, middle, _ = three_parts(act_lanes[i])
        act_sum[i, :, 0:PADDED] = mm_nt(ones, high) + mm_nt(ones, middle)
    row = iota((8, HID), 0)
    split = three_parts(act_sum[0, :, 0:HID]) + three_parts(act_sum[1, :, 0:HID])
    stacked = jnp.zeros((8, HID), f32)
    for k in range(6):
        stacked = jnp.where(row == k, split[k].astype(f32), stacked)
    shares = mm(stacked.astype(b16), w_out[...])
    row = iota((8, D), 0)
    share_0 = jnp.sum(jnp.where(row < 3, shares, 0.0), axis=0, keepdims=True)
    share_1 = jnp.sum(jnp.where((row >= 3) & (row < 6), shares, 0.0), axis=0, keepdims=True)
    first = iota((2, D), 0) == 0
    parts[mp] = jnp.where(first, share_0, share_1)
    group = (chip, other, far)
    for k, partner in enumerate(group):
        own = parts.at[mp]
        send(own, own, s.part.send.at[k], s.part.recv.at[k], partner)
    add_product(2 * TILES - 1, False)
    for k, source in enumerate((mp_chip, mp_core, mp_far)):
        arrived(parts.at[source], s.part.send.at[k], s.part.recv.at[k], group[k])
    block = parts[0] + parts[1] + parts[2] + parts[3]
    pooled = (jnp.where(first, image_sum[0, 0:2, :], image_sum[1, 0:2, :]) + block) * (1.0 / PATCH)
    pool_gather = PoolGather(s.pool)
    mine = jnp.where(core == 0, pooled[0:1, :], pooled[1:2, :])
    pooled_high = mine.astype(b16)
    pooled_rest = (mine - pooled_high.astype(f32)).astype(b16)
    rows = (pooled_high.astype(f32), pooled_rest.astype(f32), act_sum[0, 0:1, :], act_sum[1, 0:1, :])
    order = iota((4, D), 0)
    packed = jnp.broadcast_to(rows[0], (4, D))
    for k in range(1, 4):
        packed = jnp.where(order == k, rows[k], packed)
    s.pool.buf[yh, z] = packed.astype(b16)
    pool_gather.start(0)

    scale = scale_ref[0]
    shift = shift_ref[0]

    def block_gradient(values):
        norm = jnp.sqrt(jnp.sum(values * values, axis=1, keepdims=True) + epsilon)
        unit = values / norm
        emb = unit.astype(b16)
        logits = scale * mm_nt(emb, s.text_emb[...]) + shift
        if values.shape[0] == 2:
            matches = iota((2, BATCH), 1) == iota((2, BATCH), 0) * 16 + slot
        else:
            at = iota((BATCH, BATCH), 0)
            text = (((at >> 4) & 3) << 5) + ((at >> 6) << 4) + ((at & 7) << 1) + ((at >> 3) & 1)
            matches = text == iota((BATCH, BATCH), 1)
        signs = jnp.where(matches, 1.0, -1.0)
        coef = -signs * jax.nn.sigmoid(-signs * logits)
        weights = (scale * coef).astype(b16)
        grad_emb = mm(weights, s.text_emb[...])
        along = jnp.sum(unit * grad_emb, axis=1, keepdims=True)
        grad_pooled = (grad_emb - unit * along) / norm
        return (grad_pooled * (1.0 / PATCH)).astype(b16), weights, emb

    own_block, _, _ = block_gradient(pooled)
    grad_act[:, 0:HID] = mm_nt(own_block, w_out[...])

    near_z = (at_z(1), at_z(NZ - 1))
    near_x = (at_x(1), at_x(NX - 1))

    def add_into(target, index, begin, count, received):
        for r in range(0, count, 48):
            there = slice(begin + r, begin + r + 48)
            target[index, there, :] = (
                target[index, there, :].astype(f32) + received[r : r + 48, :].astype(f32)
            ).astype(b16)

    class Ring:
        def __init__(self, refs, place, size, near, steps):
            self.buf = refs.buf
            self.recv = refs.right, refs.left
            self.sems = refs.send, refs.recv
            self.place, self.size, self.near, self.steps = place, size, near, steps

        def wait(self, way, k):
            n = way * self.steps[0] + k - 1
            there = self.recv[way].at[k - 1]
            arrived(there, self.sems[0].at[n], self.sems[1].at[n], self.near[way])
            return there

        def step(self, k):
            for way in range(2):
                if k > self.steps[way]:
                    continue
                away = self.steps[way] + 1 - k
                chunk = (self.place + (self.size - away if way else away)) % self.size
                if k > 1:
                    add_into(self.buf, chunk, 0, self.buf.shape[1], self.wait(way, k - 1))
                n = way * self.steps[0] + k - 1
                send(
                    self.buf.at[chunk],
                    self.recv[way].at[k - 1],
                    self.sems[0].at[n],
                    self.sems[1].at[n],
                    self.near[way],
                )

        def finish(self):
            for way in range(2):
                self.wait(way, self.steps[way])

        def total(self, rows):
            value = self.buf[self.place, rows, :].astype(f32)
            for way in range(2):
                value += self.recv[way][self.steps[way] - 1, rows, :].astype(f32)
            return value

    class Group:
        def __init__(self, refs, begin, width):
            self.refs, self.begin, self.width = refs, begin, width
            self.span = slice(begin, begin + width)

        def send_pair(self):
            value = self.last_total()
            for h in range(NH):
                self.refs.pair.buf[h] = value[24 * h : 24 * h + 24, :]
            sems = self.refs.pair.send.at[0], self.refs.pair.recv.at[0]
            send(self.refs.pair.buf.at[1 - yh], self.refs.pair.right, *sems, at_yh())

        def result(self):
            sems = self.refs.pair.send.at[0], self.refs.pair.recv.at[0]
            arrived(self.refs.pair.right, *sems, at_yh())
            width = min(self.width, HID - self.begin)
            value = self.refs.pair.buf[yh] + self.refs.pair.right[...]
            out_in[:, self.begin : self.begin + width] = value[0:ROWS, 0:width]

    class GroupA(Group):
        def __init__(self, refs, begin, width, steps):
            super().__init__(refs, begin, width)
            self.z = Ring(refs.ring, z, NZ, near_z, steps)
            self.q1, self.q2, self.q3 = (x + 1) % NX, (x + 2) % NX, (x + 3) % NX

        def combine(self, q):
            for r in range(OWN // 48):
                rows = pl.ds(pl.multiple_of(q * OWN + 48 * r, 16), 48)
                self.refs.stage.buf[q, 48 * r : 48 * r + 48, :] = (
                    product[0, rows, self.span] * grad_act[0:1, self.span]
                    + product[1, rows, self.span] * grad_act[1:2, self.span]
                ).astype(b16)

        def pieces(self, way, k):
            n = way * 3 + k
            return (
                (self.refs.stage.left if way else self.refs.stage.right).at[k],
                self.refs.stage.send.at[n],
                self.refs.stage.recv.at[n],
                near_x[way],
            )

        def send_half(self, q, half, way, k):
            send(self.refs.stage.buf.at[q, pl.ds(144 * half, 144)], *self.pieces(way, k))

        def wait_half(self, way, k):
            arrived(*self.pieces(way, k))

        def first(self):
            self.combine(self.q2)
            self.send_half(self.q2, 0, 0, 0)
            self.send_half(self.q2, 1, 1, 0)

        def second(self):
            self.combine(self.q1)
            self.send_half(self.q1, 1, 0, 1)
            self.combine(self.q3)
            self.send_half(self.q3, 0, 1, 1)

        def third(self):
            self.wait_half(0, 0)
            add_into(self.refs.stage.buf, self.q1, 0, 144, self.refs.stage.right.at[0])
            self.send_half(self.q1, 0, 0, 2)
            self.wait_half(1, 0)
            add_into(self.refs.stage.buf, self.q3, 144, 144, self.refs.stage.left.at[0])
            self.send_half(self.q3, 1, 1, 2)

        def finish_x(self):
            total = self.refs.sum
            for k in range(1, 3):
                self.wait_half(0, k)
                self.wait_half(1, k)
            for half in range(2):
                for r in range(0, 144, 48):
                    there = slice(144 * half + r, 144 * half + r + 48)
                    here = slice(r, r + 48)
                    total[there, :] = (
                        self.refs.stage.buf[x, there, :].astype(f32)
                        + self.refs.stage.right[2 - half, here, :].astype(f32)
                        + self.refs.stage.left[1 + half, here, :].astype(f32)
                    )
            total[OWN : OWN + 8, :] = jnp.zeros((8, self.width), f32)
            for k in range(NZ):
                both = [
                    total[h * (NZ * ROWS) + k * ROWS : h * (NZ * ROWS) + k * ROWS + 24, :]
                    for h in range(NH)
                ]
                self.refs.ring.buf[k] = jnp.concatenate(both, axis=0).astype(b16)

        def last_total(self):
            self.z.finish()
            return self.z.total(slice(0, PAIR))

    class GroupB(Group):
        def __init__(self, refs, begin, width, steps):
            super().__init__(refs, begin, width)
            self.z = Ring(refs.stage, z, NZ, near_z, steps)

        def pack(self):
            pack = self.refs.pack
            weight_0, weight_1 = grad_act[0:1, self.span], grad_act[1:2, self.span]
            for k in range(NZ):
                for g in range(NX * NH):
                    begin = g * (NZ * ROWS) + k * ROWS
                    source = slice(begin, begin + ROWS)
                    pack[g * ROWS : g * ROWS + ROWS, :] = (
                        product[0, source, self.span] * weight_0
                        + product[1, source, self.span] * weight_1
                    )
                self.refs.stage.buf[k] = pack[...].astype(b16)

        def finish_z(self):
            self.z.finish()
            total = self.refs.sum
            for r in range(0, 144, 48):
                total[r : r + 48, :] = self.z.total(slice(r, r + 48))
            total[144:152, :] = jnp.zeros((8, self.width), f32)
            for k in range(NX):
                both = [
                    total[(k * NH + h) * ROWS : (k * NH + h) * ROWS + 24, :] for h in range(NH)
                ]
                self.refs.ring.buf[k] = jnp.concatenate(both, axis=0).astype(b16)

        def send_x(self):
            refs = self.refs.ring
            for d in range(1, NX):
                source, sems = refs.buf.at[(x + d) % NX], (refs.send.at[d - 1], refs.recv.at[d - 1])
                send(source, refs.right.at[d - 1], *sems, at_x(d))

        def last_total(self):
            refs = self.refs.ring
            value = refs.buf[x].astype(f32)
            for d in range(1, NX):
                arrived(refs.right.at[d - 1], refs.send.at[d - 1], refs.recv.at[d - 1], at_x(d))
                value += refs.right[d - 1].astype(f32)
            return value

    a1 = GroupA(s.a[0], *GROUPS_A[0], (3, 4))
    a2 = GroupA(s.a[1], *GROUPS_A[1], (4, 3))
    b1 = GroupB(s.b[0], *GROUPS_B[0], (4, 3))
    b2 = GroupB(s.b[1], *GROUPS_B[1], (3, 4))

    pairs = Refs({})

    def pairs_1():
        halves = [buf[...].reshape(HALF, D) for buf in (s.pool_dense, s.pool_other)]
        lower = jnp.where(core == 0, halves[0], halves[1])
        upper = jnp.where(core == 0, halves[1], halves[0])
        all_pooled = jnp.concatenate([lower, upper], axis=0)
        block, weights, emb = block_gradient(all_pooled)
        pick = (iota((D, ROWS), 0) == iota((D, ROWS), 1) + dp * ROWS).astype(b16)
        pairs.columns = mm(block, pick).astype(b16)
        pairs.features = mm(s.text_dense[...].reshape(BATCH, D), pick).astype(b16)
        pairs.weights, pairs.emb = weights, emb

    def pairs_2():
        grad_text = mm_tn(pairs.weights, pairs.emb)
        unit = s.text_unit[...]
        along = jnp.sum(unit * grad_text, axis=1, keepdims=True)
        pairs.proj = ((grad_text - unit * along) / s.text_norm[:, 0:1]).astype(b16)

    def pairs_4():
        acts = [s.act_dense[:, r, :, 0:HID].reshape(HALF, HID) for r in range(2)]
        out_out[...] = mm_tn(pairs.columns, jnp.concatenate(acts, axis=0))
        out_text[...] = mm_tn(pairs.features, pairs.proj)
        chosen = (iota((2, BATCH), 1) == iota((2, BATCH), 0) * 16 + slot).astype(b16)
        own_text = mm(chosen, pairs.proj).astype(b16)
        out_texts[...] = mm_nt(own_text, w_text[...]).astype(b16)

    a1.first()
    a2.first()
    b1.pack()
    b1.z.step(1)
    a1.second()
    b2.pack()
    b2.z.step(1)
    a2.second()
    pool_gather.wait(0)
    pool_gather.start(1)
    a1.third()
    b1.z.step(2)
    a2.third()
    b2.z.step(2)
    a1.combine(x)
    a2.combine(x)
    b1.z.step(3)
    pool_gather.wait(1)
    pool_gather.make_dense()
    b2.z.step(3)
    a1.finish_x()
    a1.z.step(1)
    b1.z.step(4)
    a2.finish_x()
    a2.z.step(1)
    pool_gather.start(2)
    b2.z.step(4)
    a1.z.step(2)
    a2.z.step(2)
    b1.finish_z()
    b1.send_x()
    b2.finish_z()
    b2.send_x()
    a1.z.step(3)
    pool_gather.wait(2)
    pool_gather.start(3)
    a2.z.step(3)
    b1.send_pair()
    a1.z.step(4)
    b2.send_pair()
    a2.z.step(4)
    pool_gather.wait(3)
    core_sems = s.core.send.at[0], s.core.recv.at[0]
    send(s.pool_dense, s.pool_other, *core_sems, other)
    a1.send_pair()
    a2.send_pair()
    arrived(s.pool_other, *core_sems, other)
    pairs_1()
    pairs_2()
    pairs_4()
    for group in (b1, b2, a1, a2):
        group.result()
    for copy in sent:
        copy.wait_send()
    text_gather.drain(3)
    pool_gather.drain(4)

    def drain_tiles(t, carry):
        for k in range(3):
            tile_copy(k, t).wait_send()
        return carry

    lax.fori_loop(0, 2 * TILES, drain_tiles, 0)


def hand_on(*refs):
    for k in range(4):
        refs[4 + k][...] = refs[k][...]


def shards(images, ln_gain, w_in, b_in, w_out, texts, w_text, b_text, logit_scale, logit_bias):
    vmem = pl.BlockSpec(memory_space=pltpu.VMEM)
    smem = pl.BlockSpec(memory_space=pltpu.SMEM)
    hbm = pl.BlockSpec(memory_space=pl.ANY)
    dma = pltpu.SemaphoreType.DMA
    V = pltpu.VMEM
    def with_sems(count, **buffers):
        return dict(send=dma(count), recv=dma(count), **buffers)

    def ring(kind, shape, steps, width):
        return with_sems(
            (sum(steps),),
            buf=V(shape + (width,), kind),
            right=V((steps[0],) + shape[1:] + (width,), kind),
            left=V((steps[1],) + shape[1:] + (width,), kind),
        )

    def pair(width):
        return with_sems((1,), buf=V((NH, 24, width), f32), right=V((24, width), f32))

    refs = dict(
        w_in=V((HID, D), b16),
        w_pad=V((PADDED, D), b16),
        before=V((PADDED, TILE), f32),
        act_lanes=V((2, PADDED, 128), f32),
        w_out=V((HID, D), b16),
        w_text=V((D, D), b16),
        gain_col=V((D, 128), f32),
        bias_col=V((D, 128), f32),
        row_pad=V((1, D), f32),
        full=V((2 * TILES, NM, OWN, TILE), b16),
        normed=V((2 * TILES, D, TILE), b16),
        slopes=V((2 * TILES, PADDED, TILE), b16),
        act_sum=V((2, 8, D), f32),
        image_sum=V((2, 8, D), f32),
        product=V((2, D, D), f32),
        parts=V((NM, 2, D), f32),
        pool_other=V((NX, 16, D), f32),
        text_dense=V((NX, 2, 16, D), b16),
        pool_dense=V((NX, 16, D), f32),
        act_dense=V((NX, 2, 16, D), b16),
        text_emb=V((BATCH, D), b16),
        text_unit=V((BATCH, D), f32),
        text_norm=V((BATCH, 128), f32),
        grad_act=V((2, D), f32),
        load_sem=dma((8,)),
        images=V((2, OWN, PATCH), b16),
        own_texts=V((2, D), b16),
        gain_row=V((D,), f32),
        bias_in=V((HID,), f32),
        bias_text=V((D,), f32),
        img=with_sems((3, 2 * TILES)),
        part=with_sems((3,)),
        core=with_sems((1,)),
        texts=with_sems((11,), buf=V((NZ, NH, 2, D), f32)),
        pool=with_sems((16,), buf=V((NH, NZ, 4, D), b16)),
    )
    def group_a(width, steps):
        stage = with_sems(
            (6,),
            buf=V((NX, OWN, width), b16),
            right=V((3, 144, width), b16),
            left=V((3, 144, width), b16),
        )
        return dict(
            stage=stage,
            sum=V((OWN + 8, width), f32),
            ring=ring(b16, (NZ, PAIR), steps, width),
            pair=pair(width),
        )

    def group_b(width, steps):
        return dict(
            pack=V((144, width), f32),
            stage=ring(b16, (NZ, 144), steps, width),
            sum=V((152, width), f32),
            ring=with_sems(
                (NX - 1,), buf=V((NX, PAIR, width), b16), right=V((NX - 1, PAIR, width), b16)
            ),
            pair=pair(width),
        )

    refs.update(
        a=[group_a(GROUPS_A[0][1], (3, 4)), group_a(GROUPS_A[1][1], (4, 3))],
        b=[group_b(GROUPS_B[0][1], (4, 3)), group_b(GROUPS_B[1][1], (3, 4))],
    )
    out_shape = [
        jax.ShapeDtypeStruct((ROWS, HID), f32),
        jax.ShapeDtypeStruct((ROWS, HID), f32),
        jax.ShapeDtypeStruct((ROWS, D), f32),
        jax.ShapeDtypeStruct((2, D), b16),
    ]
    results = pl.pallas_call(
        kernel,
        out_shape=[V(shape.shape, shape.dtype) for shape in out_shape],
        in_specs=[hbm] * 5 + [smem] * 2 + [hbm] * 3,
        out_specs=[vmem] * 4,
        scratch_shapes=[refs],
        compiler_params=pltpu.CompilerParams(
            collective_id=0, has_side_effects=True, vmem_limit_bytes=58 << 20
        ),
    )(
        images.transpose(0, 2, 1),
        ln_gain,
        b_in,
        b_text,
        texts,
        logit_scale,
        logit_bias,
        w_in.T,
        w_out,
        w_text,
    )
    grad_in, grad_out, grad_text, grad_texts = pl.pallas_call(
        hand_on,
        out_shape=out_shape,
        in_specs=[vmem] * 4,
        out_specs=[vmem] * 4,
        compiler_params=pltpu.CompilerParams(vmem_limit_bytes=4 << 20),
    )(*results)
    return grad_in, grad_out.T, grad_text, grad_texts


def solution(mesh):
    placed = (
        P("dp", None, "mp"),
        P(),
        P(None, "mp"),
        P("mp"),
        P("mp", None),
        P("dp", None),
        P(),
        P(),
        P(),
        P(),
    )
    return jax.shard_map(
        shards,
        mesh=mesh,
        in_specs=placed,
        out_specs=(P("dp", "mp"), P("mp", "dp"), P("dp", None), P("dp", None)),
        check_vma=False,
    )
```
